32 devices in a mesh: dp: 4 (over x, core), blk: 8 (over z, y).
Axes of the slice: x: 2, y: 2, z: 4, core: 2. Of those that a mesh axis runs over, the one named last changes fastest.
Arguments:
- tokens: bfloat16 [4, 1024, 2048], P('dp', 'blk'), may hold values from -6 to 6
- norm_gain: float32 [2048], replicated, may hold values from 0.5 to 1.5
- norm_bias: float32 [2048], replicated, may hold values from -3 to 3
- qkv_weight: bfloat16 [2048, 6144], replicated, may hold values from -0.125 to 0.125
- qkv_bias: float32 [6144], replicated, may hold values from -4 to 4
- out_weight: bfloat16 [2048, 2048], replicated, may hold values from -2 to 2
- gate_weight: bfloat16 [2048, 5632], replicated, may hold values from -0.125 to 0.125
- up_weight: bfloat16 [2048, 5632], replicated, may hold values from -0.125 to 0.125
- down_weight: bfloat16 [5632, 2048], replicated, may hold values from -0.078125 to 0.078125
- cotangent: bfloat16 [4, 1024, 2048], P('dp', 'blk'), may hold values from -6 to 6
- lengths: int32 [4], P('dp'), may hold values from 256 to 1024, as said below
Outputs:
- layer_out: bfloat16 [4, 1024, 2048], P('dp', 'blk')
- input_grad: bfloat16 [4, 1024, 2048], P('dp', 'blk')
- grad_norm_gain: float32 [2048], P(('dp', 'blk'))
- grad_norm_bias: float32 [2048], P(('dp', 'blk'))
- grad_qkv_weight: float32 [2048, 6144], P(('dp', 'blk'))
- grad_qkv_bias: float32 [6144], P(('dp', 'blk'))
- grad_out_weight: float32 [2048, 2048], P(('dp', 'blk'))
- grad_gate_weight: float32 [2048, 5632], P(('dp', 'blk'))
- grad_up_weight: float32 [2048, 5632], P(('dp', 'blk'))
- grad_down_weight: float32 [5632, 2048], P(('dp', 'blk'))
The draws below stay inside these ranges and needn't reach their ends.
Inputs may be any that keep to these rules, and one draw needn't show every extreme that they name: `lengths`: in each draw some bucket's sequence fills its whole slot of 1024 positions.
All inputs are finite; a program needn't handle non-finite values.
Results may differ from the reference program's by a relative error of at most 0.013.
Values may be sent and summed in bfloat16 or wider, within the bound.
No kernel may reach another device: no remote copies, remote signals or barrier semaphores. Data moves between devices by JAX's collectives and lax.ppermute only.
A program may use at most 512 MiB of HBM per device.

```python
import jax
import jax.numpy as jnp
from jax import lax

D = 2048
H = 32
HD = 64
ROT = 16
FF = 5632
TOK_DEV = 128
SLOT = 1024
N_DP = 4
N_BLK = 8


def draw_lengths(key, part):
    key = jax.random.fold_in(key, 7)
    highest = N_BLK * TOK_DEV
    lowest = highest // 4
    level_key, offset_key, chosen_key = jax.random.split(key, 3)
    levels = jax.random.randint(level_key, (N_DP,), 0, 3)
    base = jnp.left_shift(jnp.int32(lowest), levels.astype(jnp.int32))
    offsets = jax.random.randint(offset_key, (N_DP,), 0, base)
    values = jnp.minimum(base + offsets, highest)
    chosen = jax.random.randint(chosen_key, (), 0, N_DP)
    return jnp.where(jnp.arange(N_DP) == chosen, highest, values).astype(jnp.int32)


def level_of(own_key, shape, pieces, low, top_value):
    loudness, own = 1.0, jax.random.fold_in(own_key, 6)
    for axis_at, blocks in pieces:
        draws = jnp.exp(jax.random.uniform(jax.random.fold_in(own, axis_at), (blocks,), jnp.float32, low / len(pieces), top_value / len(pieces)))
        loudness = loudness * jnp.repeat(draws, shape[axis_at] // blocks).reshape([-1 if axis == axis_at else 1 for axis in range(len(shape))])
    return loudness


def bell_draw(key, shape, scale, reach, cuts=(), held_as=jnp.bfloat16):
    loudness = level_of(key, shape, cuts, -0.22, 0.18) if cuts else 1.0
    result = jax.random.normal(key, shape, jnp.float32) * scale * loudness
    return jnp.minimum(jnp.maximum(result, -reach), reach).astype(held_as)


def setup_inputs(seed: int = 0) -> dict:
    keys = jax.random.split(jax.random.key(seed), 12)
    return {
        "tokens": bell_draw(keys[0], (N_DP, SLOT, D), 1.0, 6.0, ((0, 4), (1, 8))),
        "norm_gain": jnp.clip(1.0 + 0.1 * jax.random.normal(keys[1], (D,), jnp.float32), 0.5, 1.5),
        "norm_bias": bell_draw(keys[2], (D,), 0.3, 3.0, (), jnp.float32),
        "qkv_weight": bell_draw(keys[3], (D, 3 * D), D ** -0.5, 0.125),
        "qkv_bias": bell_draw(keys[4], (3 * D,), 0.5, 4.0, (), jnp.float32),
        "out_weight": bell_draw(keys[5], (D, D), (max(D // 256, 4)) ** -0.5, 2.0),
        "gate_weight": bell_draw(keys[6], (D, FF), D ** -0.5, 0.125),
        "up_weight": bell_draw(keys[7], (D, FF), D ** -0.5, 0.125),
        "down_weight": bell_draw(keys[8], (FF, D), FF ** -0.5, 0.078125),
        "cotangent": bell_draw(keys[9], (N_DP, SLOT, D), 1.0, 6.0, ((0, 4), (1, 8))),
        "lengths": draw_lengths(jax.random.fold_in(keys[11], 71), 0),
    }


@jax.custom_vjp
def low(v):
    return lax.optimization_barrier(v.astype(jnp.bfloat16)).astype(jnp.float32)

@jax.custom_vjp
def low_back(v):
    return v

def low_keep(v):
    return (low(v), None)

def low_pass(kept, grad):
    return (grad,)

def back_keep(v):
    return (v, None)

def back_low(kept, grad):
    return (low(grad),)
low.defvjp(low_keep, low_pass)
low_back.defvjp(back_keep, back_low)
epsilon = 1e-05
masked_score = -1e+30

def matmul(left_side, right_side):
    return jnp.dot(left_side, right_side, precision=lax.Precision.HIGHEST)

def rotate(block_data, positions, direction):
    half_width = ROT // 2
    frequency = 10000.0 ** (-2.0 * jnp.arange(half_width, dtype=jnp.float32) / ROT)
    angles = positions.astype(jnp.float32)[:, None] * frequency[None, :]
    cosine = jnp.cos(angles)[:, None, :]
    sine_part = direction * jnp.sin(angles)[:, None, :]
    first_half = block_data[..., :half_width]
    second = block_data[..., half_width:ROT]
    return jnp.concatenate([first_half * cosine - second * sine_part, second * cosine + first_half * sine_part, block_data[..., ROT:]], axis=-1)

def layer(params, sequence, length):
    norm_gain, norm_bias, qkv_weight, qkv_bias, out_weight, gate_weight, up_weight, down_weight = params
    seq_span = sequence.shape[0]
    center = sequence - lax.optimization_barrier(jnp.mean(sequence, axis=1, keepdims=True))
    spread = lax.optimization_barrier(jnp.mean(center * center, axis=1, keepdims=True))
    normed = low(center * lax.rsqrt(spread + epsilon) * norm_gain + norm_bias)
    qkv_proj = low_back(matmul(normed, qkv_weight) + qkv_bias)
    positions = jnp.arange(seq_span, dtype=jnp.int32)
    query_heads = low(rotate(qkv_proj[:, :D].reshape(seq_span, H, HD), positions, 1.0))
    key_heads = low(rotate(qkv_proj[:, D:2 * D].reshape(seq_span, H, HD), positions, 1.0))
    value_heads = low(qkv_proj[:, 2 * D:].reshape(seq_span, H, HD))
    block_size = min(512, seq_span)
    block_count = seq_span // block_size
    score_scale = HD ** (-0.5)

    def attend(block_item):
        query_block, start = block_item
        scores = low_back(jnp.einsum('qhd,khd->hqk', query_block, key_heads, precision=lax.Precision.HIGHEST) * score_scale)
        query_pos = start + jnp.arange(block_size, dtype=jnp.int32)
        allowed = (positions[None, :] <= query_pos[:, None]) & (positions[None, :] < length)
        masked = jnp.where(allowed[None], scores, masked_score)
        row_best = lax.optimization_barrier(jnp.max(masked, axis=-1, keepdims=True))
        weights = jnp.exp(masked - row_best)
        probability = low(weights / lax.optimization_barrier(jnp.sum(weights, axis=-1, keepdims=True)))
        return jnp.einsum('hqk,khd->qhd', probability, value_heads, precision=lax.Precision.HIGHEST)
    starts = jnp.arange(block_count, dtype=jnp.int32) * block_size
    attended = lax.map(jax.checkpoint(attend), (query_heads.reshape(block_count, block_size, H, HD), starts))
    attended = low(low_back(attended.reshape(seq_span, D)))
    gate_proj = low_back(matmul(normed, gate_weight))
    up_proj = low_back(matmul(normed, up_weight))
    activated = low(jax.nn.silu(gate_proj) * up_proj)
    return sequence + matmul(attended, out_weight) + matmul(activated, down_weight)

def reference(tokens, norm_gain, norm_bias, qkv_weight, qkv_bias, out_weight, gate_weight, up_weight, down_weight, cotangent, lengths):
    params = (norm_gain, norm_bias, qkv_weight.astype(jnp.float32), qkv_bias, out_weight.astype(jnp.float32), gate_weight.astype(jnp.float32), up_weight.astype(jnp.float32), down_weight.astype(jnp.float32))

    def one_sequence(totals, sequence_item):
        sequence, seq_grad, length = sequence_item
        layer_value, pullback = jax.vjp(lambda weights_all, inputs: layer(weights_all, inputs, length), params, sequence.astype(jnp.float32))
        grads_params, grad_input = pullback(seq_grad.astype(jnp.float32))
        totals = jax.tree.map(lambda total_sum, grad_piece: total_sum + grad_piece, totals, grads_params)
        return (totals, (layer_value.astype(jnp.bfloat16), grad_input.astype(jnp.bfloat16)))
    start_totals = jax.tree.map(lambda weight_item: jnp.zeros(weight_item.shape, jnp.float32), params)
    totals, outputs = lax.scan(one_sequence, start_totals, (tokens, cotangent, lengths))
    layer_out, input_grad = outputs
    grad_gain, grad_bias, grad_qkv_w, grad_qkv_b, grad_out, grad_gate, grad_up, grad_down = totals
    return (layer_out, input_grad, grad_gain, grad_bias, grad_qkv_w, grad_qkv_b, grad_out, grad_gate, grad_up, grad_down)
```

```python
import functools

import jax
import jax.numpy as jnp
from jax import lax
from jax.experimental import pallas as pl
from jax.experimental.pallas import tpu as pltpu
from jax.sharding import PartitionSpec as P

HD = 64
ROT = 16
HALF = ROT // 2

epsilon = 1e-05
masked_score = -1e30
BQ = 256
F32 = jnp.float32
BF16 = jnp.bfloat16


def dot(left, right, left_dim=1, right_dim=0):
    return lax.dot_general(
        left, right, (((left_dim,), (right_dim,)), ((), ())), preferred_element_type=F32
    )


def gather_rows(shard, n_blk, b):
    if n_blk != 8:
        return lax.all_gather(shard, "blk", axis=0, tiled=True)
    order = [0, 1, 3, 2]
    along = [(2 * order[r] + y, 2 * order[(r + 1) % 4] + y) for r in range(4) for y in range(2)]
    across = [(i, i ^ 1) for i in range(8)]
    rows = shard.shape[0]
    z, y = b // 2, b % 2
    place = z ^ (z >> 1)
    full = jnp.zeros((8 * rows, shard.shape[1]), shard.dtype)
    piece = shard
    for step in range(4):
        slot = (place - step) % 4
        source = slot ^ (slot >> 1)
        other = lax.ppermute(piece, "blk", across)
        following = lax.ppermute(piece, "blk", along) if step < 3 else None
        full = lax.dynamic_update_slice(full, piece, ((2 * source + y) * rows, 0))
        full = lax.dynamic_update_slice(full, other, ((2 * source + 1 - y) * rows, 0))
        piece = following
    return full


def swap_blk(pieces):
    return lax.all_to_all(pieces, "blk", split_axis=0, concat_axis=0, tiled=True)


def reduce_dp(partial, n_dp, d):
    if n_dp != 4:
        return lax.psum_scatter(partial.astype(F32), "dp", scatter_dimension=0, tiled=False)

    def block(mask):
        return lax.dynamic_index_in_dim(partial, d ^ mask, 0, keepdims=False)

    first = lax.ppermute(
        jnp.stack([block(3), block(1)]), "dp", [(i, i ^ 1) for i in range(4)]
    ).astype(F32)
    second = lax.ppermute(
        (block(2).astype(F32) + first[0]).astype(BF16), "dp", [(i, i ^ 2) for i in range(4)]
    ).astype(F32)
    return block(0).astype(F32) + first[1] + second


def rotated(block, cosine, sine):
    a, b = block[:HALF], block[HALF:ROT]
    return jnp.concatenate([a * cosine - b * sine, b * cosine + a * sine, block[ROT:]], axis=0)


def masked_scores(keys, queries, start, length):
    scores = dot(keys, queries, 0, 0) * HD**-0.5
    key_pos = lax.broadcasted_iota(jnp.int32, scores.shape, 0)
    query_pos = start + lax.broadcasted_iota(jnp.int32, (1, scores.shape[1]), 1)
    allowed = key_pos <= jnp.minimum(query_pos, length - 1)
    return jnp.where(allowed, scores, masked_score)


def forward_kernel(length_ref, proj_ref, cos_ref, sin_ref, qkv_ref, att_ref, low_ref, lse_ref):
    span = proj_ref.shape[-1]
    length = length_ref[0]
    cosine, sine = cos_ref[...], sin_ref[...]
    qkv_ref[0, 0] = rotated(proj_ref[0, 0], cosine, sine).astype(BF16)
    qkv_ref[1, 0] = rotated(proj_ref[1, 0], cosine, sine).astype(BF16)
    qkv_ref[2, 0] = proj_ref[2, 0].astype(BF16)
    for start in range(0, span, BQ):
        end = start + BQ
        scores = masked_scores(
            qkv_ref[1, 0, :, :end], qkv_ref[0, 0, :, start:end], start, length
        )
        best = jnp.max(scores, axis=0, keepdims=True)
        weights = jnp.exp(scores - best)
        total = jnp.sum(weights, axis=0, keepdims=True)
        out = dot(qkv_ref[2, 0, :, :end], weights.astype(BF16)) / total
        att_ref[0, :, start:end] = out
        low_ref[0, :, start:end] = out.astype(BF16)
        lse_ref[0, :, start:end] = best + jnp.log(total)


def backward_kernel(
    length_ref, qkv_ref, grad_ref, att_ref, lse_ref, cos_ref, sin_ref, out_ref, dq, dk, dv
):
    span = qkv_ref.shape[-1]
    length = length_ref[0]
    scale = HD**-0.5
    dk[...] = jnp.zeros_like(dk)
    dv[...] = jnp.zeros_like(dv)
    for start in range(0, span, BQ):
        end = start + BQ
        keys, values = qkv_ref[1, 0, :, :end], qkv_ref[2, 0, :, :end]
        queries, grads = qkv_ref[0, 0, :, start:end], grad_ref[0, :, start:end]
        delta = jnp.sum(grads.astype(F32) * att_ref[0, :, start:end], axis=0, keepdims=True)
        scores = masked_scores(keys, queries, start, length)
        prob = jnp.exp(scores - lse_ref[0, :, start:end])
        grad_prob = dot(values, grads, 0, 0)
        grad_score = (prob * (grad_prob - delta)).astype(BF16)
        dq[:, start:end] = dot(keys, grad_score) * scale
        dk[:, :end] += dot(queries, grad_score, 1, 1)
        dv[:, :end] += dot(grads, prob.astype(BF16), 1, 1)
    cosine, sine = cos_ref[...], -sin_ref[...]
    out_ref[0, 0] = rotated(dq[...], cosine, sine).astype(BF16)
    out_ref[1, 0] = rotated(dk[...] * scale, cosine, sine).astype(BF16)
    out_ref[2, 0] = dv[...].astype(BF16)


def head_spec(lead, rows, span):
    if lead:
        return pl.BlockSpec((lead, 1, rows, span), lambda i: (0, i, 0, 0))
    return pl.BlockSpec((1, rows, span), lambda i: (i, 0, 0))


def attention_forward(proj, cosine, sine, length):
    _, heads, _, span = proj.shape
    table = pl.BlockSpec((HALF, span), lambda i: (0, 0))
    tiles = heads * span * span // 2
    return pl.pallas_call(
        forward_kernel,
        grid=(heads,),
        in_specs=[
            pl.BlockSpec(memory_space=pltpu.SMEM),
            head_spec(3, HD, span),
            table,
            table,
        ],
        out_specs=[
            head_spec(3, HD, span),
            head_spec(0, HD, span),
            head_spec(0, HD, span),
            head_spec(0, 1, span),
        ],
        out_shape=[
            jax.ShapeDtypeStruct((3, heads, HD, span), BF16),
            jax.ShapeDtypeStruct((heads, HD, span), F32),
            jax.ShapeDtypeStruct((heads, HD, span), BF16),
            jax.ShapeDtypeStruct((heads, 1, span), F32),
        ],
        compiler_params=pltpu.CompilerParams(vmem_limit_bytes=48 << 20),
        cost_estimate=pl.CostEstimate(
            flops=8 * tiles * HD, bytes_accessed=24 * heads * HD * span, transcendentals=tiles
        ),
        name="attention_forward",
    )(length, proj, cosine, sine)


def attention_backward(qkv, grads, att, lse, cosine, sine, length):
    _, heads, _, span = qkv.shape
    table = pl.BlockSpec((HALF, span), lambda i: (0, 0))
    tiles = heads * span * span // 2
    return pl.pallas_call(
        backward_kernel,
        grid=(heads,),
        in_specs=[
            pl.BlockSpec(memory_space=pltpu.SMEM),
            head_spec(3, HD, span),
            head_spec(0, HD, span),
            head_spec(0, HD, span),
            head_spec(0, 1, span),
            table,
            table,
        ],
        out_specs=head_spec(3, HD, span),
        out_shape=jax.ShapeDtypeStruct((3, heads, HD, span), BF16),
        scratch_shapes=[pltpu.VMEM((HD, span), F32)] * 3,
        compiler_params=pltpu.CompilerParams(vmem_limit_bytes=48 << 20),
        cost_estimate=pl.CostEstimate(
            flops=20 * tiles * HD, bytes_accessed=20 * heads * HD * span, transcendentals=tiles
        ),
        name="attention_backward",
    )(length, qkv, grads, att, lse, cosine, sine)


def on_device(
    n_dp,
    n_blk,
    tokens,
    norm_gain,
    norm_bias,
    qkv_weight,
    qkv_bias,
    out_weight,
    gate_weight,
    up_weight,
    down_weight,
    cotangent,
    lengths,
):
    rows, width = tokens.shape[1:]
    span = rows * n_blk
    hidden = gate_weight.shape[1]
    per_dev = width // HD // n_blk
    ff_block = hidden // (n_dp * n_blk)
    d, b = lax.axis_index("dp"), lax.axis_index("blk")

    inputs = tokens[0].astype(F32)
    out_grad = cotangent[0]
    center = inputs - jnp.mean(inputs, axis=1, keepdims=True)
    inverse_std = lax.rsqrt(jnp.mean(center * center, axis=1, keepdims=True) + epsilon)
    normalized = center * inverse_std
    normed = (normalized * norm_gain + norm_bias).astype(BF16)

    all_normed = gather_rows(normed, n_blk, b)
    all_grad = gather_rows(out_grad, n_blk, b)

    gate = dot(normed, gate_weight)
    up = dot(normed, up_weight)
    sig = jax.nn.sigmoid(gate)
    activated = (gate * sig * up).astype(BF16)
    ffn_out = dot(activated, down_weight)
    grad_act = dot(out_grad, down_weight, 1, 1)
    grad_gate = (grad_act * up * sig * (1.0 + gate * (1.0 - sig))).astype(BF16)
    grad_up = (grad_act * gate * sig).astype(BF16)
    ffn_grad = dot(grad_gate, gate_weight, 1, 1) + dot(grad_up, up_weight, 1, 1)

    head_starts = [(n_blk * i + b) * HD for i in range(per_dev)]
    ff_starts = [(n_blk * i + b) * ff_block for i in range(n_dp)]

    def columns(weight, starts, size):
        return jnp.concatenate(
            [lax.dynamic_slice_in_dim(weight, s, size, 1) for s in starts], axis=1
        )

    def row_blocks(weight, starts, size):
        return jnp.concatenate(
            [lax.dynamic_slice_in_dim(weight, s, size, 0) for s in starts], axis=0
        )

    qkv_starts = [part * width + s for part in range(3) for s in head_starts]
    own_qkv = columns(qkv_weight, qkv_starts, HD)
    own_bias = jnp.concatenate([lax.dynamic_slice_in_dim(qkv_bias, s, HD, 0) for s in qkv_starts])
    own_out = row_blocks(out_weight, head_starts, HD)
    own_gate = columns(gate_weight, ff_starts, ff_block)
    own_up = columns(up_weight, ff_starts, ff_block)
    own_down = row_blocks(down_weight, ff_starts, ff_block)

    frequency = 10000.0 ** (-2.0 * jnp.arange(HALF, dtype=F32) / ROT)
    angles = frequency[:, None] * jnp.arange(span, dtype=jnp.int32).astype(F32)[None, :]
    cosine, sine = jnp.cos(angles), jnp.sin(angles)

    proj = (dot(own_qkv, all_normed, 0, 1) + own_bias[:, None]).reshape(3, per_dev, HD, span)
    qkv, att, att_low, lse = attention_forward(proj, cosine, sine, lengths)

    def to_rows(whole):
        cut = whole.reshape(whole.shape[:-1] + (n_blk, rows))
        return swap_blk(jnp.moveaxis(cut, -2, 0))

    att_rows = jnp.swapaxes(to_rows(att_low), 0, 1).reshape(width, rows)
    layer_out = inputs + dot(att_rows, out_weight, 0, 0) + ffn_out

    tp_gate = dot(all_normed, own_gate)
    tp_up = dot(all_normed, own_up)
    tp_sig = jax.nn.sigmoid(tp_gate)
    tp_act = (tp_gate * tp_sig * tp_up).astype(BF16)
    tp_grad_act = dot(all_grad, own_down, 1, 1)
    tp_grad_gate = (tp_grad_act * tp_up * tp_sig * (1.0 + tp_gate * (1.0 - tp_sig))).astype(BF16)
    tp_grad_up = (tp_grad_act * tp_gate * tp_sig).astype(BF16)

    grads_att = dot(own_out, all_grad, 1, 1).astype(BF16).reshape(per_dev, HD, span)
    grad_qkv = attention_backward(qkv, grads_att, att, lse, cosine, sine, lengths)

    grad_rows = jnp.moveaxis(to_rows(grad_qkv), 0, 2).reshape(3 * width, rows)

    def down_like(partial):
        return reduce_dp(partial.astype(BF16).reshape(n_dp, -1, width), n_dp, d)

    def gate_like(partial):
        mine = reduce_dp(partial.astype(BF16).reshape(n_dp, width // n_dp, -1), n_dp, d)
        return swap_blk(mine.astype(BF16).reshape(n_blk, width // (n_dp * n_blk), -1))

    shard_down = down_like(dot(tp_act, all_grad, 0, 0))
    grad_out = dot(att_low.reshape(-1, span), all_grad)
    if per_dev % n_dp == 0:
        shard_out = down_like(grad_out)
    else:
        spread = jnp.zeros((width, width), F32)
        for i, s in enumerate(head_starts):
            spread = lax.dynamic_update_slice(spread, grad_out[i * HD : (i + 1) * HD], (s, 0))
        shard_out = lax.psum_scatter(spread, ("dp", "blk"), scatter_dimension=0, tiled=True)

    def ff_order(pieces):
        return (
            pieces.reshape(n_blk, -1, n_dp, ff_block)
            .transpose(1, 2, 0, 3)
            .reshape(-1, hidden)
            .astype(F32)
        )

    shard_gate = ff_order(gate_like(dot(all_normed, tp_grad_gate, 0, 0)))
    shard_up = ff_order(gate_like(dot(all_normed, tp_grad_up, 0, 0)))
    shard_qkv = (
        gate_like(dot(all_normed, grad_qkv.reshape(-1, span), 0, 1))
        .reshape(n_blk, -1, 3, per_dev, HD)
        .transpose(1, 2, 3, 0, 4)
        .reshape(-1, 3 * width)
        .astype(F32)
    )

    grad_hidden = ffn_grad + dot(grad_rows, qkv_weight, 0, 1)
    sums = jnp.concatenate(
        [
            part.reshape(n_dp * n_blk, -1)
            for part in (
                jnp.sum(grad_hidden * normalized, axis=0),
                jnp.sum(grad_hidden, axis=0),
                jnp.sum(grad_rows.astype(F32), axis=1),
            )
        ],
        axis=1,
    )
    sums = jnp.sum(
        lax.all_to_all(sums, ("dp", "blk"), split_axis=0, concat_axis=0, tiled=True), axis=0
    )
    cut = width // (n_dp * n_blk)
    grad_normal = grad_hidden * norm_gain
    grad_inputs = inverse_std * (
        grad_normal
        - jnp.mean(grad_normal, axis=1, keepdims=True)
        - normalized * jnp.mean(grad_normal * normalized, axis=1, keepdims=True)
    )
    input_grad = (out_grad.astype(F32) + grad_inputs).astype(BF16)
    return (
        layer_out.astype(BF16)[None],
        input_grad[None],
        sums[:cut],
        sums[cut : 2 * cut],
        shard_qkv,
        sums[2 * cut :],
        shard_out,
        shard_gate,
        shard_up,
        shard_down,
    )


def solution(mesh):
    both = P(("dp", "blk"))
    row_cut = P(("dp", "blk"), None)
    activation = P("dp", "blk", None)
    return jax.shard_map(
        functools.partial(on_device, mesh.shape["dp"], mesh.shape["blk"]),
        mesh=mesh,
        in_specs=(activation,) + (P(),) * 8 + (activation, P("dp")),
        out_specs=(activation, activation, both, both, row_cut, both) + (row_cut,) * 4,
        check_vma=False,
    )
```

```python
import functools

import jax
import jax.numpy as jnp
import numpy as np
from jax import lax
from jax.experimental import pallas as pl
from jax.experimental.pallas import tpu as pltpu
from jax.sharding import PartitionSpec as P

HD = 64
ROT = 16
HALF = ROT // 2

epsilon = 1e-05
masked_score = -1e30
BQ = 256
LANES = 128
EXTRA = 16
SCALE = 1.0
F32 = jnp.float32
BF16 = jnp.bfloat16


def dot(left, right, left_dim=1, right_dim=0):
    return lax.dot_general(
        left, right, (((left_dim,), (right_dim,)), ((), ())), preferred_element_type=F32
    )


RING = [0, 1, 3, 2]
ALONG = [(2 * RING[r] + y, 2 * RING[(r + 1) % 4] + y) for r in range(4) for y in range(2)]


def along(piece):
    return lax.ppermute(piece, "blk", ALONG)


def back(piece):
    return lax.ppermute(piece, "blk", [(target, source) for source, target in ALONG])


def beside(piece, n_blk):
    return lax.ppermute(piece, "blk", [(i, i ^ 1) for i in range(n_blk)])


def piece_slots(b):
    z, y = b // 2, b % 2
    place = z ^ (z >> 1)
    slots = []
    for step in (0, 1, 3, 2):
        slot = (place - step) % 4
        source = slot ^ (slot >> 1)
        slots += [2 * source + y, 2 * source + 1 - y]
    return jnp.stack(slots).astype(jnp.int32)


def swap_blk(pieces):
    return lax.all_to_all(pieces, "blk", split_axis=0, concat_axis=0, tiled=True)


def rotated(block, cosine, sine):
    a, b = block[:HALF], block[HALF:ROT]
    return jnp.concatenate([a * cosine - b * sine, b * cosine + a * sine, block[ROT:]], axis=0)


def masked_scores(keys, queries, start, length):
    scores = dot(keys, queries, 0, 0) * HD**-0.5
    key_pos = lax.broadcasted_iota(jnp.int32, scores.shape, 0)
    query_pos = start + lax.broadcasted_iota(jnp.int32, (1, scores.shape[1]), 1)
    allowed = key_pos <= jnp.minimum(query_pos, length - 1)
    return jnp.where(allowed, scores, masked_score)


ANY = pl.BlockSpec(memory_space=pl.ANY)
VMEM = pl.BlockSpec(memory_space=pltpu.VMEM)
SMEM = pl.BlockSpec(memory_space=pltpu.SMEM)


def kernel_call(kernel, args, after=(), prefetch=0, **options):
    in_specs = list(options.pop("in_specs")) + [ANY] * len(after)
    count = len(args)

    def body(*refs):
        kernel(*refs[:count], *refs[count + len(after) :])

    if prefetch:
        options["grid_spec"] = pltpu.PrefetchScalarGridSpec(
            num_scalar_prefetch=prefetch,
            in_specs=in_specs,
            **{k: options.pop(k) for k in ("grid", "out_specs", "scratch_shapes") if k in options},
        )
    else:
        options["in_specs"] = in_specs
    return pl.pallas_call(body, **options)(*args, *after)


def relay(arrays, after):
    count = len(arrays)
    return pl.pallas_call(
        lambda *refs: None,
        in_specs=[ANY] * (count + len(after)),
        out_specs=[ANY] * count,
        out_shape=[jax.ShapeDtypeStruct(array.shape, array.dtype) for array in arrays],
        input_output_aliases={k: k for k in range(count)},
        compiler_params=pltpu.CompilerParams(has_side_effects=True),
        cost_estimate=takes(1),
        name="relay",
    )(*arrays, *after)


def takes(us):
    return pl.CostEstimate(flops=int(us * SCALE * 1.15e9), bytes_accessed=1 << 16, transcendentals=0)


def params():
    return pltpu.CompilerParams(vmem_limit_bytes=56 << 20)


def ffn_kernel(
    tile,
    b_ref,
    n_ref,
    n_other,
    c_ref,
    c_other,
    gate_ref,
    up_ref,
    down_ref,
    out_ref,
    grad_ref,
    pass_ref,
    normed,
    flipped,
    gate_w,
    up_w,
    down_w,
    act,
    grad_gate,
    grad_up,
    sems,
):
    rows, width = n_ref.shape
    half = gate_w.shape[1]
    count = half // tile
    base = b_ref[0] % 2 * half

    def copies(t):
        here = pl.ds(pl.multiple_of(t * tile, tile), tile)
        there = pl.ds(pl.multiple_of(base + t * tile, LANES), tile)
        return [
            pltpu.make_async_copy(gate_ref.at[:, there], gate_w.at[:, here], sems.at[0, t]),
            pltpu.make_async_copy(up_ref.at[:, there], up_w.at[:, here], sems.at[1, t]),
            pltpu.make_async_copy(down_ref.at[there, :], down_w.at[here, :], sems.at[2, t]),
        ]

    for t in range(count):
        for copy in copies(t):
            copy.start()
    normed[:rows, :] = n_ref[...]
    normed[rows:, :] = n_other[...]
    flipped[:, :rows] = c_ref[...].T
    flipped[:, rows:] = c_other[...].T

    def first(t, carry):
        for copy in copies(t):
            copy.wait()
        here = pl.ds(pl.multiple_of(t * tile, tile), tile)
        gate = dot(normed[...], gate_w[:, here])
        up = dot(normed[...], up_w[:, here])
        grad_act = dot(down_w[here, :], flipped[...])
        sig = jax.nn.sigmoid(gate)
        silu = gate * sig
        act[:, here] = (silu * up).astype(BF16)
        by_gate = (up * sig * (1.0 + gate * (1.0 - sig))).T
        grad_gate[here, :] = (grad_act * by_gate).astype(BF16)
        grad_up[here, :] = (grad_act * silu.T).astype(BF16)
        return carry

    lax.fori_loop(0, count, first, 0)
    step = 512

    def second(r, carry):
        here = pl.ds(pl.multiple_of(r * step, step), step)
        out = dot(act[...], down_w[:, here])
        out_ref[:, here] = out[:rows]
        pass_ref[0, :, here] = out[rows:].astype(BF16)
        grad = (dot(gate_w[here, :], grad_gate[...]) + dot(up_w[here, :], grad_up[...])).T
        grad_ref[:, here] = grad[:rows]
        pass_ref[1, :, here] = grad[rows:].astype(BF16)
        return carry

    lax.fori_loop(0, width // step, second, 0)


def feed_forward(b, normed, out_grad, weights, after):
    rows, width = normed[0].shape
    half = weights[0].shape[1] // 2
    tile = 256
    return kernel_call(
        functools.partial(ffn_kernel, tile),
        (b, *normed, *out_grad, *weights),
        after,
        in_specs=[SMEM] + [VMEM] * 4 + [ANY] * 3,
        out_specs=[VMEM] * 3,
        out_shape=[
            jax.ShapeDtypeStruct((rows, width), F32),
            jax.ShapeDtypeStruct((rows, width), F32),
            jax.ShapeDtypeStruct((2, rows, width), BF16),
        ],
        scratch_shapes=[
            pltpu.VMEM((2 * rows, width), BF16),
            pltpu.VMEM((width, 2 * rows), BF16),
            pltpu.VMEM((width, half), BF16),
            pltpu.VMEM((width, half), BF16),
            pltpu.VMEM((half, width), BF16),
            pltpu.VMEM((2 * rows, half), BF16),
            pltpu.VMEM((half, 2 * rows), BF16),
            pltpu.VMEM((half, 2 * rows), BF16),
            pltpu.SemaphoreType.DMA((3, half // tile)),
        ],
        compiler_params=params(),
        cost_estimate=takes(24),
        name="feed_forward",
    )


def slice_kernel(size, starts, b_ref, gate_ref, up_ref, down_ref, out_ref, turned_ref, held, rows, sems, row_sems):
    depth, window = held.shape[-2:]
    b = b_ref[0]
    copies, offsets = [], []
    k = 0
    for weight in (gate_ref, up_ref):
        for column in starts(b):
            aligned = pl.multiple_of(
                jnp.minimum(column // LANES * LANES, weight.shape[1] - window), LANES
            )
            copy = pltpu.make_async_copy(
                weight.at[:, pl.ds(aligned, window)], held.at[k], sems.at[k]
            )
            copy.start()
            copies.append(copy)
            offsets.append(column - aligned)
            k += 1
    row_copies = []
    if down_ref.shape[0] > rows.shape[0]:
        for i, row in enumerate(starts(b)):
            row_copies.append(
                pltpu.make_async_copy(
                    down_ref.at[pl.ds(pl.multiple_of(row, size), size), :],
                    rows.at[pl.ds(i * size, size), :],
                    row_sems.at[i],
                )
            )
    else:
        row_copies.append(pltpu.make_async_copy(down_ref, rows, row_sems.at[0]))
    for copy in row_copies:
        copy.start()
    step = min(256, depth)
    for k, (copy, offset) in enumerate(zip(copies, offsets)):
        copy.wait()
        place = k * size % LANES
        for r in range(0, depth, step):
            block = pltpu.roll(held[k, r : r + step, :], window - offset + place, 1)
            out_ref[r : r + step, k * size : (k + 1) * size] = block[:, place : place + size]
    for copy in row_copies:
        copy.wait()
    for r in range(0, depth, step):
        turned_ref[r : r + step, :] = rows[:, r : r + step].T


def own_slices(b, gate, up, down, starts, count, size, after=()):
    depth = gate.shape[0]
    window = LANES * ((size + 2 * LANES - 2) // LANES)
    return kernel_call(
        functools.partial(slice_kernel, size, starts),
        (b, gate, up, down),
        after,
        in_specs=[SMEM] + [ANY] * 3,
        out_specs=[VMEM] * 2,
        out_shape=[
            jax.ShapeDtypeStruct((depth, 2 * count * size), BF16),
            jax.ShapeDtypeStruct((depth, count * size), BF16),
        ],
        scratch_shapes=[
            pltpu.VMEM((2 * count, depth, window), BF16),
            pltpu.VMEM((count * size, depth), BF16),
            pltpu.SemaphoreType.DMA((2 * count,)),
            pltpu.SemaphoreType.DMA((count,)),
        ],
        compiler_params=params(),
        cost_estimate=takes(12),
        name="own_slices",
    )


def fetch_rows(slots_ref, pieces, whole_ref, sems):
    rows = pieces[0].shape[0]
    copies = []
    for k, piece in enumerate(pieces):
        place = pl.multiple_of(slots_ref[k] * rows, rows)
        copies.append(
            pltpu.make_async_copy(piece, whole_ref.at[pl.ds(place, rows), :], sems.at[k])
        )
        copies[-1].start()
    return copies


def forward_kernel(
    count, b_ref, length_ref, slots_ref, weight_ref, bias_ref, cos_ref, sin_ref, *refs
):
    pieces = refs[:count]
    (
        whole_out,
        qkv_ref,
        att_ref,
        low_ref,
        flat_ref,
        lse_ref,
        whole_ref,
        window,
        proj,
        window_sem,
        sems,
        out_sem,
    ) = refs[count:]
    _, heads, _, span = qkv_ref.shape
    width = weight_ref.shape[0]
    n_blk = width // HD // heads
    length = length_ref[0]
    b = b_ref[0]
    copies = []
    for k in range(3 * heads):
        part, i = k // heads, k % heads
        column = part * width + (n_blk * i + b) * HD
        aligned = pl.multiple_of(column // LANES * LANES, LANES)
        copies.append(
            pltpu.make_async_copy(
                weight_ref.at[:, pl.ds(aligned, LANES)],
                window.at[:, pl.ds(k * LANES, LANES)],
                window_sem.at[k],
            )
        )
    rows = fetch_rows(slots_ref, pieces, whole_ref, sems)
    for copy in copies:
        copy.start()
    for copy in rows + copies:
        copy.wait()
    leaving = pltpu.make_async_copy(whole_ref, whole_out, out_sem)
    leaving.start()
    offset = pl.multiple_of(b % (LANES // HD) * HD, HD)
    cosine, sine = cos_ref[...], sin_ref[...]
    step = 256
    for r in range(0, span, step):
        block = whole_ref[r : r + step, :]
        flat = dot(block, window[...])
        for k in range(3 * heads):
            part, i = k // heads, k % heads
            proj[...] = flat[:, k * LANES : (k + 1) * LANES].T
            own = proj[pl.ds(offset, HD), :] + bias_ref[part, i]
            if part < 2:
                own = rotated(own, cosine[:, r : r + step], sine[:, r : r + step])
            qkv_ref[part, i, :, r : r + step] = own.astype(BF16)

    def head(i, carry):
        for start in range(0, span, BQ):
            end = start + BQ
            scores = masked_scores(
                qkv_ref[1, i, :, :end], qkv_ref[0, i, :, start:end], start, length
            )
            best = jnp.max(scores, axis=0, keepdims=True)
            weights = jnp.exp(scores - best)
            total = jnp.sum(weights, axis=0, keepdims=True)
            out = dot(qkv_ref[2, i, :, :end], weights.astype(BF16)) / total
            att_ref[i, :, start:end] = out
            low_ref[i, :, start:end] = out.astype(BF16)
            lse_ref[i, :, start:end] = best + jnp.log(total)
        return carry

    lax.fori_loop(0, heads, head, 0)
    for i in range(heads):
        flat_ref[:, i * HD : (i + 1) * HD] = low_ref[i].T
    leaving.wait()


def attention_forward(b, length, slots, weight, bias, cosine, sine, pieces, heads, after):
    width = weight.shape[0]
    span = len(pieces) * pieces[0].shape[0]
    count = len(pieces)
    return kernel_call(
        functools.partial(forward_kernel, count),
        (b, length, slots, weight, bias, cosine, sine, *pieces),
        after,
        in_specs=[SMEM, SMEM, SMEM, ANY, VMEM, VMEM, VMEM] + [ANY] * count,
        out_specs=[ANY] + [VMEM] * 5,
        out_shape=[
            jax.ShapeDtypeStruct((span, width), BF16),
            jax.ShapeDtypeStruct((3, heads, HD, span), BF16),
            jax.ShapeDtypeStruct((heads, HD, span), F32),
            jax.ShapeDtypeStruct((heads, HD, span), BF16),
            jax.ShapeDtypeStruct((span, heads * HD), BF16),
            jax.ShapeDtypeStruct((heads, 1, span), F32),
        ],
        scratch_shapes=[
            pltpu.VMEM((span, width), BF16),
            pltpu.VMEM((width, 3 * heads * LANES), BF16),
            pltpu.VMEM((LANES, 256), F32),
            pltpu.SemaphoreType.DMA((3 * heads,)),
            pltpu.SemaphoreType.DMA((count,)),
            pltpu.SemaphoreType.DMA,
        ],
        compiler_params=params(),
        cost_estimate=takes(20),
        name="attention_forward",
    )


def backward_kernel(
    count, b_ref, length_ref, slots_ref, weight_ref, qkv_ref, att_ref, lse_ref, cos_ref, sin_ref, *refs
):
    pieces = refs[:count]
    (
        whole_out,
        out_ref,
        flat_ref,
        whole_ref,
        weight,
        grad_ref,
        dq,
        dk,
        dv,
        turned,
        weight_sem,
        sems,
        out_sem,
    ) = refs[count:]
    _, heads, _, span = qkv_ref.shape
    length = length_ref[0]
    scale = HD**-0.5
    cosine, sine = cos_ref[...], -sin_ref[...]
    n_blk = out_ref.shape[0]
    copies = fetch_rows(slots_ref, pieces, whole_ref, sems)
    for i in range(heads):
        row = pl.multiple_of((n_blk * i + b_ref[0]) * HD, HD)
        copies.append(
            pltpu.make_async_copy(
                weight_ref.at[pl.ds(row, HD), :],
                weight.at[pl.ds(i * HD, HD), :],
                weight_sem.at[i],
            )
        )
        copies[-1].start()
    for copy in copies:
        copy.wait()
    leaving = pltpu.make_async_copy(whole_ref, whole_out, out_sem)
    leaving.start()
    across = weight[...].T
    for start in range(0, span, BQ):
        grads = dot(whole_ref[start : start + BQ, :], across).T.astype(BF16)
        for i in range(heads):
            grad_ref[i, :, start : start + BQ] = grads[i * HD : (i + 1) * HD, :]

    def head(i, carry):
        dk[...] = jnp.zeros_like(dk)
        dv[...] = jnp.zeros_like(dv)
        for start in range(0, span, BQ):
            end = start + BQ
            keys, values = qkv_ref[1, i, :, :end], qkv_ref[2, i, :, :end]
            queries, grads = qkv_ref[0, i, :, start:end], grad_ref[i, :, start:end]
            delta = jnp.sum(grads.astype(F32) * att_ref[i, :, start:end], axis=0, keepdims=True)
            scores = masked_scores(keys, queries, start, length)
            prob = jnp.exp(scores - lse_ref[i, :, start:end])
            grad_prob = dot(values, grads, 0, 0)
            grad_score = (prob * (grad_prob - delta)).astype(BF16)
            dq[:, start:end] = dot(keys, grad_score) * scale
            dk[:, :end] += dot(queries, grad_score, 1, 1)
            dv[:, :end] += dot(grads, prob.astype(BF16), 1, 1)
        turned[0, i] = rotated(dq[...], cosine, sine).astype(BF16)
        turned[1, i] = rotated(dk[...] * scale, cosine, sine).astype(BF16)
        turned[2, i] = dv[...].astype(BF16)
        return carry

    lax.fori_loop(0, heads, head, 0)
    rows = out_ref.shape[2]
    for part in range(3):
        for i in range(heads):
            k = part * heads + i
            flat_ref[:, k * HD : (k + 1) * HD] = turned[part, i].T
            for j in range(n_blk):
                out_ref[j, k * HD : (k + 1) * HD, :] = turned[part, i, :, j * rows : (j + 1) * rows]
    leaving.wait()


def attention_backward(
    b, length, slots, weight, qkv, att, lse, cosine, sine, pieces, n_blk, after=()
):
    _, heads, _, span = qkv.shape
    width = weight.shape[1]
    count = len(pieces)
    return kernel_call(
        functools.partial(backward_kernel, count),
        (b, length, slots, weight, qkv, att, lse, cosine, sine, *pieces),
        after,
        in_specs=[SMEM, SMEM, SMEM, ANY] + [VMEM] * 5 + [ANY] * count,
        out_specs=[ANY] + [VMEM] * 2,
        out_shape=[
            jax.ShapeDtypeStruct((span, width), BF16),
            jax.ShapeDtypeStruct((n_blk, 3 * heads * HD, span // n_blk), BF16),
            jax.ShapeDtypeStruct((span, 3 * heads * HD), BF16),
        ],
        scratch_shapes=[
            pltpu.VMEM((span, width), BF16),
            pltpu.VMEM((heads * HD, width), BF16),
            pltpu.VMEM((heads, HD, span), BF16),
        ]
        + [pltpu.VMEM((HD, span), F32)] * 3
        + [
            pltpu.VMEM((3, heads, HD, span), BF16),
            pltpu.SemaphoreType.DMA((heads,)),
            pltpu.SemaphoreType.DMA((count,)),
            pltpu.SemaphoreType.DMA,
        ],
        compiler_params=params(),
        cost_estimate=takes(18),
        name="attention_backward",
    )


def grads_kernel(n_dp, n_ref, c_ref, gate_up_ref, down_ref, act_ref, grad_ref):
    cols = down_ref.shape[1]
    both = dot(n_ref[...], gate_up_ref[...])
    gate, up = both[:, :cols], both[:, cols:]
    sig = jax.nn.sigmoid(gate)
    silu = gate * sig
    act = silu * up
    part = cols // n_dp
    for i in range(n_dp):
        act_ref[i] = act[:, i * part : (i + 1) * part].T.astype(BF16)
    grad_act = dot(c_ref[...], down_ref[...])
    grad_ref[:, :cols] = (grad_act * up * sig * (1.0 + gate * (1.0 - sig))).astype(BF16)
    grad_ref[:, cols:] = (grad_act * silu).astype(BF16)


def local_grads(all_normed, all_grad, gate_up, down, n_dp, after=()):
    span, width = all_normed.shape
    cols = down.shape[1]
    size = 256
    return kernel_call(
        functools.partial(grads_kernel, n_dp),
        (all_normed, all_grad, gate_up, down),
        after,
        grid=(span // size,),
        in_specs=[
            pl.BlockSpec((size, width), lambda r: (r, 0)),
            pl.BlockSpec((size, width), lambda r: (r, 0)),
            pl.BlockSpec((width, 2 * cols), lambda r: (0, 0)),
            pl.BlockSpec((width, cols), lambda r: (0, 0)),
        ],
        out_specs=[
            pl.BlockSpec((n_dp, cols // n_dp, size), lambda r: (0, 0, r)),
            pl.BlockSpec((size, 2 * cols), lambda r: (r, 0)),
        ],
        out_shape=[
            jax.ShapeDtypeStruct((n_dp, cols // n_dp, span), BF16),
            jax.ShapeDtypeStruct((span, 2 * cols), BF16),
        ],
        compiler_params=params(),
        cost_estimate=takes(15),
        name="local_grads",
    )


def keep(value, first, on_ref, mine_ref, cut):
    value += first.astype(F32)

    @pl.when(pl.program_id(0) < cut)
    def _():
        on_ref[...] = value.astype(BF16)

    @pl.when(pl.program_id(0) >= cut)
    def _():
        mine_ref[...] = value


def column_products_kernel(low, high, order_ref, left_ref, right_ref, *refs):
    value = dot(left_ref[...], right_ref[:, low:high], 0, 0)
    if len(refs) == 1:
        refs[0][0] = value.astype(BF16)
    else:
        keep(value, refs[0][0, :, low:high], *refs[1:], 2)


def column_products(order, left, right, low, high, n_dp, first=None, after=()):
    span, width = left.shape
    cols = high - low
    size = width // n_dp
    part = size // 2
    stay = [
        pl.BlockSpec((part, cols), lambda j, order: (jnp.minimum(j, 1), 0)),
        pl.BlockSpec((part, cols), lambda j, order: (jnp.maximum(j - 2, 0), 0)),
    ]
    block = pl.BlockSpec(
        (1, part, cols if first is None else right.shape[1]), lambda j, order: (j // 2, j % 2, 0)
    )
    return kernel_call(
        functools.partial(column_products_kernel, low, high),
        (order, left, right) + (() if first is None else (first,)),
        after,
        prefetch=1,
        grid=(4,),
        in_specs=[
            pl.BlockSpec((span, part), lambda j, order: (0, order[j // 2] * 2 + j % 2)),
            pl.BlockSpec(right.shape, lambda j, order: (0, 0)),
        ]
        + ([] if first is None else [block]),
        out_specs=block if first is None else stay,
        out_shape=jax.ShapeDtypeStruct((2, size, cols), BF16)
        if first is None
        else [jax.ShapeDtypeStruct((size, cols), dtype) for dtype in (BF16, F32)],
        compiler_params=params(),
        cost_estimate=takes(8),
        name="column_products",
    )


def row_products_kernel(count, order_ref, *refs):
    lefts, right_ref, rest = refs[:count], refs[count], refs[count + 1 :]
    value = [dot(left[0], right_ref[...]) for left in lefts]
    value = jnp.concatenate(value, axis=0) if count > 1 else value[0]
    if len(rest) == 1:
        rest[0][0] = value.astype(BF16)
    else:
        keep(value, rest[0][0], *rest[1:], 1)


def row_products(order, lefts, right, first=None, after=()):
    span, width = right.shape
    size = sum(left.shape[1] for left in lefts)
    block = pl.BlockSpec((1, size, width), lambda j, order: (j, 0, 0))
    stay = pl.BlockSpec((size, width), lambda j, order: (0, 0))
    return kernel_call(
        functools.partial(row_products_kernel, len(lefts)),
        (order, *lefts, right) + (() if first is None else (first,)),
        after,
        prefetch=1,
        grid=(2,),
        in_specs=[
            pl.BlockSpec((1,) + left.shape[1:], lambda j, order: (order[j], 0, 0))
            for left in lefts
        ]
        + [pl.BlockSpec((span, width), lambda j, order: (0, 0))]
        + ([] if first is None else [block]),
        out_specs=block if first is None else [stay, stay],
        out_shape=jax.ShapeDtypeStruct((2, size, width), BF16)
        if first is None
        else [jax.ShapeDtypeStruct((size, width), dtype) for dtype in (BF16, F32)],
        compiler_params=params(),
        cost_estimate=takes(8),
        name="row_products",
    )


def add_kernel(mine_ref, second_ref, *out_refs):
    total = mine_ref[...] + second_ref[...].astype(F32)
    start = 0
    for out_ref in out_refs:
        size = out_ref.shape[0]
        out_ref[...] = total[start : start + size].astype(out_ref.dtype)
        start += size


def add_second(mine, second, sizes, dtype, after=(), us=16):
    _, cols = mine.shape
    return kernel_call(
        add_kernel,
        (mine, second),
        after,
        in_specs=[VMEM] * 2,
        out_specs=[VMEM] * len(sizes),
        out_shape=[jax.ShapeDtypeStruct((part, cols), dtype) for part in sizes],
        compiler_params=params(),
        cost_estimate=takes(us),
        name="add_second",
    )


def add_beside_kernel(mine_ref, second_ref, vector_ref, out_ref):
    rows = mine_ref.shape[0] // out_ref.shape[0]
    cols = vector_ref.shape[1]
    for j in range(out_ref.shape[0]):
        here = slice(j * rows, (j + 1) * rows)
        total = mine_ref[here, :] + second_ref[here, :].astype(F32)
        out_ref[j, :rows, :] = total.astype(BF16)
        out_ref[j, rows:, :] = jnp.zeros((EXTRA, out_ref.shape[2]), BF16)
        out_ref[j, rows : rows + 1, :cols] = vector_ref[j : j + 1, :].astype(BF16)


def add_beside(mine, second, vectors, after=()):
    n_blk = vectors.shape[0]
    size, cols = mine.shape
    return kernel_call(
        add_beside_kernel,
        (mine, second, vectors),
        after,
        in_specs=[VMEM] * 3,
        out_specs=VMEM,
        out_shape=jax.ShapeDtypeStruct((n_blk, size // n_blk + EXTRA, cols), BF16),
        compiler_params=params(),
        cost_estimate=takes(16),
        name="add_beside",
    )


def spread_kernel(count, outer, size, line, *refs):
    arrays, out_refs = refs[:count], refs[count:]
    n_blk = arrays[0].shape[0]
    if line:
        *out_refs, line_ref = out_refs
        rows = out_refs[0].shape[0]
        line_ref[...] = sum(
            arrays[-1][b, rows : rows + EXTRA, :line].astype(F32) for b in range(n_blk)
        )[:1]
    for k, out_ref in enumerate(out_refs):
        rows = out_ref.shape[0]
        for i in range(outer):
            for b in range(n_blk):
                source = (k * outer + i) * size
                place = (i * n_blk + b) * size
                start = 0
                for array in arrays:
                    end = start + array.shape[2]
                    low, high = max(source, start), min(source + size, end)
                    if low < high:
                        out_ref[:, place + low - source : place + high - source] = array[
                            b, :rows, low - start : high - start
                        ].astype(F32)
                    start = end


def spread(arrays, rows, outputs, outer, size, line=0, after=()):
    n_blk = arrays[0].shape[0]
    return kernel_call(
        functools.partial(spread_kernel, len(arrays), outer, size, line),
        tuple(arrays),
        after,
        in_specs=[VMEM] * len(arrays),
        out_specs=[VMEM] * (outputs + (line > 0)),
        out_shape=[jax.ShapeDtypeStruct((rows, outer * n_blk * size), F32)] * outputs
        + [jax.ShapeDtypeStruct((1, line), F32)] * (line > 0),
        compiler_params=params(),
        cost_estimate=takes(3),
        name="spread",
    )


def out_kernel(x_ref, ffn_ref, other_ref, weight_ref, pieces, out_ref, left, total):
    n_blk, _, cols = pieces.shape
    step = pl.program_id(0)
    size = left.shape[2]

    @pl.when(step == 0)
    def _():
        for i in range(cols // HD):
            for b in range(n_blk):
                place = (i * n_blk + b) * HD
                block, start = place // size, place % size
                left[block, :, start : start + HD] = pieces[b, :, i * HD : (i + 1) * HD]
        total[...] = x_ref[...].astype(F32) + ffn_ref[...] + other_ref[0].astype(F32)

    total[...] += dot(left[step], weight_ref[...])

    @pl.when(step == pl.num_programs(0) - 1)
    def _():
        out_ref[...] = total[...].astype(BF16)


def project_out(tokens, ffn_out, other, weight, pieces, after=()):
    rows, width = tokens.shape
    steps = 4
    size = width // steps
    whole = pl.BlockSpec((rows, width), lambda t: (0, 0))
    return kernel_call(
        out_kernel,
        (tokens, ffn_out, other, weight, pieces),
        after,
        grid=(steps,),
        in_specs=[
            whole,
            whole,
            pl.BlockSpec((1, rows, width), lambda t: (0, 0, 0)),
            pl.BlockSpec((size, width), lambda t: (t, 0)),
            pl.BlockSpec(pieces.shape, lambda t: (0, 0, 0)),
        ],
        out_specs=whole,
        out_shape=jax.ShapeDtypeStruct((rows, width), BF16),
        scratch_shapes=[pltpu.VMEM((steps, rows, size), BF16), pltpu.VMEM((rows, width), F32)],
        compiler_params=params(),
        cost_estimate=takes(6),
        name="project_out",
    )


def input_kernel(
    x_ref, c_ref, gain_ref, ffn_ref, other_ref, weight_ref, pieces, out_ref, sums_ref, left, total
):
    n_blk, cols, _ = pieces.shape
    step, steps = pl.program_id(0), pl.num_programs(0)
    size = left.shape[1]

    @pl.when(step == 0)
    def _():
        for i in range(cols // HD):
            for b in range(n_blk):
                place = (i * n_blk + b) * HD
                block, start = place // size, place % size
                left[block, start : start + HD, :] = pieces[b, i * HD : (i + 1) * HD, :]
        total[...] = jnp.zeros_like(total)

    total[...] += dot(weight_ref[...], left[step])

    @pl.when(step == steps - 1)
    def _():
        x = x_ref[...].astype(F32)
        center = x - jnp.mean(x, axis=1, keepdims=True)
        inverse_std = lax.rsqrt(jnp.mean(center * center, axis=1, keepdims=True) + epsilon)
        normalized = center * inverse_std
        grad = ffn_ref[...] + other_ref[0].astype(F32) + total[...].T
        vectors = [
            jnp.sum(grad * normalized, axis=0, keepdims=True),
            jnp.sum(grad, axis=0, keepdims=True),
        ] + [jnp.sum(left[t].astype(F32).T, axis=0, keepdims=True) for t in range(left.shape[0])]
        flat = jnp.concatenate(vectors, axis=1)
        shards = sums_ref.shape[0]
        width = grad.shape[1]
        cut = width // shards
        for j in range(shards):
            sums_ref[j : j + 1, :cut] = flat[:, j * cut : (j + 1) * cut]
            sums_ref[j : j + 1, cut : 2 * cut] = flat[:, width + j * cut : width + (j + 1) * cut]
            start = 2 * width + 3 * j * cut
            sums_ref[j : j + 1, 2 * cut :] = flat[:, start : start + 3 * cut]
        grad = grad * gain_ref[...]
        grad_inputs = inverse_std * (
            grad
            - jnp.mean(grad, axis=1, keepdims=True)
            - normalized * jnp.mean(grad * normalized, axis=1, keepdims=True)
        )
        out_ref[...] = (c_ref[...].astype(F32) + grad_inputs).astype(BF16)


def input_grads(
    tokens, out_grad, gain, ffn_grad, other, weight, pieces, shards, after=()
):
    rows, width = tokens.shape
    cols = weight.shape[1]
    steps = 8
    size = cols // steps
    whole = pl.BlockSpec((rows, width), lambda t: (0, 0))
    return kernel_call(
        input_kernel,
        (tokens, out_grad, gain, ffn_grad, other, weight, pieces),
        after,
        grid=(steps,),
        in_specs=[
            whole,
            whole,
            pl.BlockSpec((1, width), lambda t: (0, 0)),
            whole,
            pl.BlockSpec((1, rows, width), lambda t: (1, 0, 0)),
            pl.BlockSpec((width, size), lambda t: (0, t)),
            pl.BlockSpec(pieces.shape, lambda t: (0, 0, 0)),
        ],
        out_specs=[whole, pl.BlockSpec((shards, 5 * width // shards), lambda t: (0, 0))],
        out_shape=[
            jax.ShapeDtypeStruct((rows, width), BF16),
            jax.ShapeDtypeStruct((shards, 5 * width // shards), F32),
        ],
        scratch_shapes=[pltpu.VMEM((steps, size, rows), BF16), pltpu.VMEM((width, rows), F32)],
        compiler_params=params(),
        cost_estimate=takes(13),
        name="input_grads",
    )


def on_device(
    n_dp,
    n_blk,
    tokens,
    norm_gain,
    norm_bias,
    qkv_weight,
    qkv_bias,
    out_weight,
    gate_weight,
    up_weight,
    down_weight,
    cotangent,
    lengths,
):
    rows, width = tokens.shape[1:]
    span = rows * n_blk
    hidden = gate_weight.shape[1]
    per_dev = width // HD // n_blk
    ff_block = hidden // (n_dp * n_blk)
    d, b = lax.axis_index("dp").astype(jnp.int32), lax.axis_index("blk").astype(jnp.int32)
    own_tokens, out_grad = tokens[0], cotangent[0]

    inputs = own_tokens.astype(F32)
    center = inputs - jnp.mean(inputs, axis=1, keepdims=True)
    inverse_std = lax.rsqrt(jnp.mean(center * center, axis=1, keepdims=True) + epsilon)
    normed = (center * inverse_std * norm_gain + norm_bias).astype(BF16)

    position = b.reshape(1)

    def ff_starts(b):
        return [(n_blk * i + b) * ff_block for i in range(n_dp)]

    def own_blocks(array, outer, size):
        cut = array.reshape((outer, n_blk, size) + array.shape[1:])
        return lax.dynamic_index_in_dim(cut, b, 1, keepdims=False).reshape(
            (-1,) + array.shape[1:]
        )

    down_rows = down_weight if ff_block % 16 == 0 else own_blocks(down_weight, n_dp, ff_block)

    def slices():
        return own_slices(
            position, gate_weight, up_weight, down_rows, ff_starts, n_dp, ff_block
        )

    def ffn(normed_other, grad_other, after):
        return feed_forward(
            position,
            (normed, normed_other),
            (out_grad, grad_other),
            (gate_weight, up_weight, down_weight),
            after,
        )

    if n_blk == 8:
        slots = piece_slots(b)
        n1, m0, c1, e0 = along(normed), beside(normed, 8), along(out_grad), beside(out_grad, 8)
        own_gate_up, own_down = slices()
        n1, c1, n3 = relay([n1, c1, normed], [own_down])
        n2, m1, c2, e1 = along(n1), beside(n1, 8), along(c1), beside(c1, 8)
        n3 = back(n3)
        ffn_out, ffn_grad, passed = ffn(m0, e0, [n1, c1])
        n2, c2, c3 = relay([n2, c2, out_grad], [ffn_out, m1, e1])
        m2, c3 = beside(n2, 8), back(c3)
        (n3,) = relay([n3], [n2])
        m3, e2 = beside(n3, 8), beside(c2, 8)
        (c3,) = relay([c3], [n3])
        e3 = beside(c3, 8)
        normed_pieces = [normed, m0, n1, m1, n3, m3, n2, m2]
        grad_pieces = [out_grad, e0, c1, e1, c3, e3, c2, e2]
        early = [c3]
    else:
        slots = jnp.zeros((1,), jnp.int32)
        normed_pieces = [lax.all_gather(normed, "blk", axis=0, tiled=True)]
        grad_pieces = [lax.all_gather(out_grad, "blk", axis=0, tiled=True)]
        own_gate_up, own_down = slices()
        ffn_out, ffn_grad, passed = ffn(
            beside(normed, n_blk), beside(out_grad, n_blk), [own_down]
        )
        early = []

    own_bias = own_blocks(qkv_bias, 3 * per_dev, HD).reshape(3, per_dev, HD, 1)
    frequency = 10000.0 ** (-2.0 * np.arange(HALF) / ROT)
    angles = frequency[:, None] * np.arange(span)[None, :]
    cosine, sine = np.cos(angles).astype(np.float32), np.sin(angles).astype(np.float32)

    all_normed, qkv, att, att_low, att_flat, lse = attention_forward(
        position,
        lengths,
        slots,
        qkv_weight,
        own_bias,
        cosine,
        sine,
        normed_pieces,
        per_dev,
        [ffn_out, *early],
    )
    all_grad, grad_cut, grad_qkv = attention_backward(
        position,
        lengths,
        slots,
        out_weight,
        qkv,
        att,
        lse,
        cosine,
        sine,
        grad_pieces,
        n_blk,
    )
    grad_rows = swap_blk(grad_cut)

    sent = jnp.stack([d ^ 3, d ^ 1])
    kept = jnp.stack([d ^ 2, d])

    def over_first(array):
        return lax.ppermute(array, "dp", [(i, i ^ 1) for i in range(4)])

    def over_second(array):
        return lax.ppermute(array, "dp", [(i, i ^ 2) for i in range(4)])

    def row_cut(total):
        return swap_blk(total.reshape(n_blk, -1, total.shape[1]))

    ff_cols, qkv_cols = 2 * n_dp * ff_block, 3 * per_dev * HD
    aligned = per_dev == n_dp
    shards = n_dp * n_blk
    line = 5 * width // shards
    full = [width // n_dp]

    qkv_sent = column_products(sent, all_normed, grad_qkv, 0, qkv_cols, n_dp)
    qkv_first = over_first(qkv_sent)
    act, grad_ff = local_grads(
        all_normed, all_grad, own_gate_up, own_down, n_dp, [qkv_sent]
    )
    lefts = [act, att_low] if aligned else [act]
    qkv_on, qkv_mine = column_products(
        kept, all_normed, grad_qkv, 0, qkv_cols, n_dp, qkv_first, [act]
    )
    qkv_second = over_second(qkv_on)
    ff_sent = column_products(sent, all_normed, grad_ff, 0, ff_cols, n_dp, None, [qkv_on])
    ff_first = over_first(ff_sent)
    row_sent = row_products(sent, lefts, all_grad, None, [ff_sent])
    row_first = over_first(row_sent)
    (att_flat,) = relay([att_flat], [grad_rows])
    att_pieces = swap_blk(att_flat.reshape(n_blk, rows, -1))
    (qkv_total,) = add_second(
        qkv_mine, qkv_second, full, BF16, [row_sent, att_flat], 24
    )
    qkv_pieces = row_cut(qkv_total)
    ff_on, ff_mine = column_products(
        kept, all_normed, grad_ff, 0, ff_cols, n_dp, ff_first, [qkv_total]
    )
    ff_second = over_second(ff_on)
    row_on, row_mine = row_products(kept, lefts, all_grad, row_first, [ff_on])
    (passed,) = relay([passed], [grad_cut])
    ffn_other = beside(passed, n_blk)
    input_grad, vectors = input_grads(
        own_tokens,
        out_grad,
        norm_gain[None],
        ffn_grad,
        ffn_other,
        qkv_weight,
        grad_rows,
        shards,
        [row_on, att_pieces],
    )
    (ff_total,) = add_second(ff_mine, ff_second, full, BF16, [input_grad], 1)
    vectors = vectors.reshape(n_dp, n_blk, line)

    def of(mask):
        return lax.dynamic_index_in_dim(vectors, d ^ mask, 0, keepdims=False)

    vector_first = over_first(jnp.stack([of(3), of(1)]))
    vector_second = over_second(of(2) + vector_first[0])
    (row_on,) = relay([row_on], [vector_second])
    row_second = over_second(row_on)
    layer_out = project_out(own_tokens, ffn_out, ffn_other, out_weight, att_pieces, [input_grad])
    vectors = of(0) + vector_first[1] + vector_second
    below = jnp.pad(vectors.astype(BF16)[:, None], ((0, 0), (0, EXTRA - 1), (0, ff_cols - line)))
    ff_pieces = swap_blk(
        jnp.concatenate([ff_total.reshape(n_blk, -1, ff_cols), below], axis=1)
    )
    sizes = [ff_block, HD] if aligned else [ff_block]
    shard_down, *shard_out = add_second(row_mine, row_second, sizes, F32)
    if aligned:
        shard_out = shard_out[0]
    else:
        grad_out = dot(att_low.reshape(-1, span), all_grad)
        wide = jnp.zeros((width, width), F32)
        for i in range(per_dev):
            start = (n_blk * i + b) * HD
            wide = lax.dynamic_update_slice(wide, grad_out[i * HD : (i + 1) * HD], (start, 0))
        shard_out = lax.psum_scatter(wide, ("dp", "blk"), scatter_dimension=0, tiled=True)
    cut = width // shards
    (shard_qkv,) = spread([qkv_pieces], cut, 1, 3 * per_dev, HD)
    shard_gate, shard_up, sums = spread([ff_pieces], cut, 2, n_dp, ff_block, line)
    sums = sums[0]
    return (
        layer_out[None],
        input_grad[None],
        sums[:cut],
        sums[cut : 2 * cut],
        shard_qkv,
        sums[2 * cut :],
        shard_out,
        shard_gate,
        shard_up,
        shard_down,
    )


def solution(mesh):
    both = P(("dp", "blk"))
    row_cut = P(("dp", "blk"), None)
    activation = P("dp", "blk", None)
    return jax.shard_map(
        functools.partial(on_device, mesh.shape["dp"], mesh.shape["blk"]),
        mesh=mesh,
        in_specs=(activation,) + (P(),) * 8 + (activation, P("dp")),
        out_specs=(activation, activation, both, both, row_cut, both) + (row_cut,) * 4,
        check_vma=False,
    )
```

```python
import functools

import jax
import jax.numpy as jnp
import numpy as np
from jax import lax
from jax.experimental import pallas as pl
from jax.experimental.pallas import tpu as pltpu
from jax.sharding import PartitionSpec as P

HD = 64
ROT = 16
HALF = ROT // 2

epsilon = 1e-05
masked_score = -1e30
BQ = 256
LANES = 128
EXTRA = 8
SCALE = 1.0
F32 = jnp.float32
BF16 = jnp.bfloat16


def dot(left, right, left_dim=1, right_dim=0):
    return lax.dot_general(
        left, right, (((left_dim,), (right_dim,)), ((), ())), preferred_element_type=F32
    )


RING = [0, 1, 3, 2]
ALONG = [(2 * RING[r] + y, 2 * RING[(r + 1) % 4] + y) for r in range(4) for y in range(2)]


def along(piece):
    return lax.ppermute(piece, "blk", ALONG)


def back(piece):
    return lax.ppermute(piece, "blk", [(target, source) for source, target in ALONG])


def beside(piece, n_blk):
    return lax.ppermute(piece, "blk", [(i, i ^ 1) for i in range(n_blk)])


def piece_slots(b):
    z, y = b // 2, b % 2
    place = z ^ (z >> 1)
    slots = []
    for step in (0, 1, 3, 2):
        slot = (place - step) % 4
        source = slot ^ (slot >> 1)
        slots += [2 * source + y, 2 * source + 1 - y]
    return jnp.stack(slots).astype(jnp.int32)


def swap_blk(pieces):
    return lax.all_to_all(pieces, "blk", split_axis=0, concat_axis=0, tiled=True)


def rotated(block, cosine, sine):
    a, b = block[:HALF], block[HALF:ROT]
    return jnp.concatenate([a * cosine - b * sine, b * cosine + a * sine, block[ROT:]], axis=0)


def masked_scores(keys, queries, start, length):
    scores = dot(keys, queries, 0, 0) * HD**-0.5
    key_pos = lax.broadcasted_iota(jnp.int32, scores.shape, 0)
    query_pos = start + lax.broadcasted_iota(jnp.int32, (1, scores.shape[1]), 1)
    allowed = key_pos <= jnp.minimum(query_pos, length - 1)
    return jnp.where(allowed, scores, masked_score)


ANY = pl.BlockSpec(memory_space=pl.ANY)
VMEM = pl.BlockSpec(memory_space=pltpu.VMEM)
SMEM = pl.BlockSpec(memory_space=pltpu.SMEM)


def kernel_call(kernel, args, after=(), prefetch=0, **options):
    in_specs = list(options.pop("in_specs")) + [ANY] * len(after)
    count = len(args)

    def body(*refs):
        kernel(*refs[:count], *refs[count + len(after) :])

    if prefetch:
        options["grid_spec"] = pltpu.PrefetchScalarGridSpec(
            num_scalar_prefetch=prefetch,
            in_specs=in_specs,
            **{k: options.pop(k) for k in ("grid", "out_specs", "scratch_shapes") if k in options},
        )
    else:
        options["in_specs"] = in_specs
    return pl.pallas_call(body, **options)(*args, *after)


def relay(arrays, after):
    count = len(arrays)
    return pl.pallas_call(
        lambda *refs: None,
        in_specs=[ANY] * (count + len(after)),
        out_specs=[ANY] * count,
        out_shape=[jax.ShapeDtypeStruct(array.shape, array.dtype) for array in arrays],
        input_output_aliases={k: k for k in range(count)},
        compiler_params=pltpu.CompilerParams(has_side_effects=True),
        cost_estimate=takes(1),
        name="relay",
    )(*arrays, *after)


def takes(us):
    return pl.CostEstimate(flops=int(us * SCALE * 1.15e9), bytes_accessed=1 << 16, transcendentals=0)


def params(mib):
    return pltpu.CompilerParams(vmem_limit_bytes=mib << 20)


def ffn_kernel(
    tile,
    b_ref,
    n_ref,
    n_other,
    c_ref,
    c_other,
    gate_ref,
    up_ref,
    down_ref,
    out_ref,
    grad_ref,
    pass_ref,
    normed,
    flipped,
    gate_w,
    up_w,
    down_w,
    act,
    grad_gate,
    grad_up,
    sems,
):
    rows, width = n_ref.shape
    half = gate_w.shape[1]
    count = half // tile
    base = b_ref[0] % 2 * half

    def copies(t):
        here = pl.ds(pl.multiple_of(t * tile, tile), tile)
        there = pl.ds(pl.multiple_of(base + t * tile, LANES), tile)
        return [
            pltpu.make_async_copy(gate_ref.at[:, there], gate_w.at[:, here], sems.at[0, t]),
            pltpu.make_async_copy(up_ref.at[:, there], up_w.at[:, here], sems.at[1, t]),
            pltpu.make_async_copy(down_ref.at[there, :], down_w.at[here, :], sems.at[2, t]),
        ]

    for t in range(count):
        for copy in copies(t):
            copy.start()
    normed[:rows, :] = n_ref[...]
    normed[rows:, :] = n_other[...]
    flipped[:, :rows] = c_ref[...].T
    flipped[:, rows:] = c_other[...].T

    def first(t, carry):
        for copy in copies(t):
            copy.wait()
        here = pl.ds(pl.multiple_of(t * tile, tile), tile)
        gate = dot(normed[...], gate_w[:, here])
        up = dot(normed[...], up_w[:, here])
        grad_act = dot(down_w[here, :], flipped[...])
        sig = jax.nn.sigmoid(gate)
        silu = gate * sig
        act[:, here] = (silu * up).astype(BF16)
        by_gate = (up * sig * (1.0 + gate * (1.0 - sig))).T
        grad_gate[here, :] = (grad_act * by_gate).astype(BF16)
        grad_up[here, :] = (grad_act * silu.T).astype(BF16)
        return carry

    lax.fori_loop(0, count, first, 0)
    step = 512

    def second(r, carry):
        here = pl.ds(pl.multiple_of(r * step, step), step)
        out = dot(act[...], down_w[:, here])
        out_ref[:, here] = out[:rows]
        pass_ref[0, :, here] = out[rows:].astype(BF16)
        grad = (dot(gate_w[here, :], grad_gate[...]) + dot(up_w[here, :], grad_up[...])).T
        grad_ref[:, here] = grad[:rows]
        pass_ref[1, :, here] = grad[rows:].astype(BF16)
        return carry

    lax.fori_loop(0, width // step, second, 0)


def feed_forward(b, normed, out_grad, weights, after):
    rows, width = normed[0].shape
    half = weights[0].shape[1] // 2
    tile = 256
    return kernel_call(
        functools.partial(ffn_kernel, tile),
        (b, *normed, *out_grad, *weights),
        after,
        in_specs=[SMEM] + [VMEM] * 4 + [ANY] * 3,
        out_specs=[VMEM] * 3,
        out_shape=[
            jax.ShapeDtypeStruct((rows, width), F32),
            jax.ShapeDtypeStruct((rows, width), F32),
            jax.ShapeDtypeStruct((2, rows, width), BF16),
        ],
        scratch_shapes=[
            pltpu.VMEM((2 * rows, width), BF16),
            pltpu.VMEM((width, 2 * rows), BF16),
            pltpu.VMEM((width, half), BF16),
            pltpu.VMEM((width, half), BF16),
            pltpu.VMEM((half, width), BF16),
            pltpu.VMEM((2 * rows, half), BF16),
            pltpu.VMEM((half, 2 * rows), BF16),
            pltpu.VMEM((half, 2 * rows), BF16),
            pltpu.SemaphoreType.DMA((3, half // tile)),
        ],
        compiler_params=params(54),
        cost_estimate=takes(24),
        name="feed_forward",
    )


def cut_columns(size, weight, starts, window, held, sems):
    copies = []
    for k, column in enumerate(starts):
        aligned = pl.multiple_of(
            jnp.minimum(column // LANES * LANES, weight.shape[1] - window), LANES
        )
        copy = pltpu.make_async_copy(weight.at[:, pl.ds(aligned, window)], held.at[k], sems.at[k])
        copy.start()
        copies.append((copy, column - aligned))
    return copies


def place_columns(size, copies, held, out_ref, first):
    depth, window = held.shape[-2:]
    step = min(256, depth)
    for k, (copy, offset) in enumerate(copies):
        copy.wait()
        start = (first + k) * size
        place = start % LANES
        for r in range(0, depth, step):
            block = pltpu.roll(held[k, r : r + step, :], window - offset + place, 1)
            out_ref[r : r + step, start : start + size] = block[:, place : place + size]


def slice_kernel(
    size,
    starts,
    qkv_starts,
    b_ref,
    gate_ref,
    up_ref,
    down_ref,
    qkv_ref,
    out_ref,
    turned_ref,
    qkv_out,
    gate_held,
    up_held,
    qkv_held,
    rows,
    gate_sems,
    up_sems,
    qkv_sems,
    row_sems,
):
    depth, window = gate_held.shape[-2:]
    b = b_ref[0]
    gates = cut_columns(size, gate_ref, starts(b), window, gate_held, gate_sems)
    ups = cut_columns(size, up_ref, starts(b), window, up_held, up_sems)
    row_copies = []
    if down_ref.shape[0] > rows.shape[0]:
        for i, row in enumerate(starts(b)):
            row_copies.append(
                pltpu.make_async_copy(
                    down_ref.at[pl.ds(pl.multiple_of(row, size), size), :],
                    rows.at[pl.ds(i * size, size), :],
                    row_sems.at[i],
                )
            )
    else:
        row_copies.append(pltpu.make_async_copy(down_ref, rows, row_sems.at[0]))
    for copy in row_copies:
        copy.start()
    heads = cut_columns(HD, qkv_ref, qkv_starts(b), LANES, qkv_held, qkv_sems)
    place_columns(size, gates, gate_held, out_ref, 0)
    place_columns(size, ups, up_held, out_ref, len(gates))
    for copy in row_copies:
        copy.wait()
    step = min(256, depth)
    for r in range(0, depth, step):
        turned_ref[r : r + step, :] = rows[:, r : r + step].T
    place_columns(HD, heads, qkv_held, qkv_out, 0)


def own_slices(b, gate, up, down, qkv, starts, qkv_starts, count, size, after=()):
    depth = gate.shape[0]
    heads = len(qkv_starts(0))
    window = LANES * ((size + 2 * LANES - 2) // LANES)
    held = pltpu.VMEM((count, depth, window), BF16)
    sems = pltpu.SemaphoreType.DMA((count,))
    return kernel_call(
        functools.partial(slice_kernel, size, starts, qkv_starts),
        (b, gate, up, down, qkv),
        after,
        in_specs=[SMEM] + [ANY] * 4,
        out_specs=[VMEM] * 3,
        out_shape=[
            jax.ShapeDtypeStruct((depth, 2 * count * size), BF16),
            jax.ShapeDtypeStruct((depth, count * size), BF16),
            jax.ShapeDtypeStruct((depth, heads * HD), BF16),
        ],
        scratch_shapes=[
            held,
            held,
            pltpu.VMEM((heads, depth, LANES), BF16),
            pltpu.VMEM((count * size, depth), BF16),
            sems,
            sems,
            pltpu.SemaphoreType.DMA((heads,)),
            sems,
        ],
        compiler_params=params(44),
        cost_estimate=takes(14),
        name="own_slices",
    )


def fetch_rows(slots_ref, pieces, whole_ref, sems):
    rows = pieces[0].shape[0]
    copies = []
    for k, piece in enumerate(pieces):
        place = pl.multiple_of(slots_ref[k] * rows, rows)
        copies.append(
            pltpu.make_async_copy(piece, whole_ref.at[pl.ds(place, rows), :], sems.at[k])
        )
        copies[-1].start()
    return copies


def forward_kernel(
    count, length_ref, slots_ref, weight_ref, bias_ref, cos_ref, sin_ref, *refs
):
    pieces = refs[:count]
    whole_out, qkv_ref, att_ref, low_ref, lse_ref, whole_ref, sems, out_sem = refs[count:]
    _, heads, _, span = qkv_ref.shape
    length = length_ref[0]
    for copy in fetch_rows(slots_ref, pieces, whole_ref, sems):
        copy.wait()
    leaving = pltpu.make_async_copy(whole_ref, whole_out, out_sem)
    leaving.start()
    cosine, sine = cos_ref[...], sin_ref[...]
    step = 256
    for r in range(0, span, step):
        flat = dot(whole_ref[r : r + step, :], weight_ref[...]).T
        for k in range(3 * heads):
            part, i = k // heads, k % heads
            own = flat[k * HD : (k + 1) * HD, :] + bias_ref[part, i]
            if part < 2:
                own = rotated(own, cosine[:, r : r + step], sine[:, r : r + step])
            qkv_ref[part, i, :, r : r + step] = own.astype(BF16)

    def head(i, carry):
        for start in range(0, span, BQ):
            end = start + BQ
            scores = masked_scores(
                qkv_ref[1, i, :, :end], qkv_ref[0, i, :, start:end], start, length
            )
            best = jnp.max(scores, axis=0, keepdims=True)
            weights = jnp.exp(scores - best)
            total = jnp.sum(weights, axis=0, keepdims=True)
            out = dot(qkv_ref[2, i, :, :end], weights.astype(BF16)) / total
            att_ref[i, :, start:end] = out
            low_ref[i, :, start:end] = out.astype(BF16)
            lse_ref[i, :, start:end] = best + jnp.log(total)
        return carry

    lax.fori_loop(0, heads, head, 0)
    leaving.wait()


def attention_forward(length, slots, weight, bias, cosine, sine, pieces, heads, after):
    width = weight.shape[0]
    span = len(pieces) * pieces[0].shape[0]
    count = len(pieces)
    return kernel_call(
        functools.partial(forward_kernel, count),
        (length, slots, weight, bias, cosine, sine, *pieces),
        after,
        in_specs=[SMEM, SMEM, VMEM, VMEM, VMEM, VMEM] + [ANY] * count,
        out_specs=[ANY] + [VMEM] * 4,
        out_shape=[
            jax.ShapeDtypeStruct((span, width), BF16),
            jax.ShapeDtypeStruct((3, heads, HD, span), BF16),
            jax.ShapeDtypeStruct((heads, HD, span), F32),
            jax.ShapeDtypeStruct((heads, HD, span), BF16),
            jax.ShapeDtypeStruct((heads, 1, span), F32),
        ],
        scratch_shapes=[
            pltpu.VMEM((span, width), BF16),
            pltpu.SemaphoreType.DMA((count,)),
            pltpu.SemaphoreType.DMA,
        ],
        compiler_params=params(48),
        cost_estimate=takes(20),
        name="attention_forward",
    )


def backward_kernel(
    count, b_ref, length_ref, slots_ref, weight_ref, qkv_ref, att_ref, lse_ref, cos_ref, sin_ref, *refs
):
    pieces = refs[:count]
    (
        whole_out,
        out_ref,
        flat_ref,
        whole_ref,
        weight,
        grad_ref,
        dq,
        dk,
        dv,
        turned,
        weight_sem,
        sems,
        out_sem,
    ) = refs[count:]
    _, heads, _, span = qkv_ref.shape
    length = length_ref[0]
    scale = HD**-0.5
    cosine, sine = cos_ref[...], -sin_ref[...]
    n_blk = out_ref.shape[0]
    copies = fetch_rows(slots_ref, pieces, whole_ref, sems)
    for i in range(heads):
        row = pl.multiple_of((n_blk * i + b_ref[0]) * HD, HD)
        copies.append(
            pltpu.make_async_copy(
                weight_ref.at[pl.ds(row, HD), :],
                weight.at[pl.ds(i * HD, HD), :],
                weight_sem.at[i],
            )
        )
        copies[-1].start()
    for copy in copies:
        copy.wait()
    leaving = pltpu.make_async_copy(whole_ref, whole_out, out_sem)
    leaving.start()
    across = weight[...].T
    for start in range(0, span, BQ):
        grads = dot(whole_ref[start : start + BQ, :], across).T.astype(BF16)
        for i in range(heads):
            grad_ref[i, :, start : start + BQ] = grads[i * HD : (i + 1) * HD, :]

    def head(i, carry):
        dk[...] = jnp.zeros_like(dk)
        dv[...] = jnp.zeros_like(dv)
        for start in range(0, span, BQ):
            end = start + BQ
            keys, values = qkv_ref[1, i, :, :end], qkv_ref[2, i, :, :end]
            queries, grads = qkv_ref[0, i, :, start:end], grad_ref[i, :, start:end]
            delta = jnp.sum(grads.astype(F32) * att_ref[i, :, start:end], axis=0, keepdims=True)
            scores = masked_scores(keys, queries, start, length)
            prob = jnp.exp(scores - lse_ref[i, :, start:end])
            grad_prob = dot(values, grads, 0, 0)
            grad_score = (prob * (grad_prob - delta)).astype(BF16)
            dq[:, start:end] = dot(keys, grad_score) * scale
            dk[:, :end] += dot(queries, grad_score, 1, 1)
            dv[:, :end] += dot(grads, prob.astype(BF16), 1, 1)
        turned[0, i] = rotated(dq[...], cosine, sine).astype(BF16)
        turned[1, i] = rotated(dk[...] * scale, cosine, sine).astype(BF16)
        turned[2, i] = dv[...].astype(BF16)
        return carry

    lax.fori_loop(0, heads, head, 0)
    rows = out_ref.shape[2]
    for part in range(3):
        for i in range(heads):
            k = part * heads + i
            flat_ref[:, k * HD : (k + 1) * HD] = turned[part, i].T
            for j in range(n_blk):
                out_ref[j, k * HD : (k + 1) * HD, :] = turned[part, i, :, j * rows : (j + 1) * rows]
    for i in range(heads):
        k = 3 * heads + i
        for j in range(n_blk):
            out_ref[j, k * HD : (k + 1) * HD, :] = att_ref[
                i, :, j * rows : (j + 1) * rows
            ].astype(BF16)
    leaving.wait()


def attention_backward(
    b, length, slots, weight, qkv, att, lse, cosine, sine, pieces, n_blk, after=()
):
    _, heads, _, span = qkv.shape
    width = weight.shape[1]
    count = len(pieces)
    return kernel_call(
        functools.partial(backward_kernel, count),
        (b, length, slots, weight, qkv, att, lse, cosine, sine, *pieces),
        after,
        in_specs=[SMEM, SMEM, SMEM, ANY] + [VMEM] * 5 + [ANY] * count,
        out_specs=[ANY] + [VMEM] * 2,
        out_shape=[
            jax.ShapeDtypeStruct((span, width), BF16),
            jax.ShapeDtypeStruct((n_blk, 4 * heads * HD, span // n_blk), BF16),
            jax.ShapeDtypeStruct((span, 3 * heads * HD), BF16),
        ],
        scratch_shapes=[
            pltpu.VMEM((span, width), BF16),
            pltpu.VMEM((heads * HD, width), BF16),
            pltpu.VMEM((heads, HD, span), BF16),
        ]
        + [pltpu.VMEM((HD, span), F32)] * 3
        + [
            pltpu.VMEM((3, heads, HD, span), BF16),
            pltpu.SemaphoreType.DMA((heads,)),
            pltpu.SemaphoreType.DMA((count,)),
            pltpu.SemaphoreType.DMA,
        ],
        compiler_params=params(40),
        cost_estimate=takes(18),
        name="attention_backward",
    )


def grads_kernel(n_dp, n_ref, c_ref, gate_up_ref, down_ref, act_ref, grad_ref):
    cols = down_ref.shape[1]
    both = dot(n_ref[...], gate_up_ref[...])
    gate, up = both[:, :cols], both[:, cols:]
    sig = jax.nn.sigmoid(gate)
    silu = gate * sig
    act = silu * up
    part = cols // n_dp
    for i in range(n_dp):
        act_ref[i] = act[:, i * part : (i + 1) * part].T.astype(BF16)
    grad_act = dot(c_ref[...], down_ref[...])
    grad_ref[:, :cols] = (grad_act * up * sig * (1.0 + gate * (1.0 - sig))).astype(BF16)
    grad_ref[:, cols:] = (grad_act * silu).astype(BF16)


def local_grads(all_normed, all_grad, gate_up, down, n_dp, after=()):
    span, width = all_normed.shape
    cols = down.shape[1]
    size = 256
    return kernel_call(
        functools.partial(grads_kernel, n_dp),
        (all_normed, all_grad, gate_up, down),
        after,
        grid=(span // size,),
        in_specs=[
            pl.BlockSpec((size, width), lambda r: (r, 0)),
            pl.BlockSpec((size, width), lambda r: (r, 0)),
            pl.BlockSpec((width, 2 * cols), lambda r: (0, 0)),
            pl.BlockSpec((width, cols), lambda r: (0, 0)),
        ],
        out_specs=[
            pl.BlockSpec((n_dp, cols // n_dp, size), lambda r: (0, 0, r)),
            pl.BlockSpec((size, 2 * cols), lambda r: (r, 0)),
        ],
        out_shape=[
            jax.ShapeDtypeStruct((n_dp, cols // n_dp, span), BF16),
            jax.ShapeDtypeStruct((span, 2 * cols), BF16),
        ],
        compiler_params=params(48),
        cost_estimate=takes(15),
        name="local_grads",
    )


def keep(value, first, on_ref, mine_ref, cut):
    value += first.astype(F32)

    @pl.when(pl.program_id(0) < cut)
    def _():
        on_ref[...] = value.astype(BF16)

    @pl.when(pl.program_id(0) >= cut)
    def _():
        mine_ref[...] = value


def column_products_kernel(low, high, order_ref, left_ref, right_ref, *refs):
    value = dot(left_ref[...], right_ref[:, low:high], 0, 0)
    if len(refs) == 1:
        refs[0][0] = value.astype(BF16)
    else:
        keep(value, refs[0][0, :, low:high], *refs[1:], 2)


def column_products(order, left, right, low, high, n_dp, first=None, after=()):
    span, width = left.shape
    cols = high - low
    size = width // n_dp
    part = size // 2
    stay = [
        pl.BlockSpec((part, cols), lambda j, order: (jnp.minimum(j, 1), 0)),
        pl.BlockSpec((part, cols), lambda j, order: (jnp.maximum(j - 2, 0), 0)),
    ]
    block = pl.BlockSpec(
        (1, part, cols if first is None else right.shape[1]), lambda j, order: (j // 2, j % 2, 0)
    )
    return kernel_call(
        functools.partial(column_products_kernel, low, high),
        (order, left, right) + (() if first is None else (first,)),
        after,
        prefetch=1,
        grid=(4,),
        in_specs=[
            pl.BlockSpec((span, part), lambda j, order: (0, order[j // 2] * 2 + j % 2)),
            pl.BlockSpec(right.shape, lambda j, order: (0, 0)),
        ]
        + ([] if first is None else [block]),
        out_specs=block if first is None else stay,
        out_shape=jax.ShapeDtypeStruct((2, size, cols), BF16)
        if first is None
        else [jax.ShapeDtypeStruct((size, cols), dtype) for dtype in (BF16, F32)],
        compiler_params=params(24),
        cost_estimate=takes(8),
        name="column_products",
    )


def row_products_kernel(count, order_ref, *refs):
    lefts, right_ref, rest = refs[:count], refs[count], refs[count + 1 :]
    value = [dot(left[0], right_ref[...]) for left in lefts]
    value = jnp.concatenate(value, axis=0) if count > 1 else value[0]
    if len(rest) == 1:
        rest[0][0] = value.astype(BF16)
    else:
        keep(value, rest[0][0], *rest[1:], 1)


def row_products(order, lefts, right, first=None, after=()):
    span, width = right.shape
    size = sum(left.shape[1] for left in lefts)
    block = pl.BlockSpec((1, size, width), lambda j, order: (j, 0, 0))
    stay = pl.BlockSpec((size, width), lambda j, order: (0, 0))
    return kernel_call(
        functools.partial(row_products_kernel, len(lefts)),
        (order, *lefts, right) + (() if first is None else (first,)),
        after,
        prefetch=1,
        grid=(2,),
        in_specs=[
            pl.BlockSpec((1,) + left.shape[1:], lambda j, order: (order[j], 0, 0))
            for left in lefts
        ]
        + [pl.BlockSpec((span, width), lambda j, order: (0, 0))]
        + ([] if first is None else [block]),
        out_specs=block if first is None else [stay, stay],
        out_shape=jax.ShapeDtypeStruct((2, size, width), BF16)
        if first is None
        else [jax.ShapeDtypeStruct((size, width), dtype) for dtype in (BF16, F32)],
        compiler_params=params(24),
        cost_estimate=takes(8),
        name="row_products",
    )


def add_kernel(mine_ref, second_ref, *out_refs):
    total = mine_ref[...] + second_ref[...].astype(F32)
    start = 0
    for out_ref in out_refs:
        size = out_ref.shape[0]
        out_ref[...] = total[start : start + size].astype(out_ref.dtype)
        start += size


def add_second(mine, second, sizes, dtype, after=(), us=16):
    _, cols = mine.shape
    return kernel_call(
        add_kernel,
        (mine, second),
        after,
        in_specs=[VMEM] * 2,
        out_specs=[VMEM] * len(sizes),
        out_shape=[jax.ShapeDtypeStruct((part, cols), dtype) for part in sizes],
        compiler_params=params(16),
        cost_estimate=takes(us),
        name="add_second",
    )


def spread_kernel(count, outer, size, line, *refs):
    arrays, out_refs = refs[:count], refs[count:]
    n_blk = arrays[0].shape[0]
    if line:
        out_refs, line_refs = out_refs[:-3], out_refs[-3:]
        rows = out_refs[0].shape[0]
        sums = sum(arrays[-1][b, rows : rows + EXTRA, :line].astype(F32) for b in range(n_blk))
        start = 0
        for line_ref in line_refs:
            end = start + line_ref.shape[1]
            line_ref[...] = sums[:1, start:end]
            start = end
    for k, out_ref in enumerate(out_refs):
        rows = out_ref.shape[0]
        for i in range(outer):
            for b in range(n_blk):
                source = (k * outer + i) * size
                place = (i * n_blk + b) * size
                start = 0
                for array in arrays:
                    end = start + array.shape[2]
                    low, high = max(source, start), min(source + size, end)
                    if low < high:
                        out_ref[:, place + low - source : place + high - source] = array[
                            b, :rows, low - start : high - start
                        ].astype(F32)
                    start = end


def spread(arrays, rows, outputs, outer, size, line=0, after=()):
    n_blk = arrays[0].shape[0]
    return kernel_call(
        functools.partial(spread_kernel, len(arrays), outer, size, line),
        tuple(arrays),
        after,
        in_specs=[VMEM] * len(arrays),
        out_specs=[VMEM] * (outputs + 3 * (line > 0)),
        out_shape=[jax.ShapeDtypeStruct((rows, outer * n_blk * size), F32)] * outputs
        + [jax.ShapeDtypeStruct((1, n * line // 5), F32) for n in (1, 1, 3) if line],
        compiler_params=params(16),
        cost_estimate=takes(3),
        name="spread",
    )


def out_kernel(x_ref, ffn_ref, other_ref, weight_ref, pieces, out_ref, left, total):
    n_blk, lines, _ = pieces.shape
    heads = lines // HD // 4
    step = pl.program_id(0)
    size = left.shape[2]

    @pl.when(step == 0)
    def _():
        for i in range(heads):
            for b in range(n_blk):
                place = (i * n_blk + b) * HD
                block, start = place // size, place % size
                k = 3 * heads + i
                left[block, :, start : start + HD] = pieces[b, k * HD : (k + 1) * HD, :].T
        total[...] = x_ref[...].astype(F32) + ffn_ref[...] + other_ref[0].astype(F32)

    total[...] += dot(left[step], weight_ref[...])

    @pl.when(step == pl.num_programs(0) - 1)
    def _():
        out_ref[...] = total[...].astype(BF16)


def project_out(tokens, ffn_out, other, weight, pieces, after=()):
    rows, width = tokens.shape
    steps = 4
    size = width // steps
    whole = pl.BlockSpec((rows, width), lambda t: (0, 0))
    return kernel_call(
        out_kernel,
        (tokens, ffn_out, other, weight, pieces),
        after,
        grid=(steps,),
        in_specs=[
            whole,
            whole,
            pl.BlockSpec((1, rows, width), lambda t: (0, 0, 0)),
            pl.BlockSpec((size, width), lambda t: (t, 0)),
            pl.BlockSpec(pieces.shape, lambda t: (0, 0, 0)),
        ],
        out_specs=whole,
        out_shape=jax.ShapeDtypeStruct((rows, width), BF16),
        scratch_shapes=[pltpu.VMEM((steps, rows, size), BF16), pltpu.VMEM((rows, width), F32)],
        compiler_params=params(20),
        cost_estimate=takes(6),
        name="project_out",
    )


def input_kernel(
    x_ref, c_ref, gain_ref, ffn_ref, other_ref, weight_ref, pieces, out_ref, sums_ref, left, total
):
    n_blk, lines, _ = pieces.shape
    step, steps = pl.program_id(0), pl.num_programs(0)
    size = left.shape[1]

    @pl.when(step == 0)
    def _():
        for i in range(3 * (lines // HD // 4)):
            for b in range(n_blk):
                place = (i * n_blk + b) * HD
                block, start = place // size, place % size
                left[block, start : start + HD, :] = pieces[b, i * HD : (i + 1) * HD, :]
        total[...] = jnp.zeros_like(total)

    total[...] += dot(weight_ref[...], left[step])

    @pl.when(step == steps - 1)
    def _():
        x = x_ref[...].astype(F32)
        center = x - jnp.mean(x, axis=1, keepdims=True)
        inverse_std = lax.rsqrt(jnp.mean(center * center, axis=1, keepdims=True) + epsilon)
        normalized = center * inverse_std
        grad = ffn_ref[...] + other_ref[0].astype(F32) + total[...].T
        vectors = [
            jnp.sum(grad * normalized, axis=0, keepdims=True),
            jnp.sum(grad, axis=0, keepdims=True),
        ] + [jnp.sum(left[t].astype(F32).T, axis=0, keepdims=True) for t in range(left.shape[0])]
        flat = jnp.concatenate(vectors, axis=1)
        shards = sums_ref.shape[0]
        width = grad.shape[1]
        cut = width // shards
        for j in range(shards):
            sums_ref[j : j + 1, :cut] = flat[:, j * cut : (j + 1) * cut]
            sums_ref[j : j + 1, cut : 2 * cut] = flat[:, width + j * cut : width + (j + 1) * cut]
            start = 2 * width + 3 * j * cut
            sums_ref[j : j + 1, 2 * cut :] = flat[:, start : start + 3 * cut]
        grad = grad * gain_ref[...]
        grad_inputs = inverse_std * (
            grad
            - jnp.mean(grad, axis=1, keepdims=True)
            - normalized * jnp.mean(grad * normalized, axis=1, keepdims=True)
        )
        out_ref[...] = (c_ref[...].astype(F32) + grad_inputs).astype(BF16)


def input_grads(
    tokens, out_grad, gain, ffn_grad, other, weight, pieces, shards, after=()
):
    rows, width = tokens.shape
    cols = weight.shape[1]
    steps = 8
    size = cols // steps
    whole = pl.BlockSpec((rows, width), lambda t: (0, 0))
    return kernel_call(
        input_kernel,
        (tokens, out_grad, gain, ffn_grad, other, weight, pieces),
        after,
        grid=(steps,),
        in_specs=[
            whole,
            whole,
            pl.BlockSpec((1, width), lambda t: (0, 0)),
            whole,
            pl.BlockSpec((1, rows, width), lambda t: (1, 0, 0)),
            pl.BlockSpec((width, size), lambda t: (0, t)),
            pl.BlockSpec(pieces.shape, lambda t: (0, 0, 0)),
        ],
        out_specs=[whole, pl.BlockSpec((shards, 5 * width // shards), lambda t: (0, 0))],
        out_shape=[
            jax.ShapeDtypeStruct((rows, width), BF16),
            jax.ShapeDtypeStruct((shards, 5 * width // shards), F32),
        ],
        scratch_shapes=[pltpu.VMEM((steps, size, rows), BF16), pltpu.VMEM((width, rows), F32)],
        compiler_params=params(28),
        cost_estimate=takes(13),
        name="input_grads",
    )


def on_device(
    n_dp,
    n_blk,
    tokens,
    norm_gain,
    norm_bias,
    qkv_weight,
    qkv_bias,
    out_weight,
    gate_weight,
    up_weight,
    down_weight,
    cotangent,
    lengths,
):
    rows, width = tokens.shape[1:]
    span = rows * n_blk
    hidden = gate_weight.shape[1]
    per_dev = width // HD // n_blk
    ff_block = hidden // (n_dp * n_blk)
    d, b = lax.axis_index("dp").astype(jnp.int32), lax.axis_index("blk").astype(jnp.int32)
    own_tokens, out_grad = tokens[0], cotangent[0]

    inputs = own_tokens.astype(F32)
    center = inputs - jnp.mean(inputs, axis=1, keepdims=True)
    inverse_std = lax.rsqrt(jnp.mean(center * center, axis=1, keepdims=True) + epsilon)
    normed = (center * inverse_std * norm_gain + norm_bias).astype(BF16)

    position = b.reshape(1)

    def ff_starts(b):
        return [(n_blk * i + b) * ff_block for i in range(n_dp)]

    def qkv_starts(b):
        return [part * width + (n_blk * i + b) * HD for part in range(3) for i in range(per_dev)]

    def own_blocks(array, outer, size):
        cut = array.reshape((outer, n_blk, size) + array.shape[1:])
        return lax.dynamic_index_in_dim(cut, b, 1, keepdims=False).reshape(
            (-1,) + array.shape[1:]
        )

    down_rows = down_weight if ff_block % 16 == 0 else own_blocks(down_weight, n_dp, ff_block)

    def slices():
        return own_slices(
            position,
            gate_weight,
            up_weight,
            down_rows,
            qkv_weight,
            ff_starts,
            qkv_starts,
            n_dp,
            ff_block,
        )

    def ffn(normed_other, grad_other, after):
        return feed_forward(
            position,
            (normed, normed_other),
            (out_grad, grad_other),
            (gate_weight, up_weight, down_weight),
            after,
        )

    if n_blk == 8:
        slots = piece_slots(b)
        n1, m0, c1, e0 = along(normed), beside(normed, 8), along(out_grad), beside(out_grad, 8)
        own_gate_up, own_down, own_qkv = slices()
        n1, c1, n3 = relay([n1, c1, normed], [own_down])
        n2, m1, c2, e1 = along(n1), beside(n1, 8), along(c1), beside(c1, 8)
        n3 = back(n3)
        ffn_out, ffn_grad, passed = ffn(m0, e0, [n1, c1])
        n2, c3 = relay([n2, out_grad], [ffn_out, m1, e1])
        m2, c3 = beside(n2, 8), back(c3)
        (n3,) = relay([n3], [n2])
        m3 = beside(n3, 8)
        (c2,) = relay([c2], [n3])
        e2 = beside(c2, 8)
        (c3,) = relay([c3], [c2])
        e3 = beside(c3, 8)
        normed_pieces = [normed, m0, n1, m1, n3, m3, n2, m2]
        grad_pieces = [out_grad, e0, c1, e1, c3, e3, c2, e2]
        early = [c3]
    else:
        slots = jnp.zeros((1,), jnp.int32)
        normed_pieces = [lax.all_gather(normed, "blk", axis=0, tiled=True)]
        grad_pieces = [lax.all_gather(out_grad, "blk", axis=0, tiled=True)]
        own_gate_up, own_down, own_qkv = slices()
        ffn_out, ffn_grad, passed = ffn(
            beside(normed, n_blk), beside(out_grad, n_blk), [own_down]
        )
        early = []

    own_bias = own_blocks(qkv_bias, 3 * per_dev, HD).reshape(3, per_dev, HD, 1)
    frequency = 10000.0 ** (-2.0 * np.arange(HALF) / ROT)
    angles = frequency[:, None] * np.arange(span)[None, :]
    cosine, sine = np.cos(angles).astype(np.float32), np.sin(angles).astype(np.float32)

    all_normed, qkv, att, att_low, lse = attention_forward(
        lengths,
        slots,
        own_qkv,
        own_bias,
        cosine,
        sine,
        normed_pieces,
        per_dev,
        [ffn_out, *early],
    )
    all_grad, grad_cut, grad_qkv = attention_backward(
        position,
        lengths,
        slots,
        out_weight,
        qkv,
        att,
        lse,
        cosine,
        sine,
        grad_pieces,
        n_blk,
    )
    grad_rows = swap_blk(grad_cut)

    sent = jnp.stack([d ^ 3, d ^ 1])
    kept = jnp.stack([d ^ 2, d])

    def over_first(array):
        return lax.ppermute(array, "dp", [(i, i ^ 1) for i in range(4)])

    def over_second(array):
        return lax.ppermute(array, "dp", [(i, i ^ 2) for i in range(4)])

    def row_cut(total):
        return swap_blk(total.reshape(n_blk, -1, total.shape[1]))

    ff_cols, qkv_cols = 2 * n_dp * ff_block, 3 * per_dev * HD
    aligned = per_dev == n_dp
    shards = n_dp * n_blk
    line = 5 * width // shards
    full = [width // n_dp]

    qkv_sent = column_products(sent, all_normed, grad_qkv, 0, qkv_cols, n_dp)
    qkv_first = over_first(qkv_sent)
    act, grad_ff = local_grads(
        all_normed, all_grad, own_gate_up, own_down, n_dp, [qkv_sent]
    )
    lefts = [act, att_low] if aligned else [act]
    qkv_on, qkv_mine = column_products(
        kept, all_normed, grad_qkv, 0, qkv_cols, n_dp, qkv_first, [act]
    )
    qkv_second = over_second(qkv_on)
    ff_sent = column_products(sent, all_normed, grad_ff, 0, ff_cols, n_dp, None, [qkv_on])
    ff_first = over_first(ff_sent)
    row_sent = row_products(sent, lefts, all_grad, None, [ff_sent])
    row_first = over_first(row_sent)
    (qkv_total,) = add_second(qkv_mine, qkv_second, full, BF16, [row_sent], 24)
    qkv_pieces = row_cut(qkv_total)
    ff_on, ff_mine = column_products(
        kept, all_normed, grad_ff, 0, ff_cols, n_dp, ff_first, [qkv_total]
    )
    ff_second = over_second(ff_on)
    row_on, row_mine = row_products(kept, lefts, all_grad, row_first, [ff_on])
    (passed,) = relay([passed], [grad_cut])
    ffn_other = beside(passed, n_blk)
    input_grad, vectors = input_grads(
        own_tokens,
        out_grad,
        norm_gain[None],
        ffn_grad,
        ffn_other,
        qkv_weight,
        grad_rows,
        shards,
        [row_on],
    )
    (ff_total,) = add_second(ff_mine, ff_second, full, BF16, [input_grad], 1)
    vectors = vectors.reshape(n_dp, n_blk, line)

    def of(mask):
        return lax.dynamic_index_in_dim(vectors, d ^ mask, 0, keepdims=False)

    vector_first = over_first(jnp.stack([of(3), of(1)]))
    vector_second = over_second(of(2) + vector_first[0])
    (row_on,) = relay([row_on], [vector_second])
    row_second = over_second(row_on)
    layer_out = project_out(own_tokens, ffn_out, ffn_other, out_weight, grad_rows, [input_grad])
    vectors = of(0) + vector_first[1] + vector_second
    below = jnp.pad(vectors.astype(BF16)[:, None], ((0, 0), (0, EXTRA - 1), (0, ff_cols - line)))
    ff_pieces = swap_blk(
        jnp.concatenate([ff_total.reshape(n_blk, -1, ff_cols), below], axis=1)
    )
    sizes = [ff_block, HD] if aligned else [ff_block]
    shard_down, *shard_out = add_second(row_mine, row_second, sizes, F32)
    if aligned:
        shard_out = shard_out[0]
    else:
        grad_out = dot(att_low.reshape(-1, span), all_grad)
        wide = jnp.zeros((width, width), F32)
        for i in range(per_dev):
            start = (n_blk * i + b) * HD
            wide = lax.dynamic_update_slice(wide, grad_out[i * HD : (i + 1) * HD], (start, 0))
        shard_out = lax.psum_scatter(wide, ("dp", "blk"), scatter_dimension=0, tiled=True)
    cut = width // shards
    (shard_qkv,) = spread([qkv_pieces], cut, 1, 3 * per_dev, HD)
    shard_gate, shard_up, *sums = spread([ff_pieces], cut, 2, n_dp, ff_block, line)
    return (
        layer_out[None],
        input_grad[None],
        sums[0].reshape(-1),
        sums[1].reshape(-1),
        shard_qkv,
        sums[2].reshape(-1),
        shard_out,
        shard_gate,
        shard_up,
        shard_down,
    )


def solution(mesh):
    both = P(("dp", "blk"))
    row_cut = P(("dp", "blk"), None)
    activation = P("dp", "blk", None)
    return jax.shard_map(
        functools.partial(on_device, mesh.shape["dp"], mesh.shape["blk"]),
        mesh=mesh,
        in_specs=(activation,) + (P(),) * 8 + (activation, P("dp")),
        out_specs=(activation, activation, both, both, row_cut, both) + (row_cut,) * 4,
        check_vma=False,
    )
```

```python
import functools

import jax
import jax.numpy as jnp
import numpy as np
from jax import lax
from jax.experimental import pallas as pl
from jax.experimental.pallas import tpu as pltpu
from jax.sharding import PartitionSpec as P

HD = 64
ROT = 16
HALF = ROT // 2

epsilon = 1e-05
masked_score = -1e30
BQ = 256
LANES = 128
EXTRA = 8
SCALE = 1.0
F32 = jnp.float32
BF16 = jnp.bfloat16


def dot(left, right, left_dim=1, right_dim=0):
    return lax.dot_general(
        left, right, (((left_dim,), (right_dim,)), ((), ())), preferred_element_type=F32
    )


RING = [0, 1, 3, 2]
ALONG = [(2 * RING[r] + y, 2 * RING[(r + 1) % 4] + y) for r in range(4) for y in range(2)]


def along(piece):
    return lax.ppermute(piece, "blk", ALONG)


def back(piece):
    return lax.ppermute(piece, "blk", [(target, source) for source, target in ALONG])


def beside(piece, n_blk):
    return lax.ppermute(piece, "blk", [(i, i ^ 1) for i in range(n_blk)])


def piece_slots(b):
    z, y = b // 2, b % 2
    place = z ^ (z >> 1)
    slots = []
    for step in (0, 1, 3, 2):
        slot = (place - step) % 4
        source = slot ^ (slot >> 1)
        slots += [2 * source + y, 2 * source + 1 - y]
    return jnp.stack(slots).astype(jnp.int32)


def swap_blk(pieces):
    return lax.all_to_all(pieces, "blk", split_axis=0, concat_axis=0, tiled=True)


def rotated(block, cosine, sine):
    a, b = block[:HALF], block[HALF:ROT]
    return jnp.concatenate([a * cosine - b * sine, b * cosine + a * sine, block[ROT:]], axis=0)


def masked_scores(keys, queries, start, length):
    scores = dot(keys, queries, 0, 0) * HD**-0.5
    key_pos = lax.broadcasted_iota(jnp.int32, scores.shape, 0)
    query_pos = start + lax.broadcasted_iota(jnp.int32, (1, scores.shape[1]), 1)
    allowed = key_pos <= jnp.minimum(query_pos, length - 1)
    return jnp.where(allowed, scores, masked_score)


ANY = pl.BlockSpec(memory_space=pl.ANY)
VMEM = pl.BlockSpec(memory_space=pltpu.VMEM)
SMEM = pl.BlockSpec(memory_space=pltpu.SMEM)


def kernel_call(kernel, args, after=(), prefetch=0, **options):
    in_specs = list(options.pop("in_specs")) + [ANY] * len(after)
    count = len(args)

    def body(*refs):
        kernel(*refs[:count], *refs[count + len(after) :])

    if prefetch:
        options["grid_spec"] = pltpu.PrefetchScalarGridSpec(
            num_scalar_prefetch=prefetch,
            in_specs=in_specs,
            **{k: options.pop(k) for k in ("grid", "out_specs", "scratch_shapes") if k in options},
        )
    else:
        options["in_specs"] = in_specs
    return pl.pallas_call(body, **options)(*args, *after)


def relay(arrays, after):
    count = len(arrays)
    return pl.pallas_call(
        lambda *refs: None,
        in_specs=[ANY] * (count + len(after)),
        out_specs=[ANY] * count,
        out_shape=[jax.ShapeDtypeStruct(array.shape, array.dtype) for array in arrays],
        input_output_aliases={k: k for k in range(count)},
        compiler_params=pltpu.CompilerParams(has_side_effects=True),
        cost_estimate=takes(1),
        name="relay",
    )(*arrays, *after)


def takes(us):
    return pl.CostEstimate(flops=int(us * SCALE * 1.15e9), bytes_accessed=1 << 16, transcendentals=0)


def params(mib):
    return pltpu.CompilerParams(vmem_limit_bytes=mib << 20)


def ffn_kernel(
    tile,
    b_ref,
    n_ref,
    n_other,
    c_ref,
    c_other,
    gate_ref,
    up_ref,
    down_ref,
    out_ref,
    grad_ref,
    pass_ref,
    normed,
    flipped,
    gate_w,
    up_w,
    down_w,
    act,
    grad_gate,
    grad_up,
    sems,
):
    rows, width = n_ref.shape
    half = gate_w.shape[1]
    count = half // tile
    base = b_ref[0] % 2 * half

    def copies(t):
        here = pl.ds(pl.multiple_of(t * tile, tile), tile)
        there = pl.ds(pl.multiple_of(base + t * tile, LANES), tile)
        return [
            pltpu.make_async_copy(gate_ref.at[:, there], gate_w.at[:, here], sems.at[0, t]),
            pltpu.make_async_copy(up_ref.at[:, there], up_w.at[:, here], sems.at[1, t]),
            pltpu.make_async_copy(down_ref.at[there, :], down_w.at[here, :], sems.at[2, t]),
        ]

    for t in range(count):
        for copy in copies(t):
            copy.start()
    normed[:rows, :] = n_ref[...]
    normed[rows:, :] = n_other[...]
    flipped[:, :rows] = c_ref[...].T
    flipped[:, rows:] = c_other[...].T

    def first(t, carry):
        for copy in copies(t):
            copy.wait()
        here = pl.ds(pl.multiple_of(t * tile, tile), tile)
        gate = dot(normed[...], gate_w[:, here])
        up = dot(normed[...], up_w[:, here])
        grad_act = dot(down_w[here, :], flipped[...])
        sig = jax.nn.sigmoid(gate)
        silu = gate * sig
        act[:, here] = (silu * up).astype(BF16)
        by_gate = (up * sig * (1.0 + gate * (1.0 - sig))).T
        grad_gate[here, :] = (grad_act * by_gate).astype(BF16)
        grad_up[here, :] = (grad_act * silu.T).astype(BF16)
        return carry

    lax.fori_loop(0, count, first, 0)
    step = 512

    def second(r, carry):
        here = pl.ds(pl.multiple_of(r * step, step), step)
        out = dot(act[...], down_w[:, here])
        out_ref[:, here] = out[:rows]
        pass_ref[0, :, here] = out[rows:].astype(BF16)
        grad = (dot(gate_w[here, :], grad_gate[...]) + dot(up_w[here, :], grad_up[...])).T
        grad_ref[:, here] = grad[:rows]
        pass_ref[1, :, here] = grad[rows:].astype(BF16)
        return carry

    lax.fori_loop(0, width // step, second, 0)


def feed_forward(b, normed, out_grad, weights, after):
    rows, width = normed[0].shape
    half = weights[0].shape[1] // 2
    tile = 256
    return kernel_call(
        functools.partial(ffn_kernel, tile),
        (b, *normed, *out_grad, *weights),
        after,
        in_specs=[SMEM] + [VMEM] * 4 + [ANY] * 3,
        out_specs=[VMEM] * 3,
        out_shape=[
            jax.ShapeDtypeStruct((rows, width), F32),
            jax.ShapeDtypeStruct((rows, width), F32),
            jax.ShapeDtypeStruct((2, rows, width), BF16),
        ],
        scratch_shapes=[
            pltpu.VMEM((2 * rows, width), BF16),
            pltpu.VMEM((width, 2 * rows), BF16),
            pltpu.VMEM((width, half), BF16),
            pltpu.VMEM((width, half), BF16),
            pltpu.VMEM((half, width), BF16),
            pltpu.VMEM((2 * rows, half), BF16),
            pltpu.VMEM((half, 2 * rows), BF16),
            pltpu.VMEM((half, 2 * rows), BF16),
            pltpu.SemaphoreType.DMA((3, half // tile)),
        ],
        compiler_params=params(54),
        cost_estimate=takes(24),
        name="feed_forward",
    )


def cut_columns(size, weight, starts, window, held, sems):
    copies = []
    for k, column in enumerate(starts):
        aligned = pl.multiple_of(
            jnp.minimum(column // LANES * LANES, weight.shape[1] - window), LANES
        )
        copy = pltpu.make_async_copy(weight.at[:, pl.ds(aligned, window)], held.at[k], sems.at[k])
        copy.start()
        copies.append((copy, column - aligned))
    return copies


def place_columns(size, copies, held, out_ref, first):
    depth, window = held.shape[-2:]
    step = min(256, depth)
    for k, (copy, offset) in enumerate(copies):
        copy.wait()
        start = (first + k) * size
        place = start % LANES
        for r in range(0, depth, step):
            block = pltpu.roll(held[k, r : r + step, :], window - offset + place, 1)
            out_ref[r : r + step, start : start + size] = block[:, place : place + size]


def slice_kernel(
    size,
    starts,
    qkv_starts,
    b_ref,
    gate_ref,
    up_ref,
    down_ref,
    qkv_ref,
    out_ref,
    turned_ref,
    qkv_out,
    gate_held,
    up_held,
    qkv_held,
    rows,
    gate_sems,
    up_sems,
    qkv_sems,
    row_sems,
):
    depth, window = gate_held.shape[-2:]
    b = b_ref[0]
    gates = cut_columns(size, gate_ref, starts(b), window, gate_held, gate_sems)
    ups = cut_columns(size, up_ref, starts(b), window, up_held, up_sems)
    row_copies = []
    if down_ref.shape[0] > rows.shape[0]:
        for i, row in enumerate(starts(b)):
            row_copies.append(
                pltpu.make_async_copy(
                    down_ref.at[pl.ds(pl.multiple_of(row, size), size), :],
                    rows.at[pl.ds(i * size, size), :],
                    row_sems.at[i],
                )
            )
    else:
        row_copies.append(pltpu.make_async_copy(down_ref, rows, row_sems.at[0]))
    for copy in row_copies:
        copy.start()
    heads = cut_columns(HD, qkv_ref, qkv_starts(b), LANES, qkv_held, qkv_sems)
    place_columns(size, gates, gate_held, out_ref, 0)
    place_columns(size, ups, up_held, out_ref, len(gates))
    for copy in row_copies:
        copy.wait()
    step = min(256, depth)
    for r in range(0, depth, step):
        turned_ref[r : r + step, :] = rows[:, r : r + step].T
    place_columns(HD, heads, qkv_held, qkv_out, 0)


def own_slices(b, gate, up, down, qkv, starts, qkv_starts, count, size, after=()):
    depth = gate.shape[0]
    heads = len(qkv_starts(0))
    window = LANES * ((size + 2 * LANES - 2) // LANES)
    held = pltpu.VMEM((count, depth, window), BF16)
    sems = pltpu.SemaphoreType.DMA((count,))
    return kernel_call(
        functools.partial(slice_kernel, size, starts, qkv_starts),
        (b, gate, up, down, qkv),
        after,
        in_specs=[SMEM] + [ANY] * 4,
        out_specs=[VMEM] * 3,
        out_shape=[
            jax.ShapeDtypeStruct((depth, 2 * count * size), BF16),
            jax.ShapeDtypeStruct((depth, count * size), BF16),
            jax.ShapeDtypeStruct((depth, heads * HD), BF16),
        ],
        scratch_shapes=[
            held,
            held,
            pltpu.VMEM((heads, depth, LANES), BF16),
            pltpu.VMEM((count * size, depth), BF16),
            sems,
            sems,
            pltpu.SemaphoreType.DMA((heads,)),
            sems,
        ],
        compiler_params=params(44),
        cost_estimate=takes(14),
        name="own_slices",
    )


def fetch_rows(slots_ref, pieces, whole_ref, sems):
    rows = pieces[0].shape[0]
    copies = []
    for k, piece in enumerate(pieces):
        place = pl.multiple_of(slots_ref[k] * rows, rows)
        copies.append(
            pltpu.make_async_copy(piece, whole_ref.at[pl.ds(place, rows), :], sems.at[k])
        )
        copies[-1].start()
    return copies


def project(block, weight, bias_ref, cos_ref, sin_ref, qkv_ref, base):
    here = pl.ds(base, block.shape[0])
    cosine, sine = cos_ref[:, here], sin_ref[:, here]
    heads = qkv_ref.shape[1]
    flat = dot(block, weight).T
    for k in range(3 * heads):
        part, i = k // heads, k % heads
        own = flat[k * HD : (k + 1) * HD, :] + bias_ref[part, i]
        if part < 2:
            own = rotated(own, cosine, sine)
        qkv_ref[part, i, :, here] = own.astype(BF16)


def early_kernel(count, slots_ref, weight_ref, bias_ref, cos_ref, sin_ref, *refs):
    pieces, (qkv_ref, held, sems) = refs[:count], refs[count:]
    rows = pieces[0].shape[0]
    copies = []
    for k, piece in enumerate(pieces):
        place = pl.multiple_of((k // 2 * 2 + slots_ref[k] % 2) * rows, rows)
        copies.append(pltpu.make_async_copy(piece, held.at[pl.ds(place, rows), :], sems.at[k]))
        copies[-1].start()
    for copy in copies:
        copy.wait()
    size = 2 * rows
    for k in range(count // 2):
        base = pl.multiple_of(slots_ref[2 * k] // 2 * size, size)
        block = held[k * size : (k + 1) * size, :]
        project(block, weight_ref[...], bias_ref, cos_ref, sin_ref, qkv_ref, base)


def early_projection(slots, weight, bias, cosine, sine, pieces, heads, span, after):
    rows, width = pieces[0].shape
    count = len(pieces)
    return kernel_call(
        functools.partial(early_kernel, count),
        (slots, weight, bias, cosine, sine, *pieces),
        after,
        in_specs=[SMEM, VMEM, VMEM, VMEM, VMEM] + [ANY] * count,
        out_specs=VMEM,
        out_shape=jax.ShapeDtypeStruct((3, heads, HD, span), BF16),
        scratch_shapes=[
            pltpu.VMEM((count * rows, width), BF16),
            pltpu.SemaphoreType.DMA((count,)),
        ],
        compiler_params=params(32),
        cost_estimate=takes(8),
        name="early_projection",
    )


def forward_kernel(
    count, early, length_ref, slots_ref, weight_ref, bias_ref, cos_ref, sin_ref, *refs
):
    pieces = refs[:count]
    refs = refs[count:]
    if early:
        early_ref, refs = refs[0], refs[1:]
    whole_out, qkv_ref, att_ref, low_ref, lse_ref, whole_ref, sems, out_sem = refs
    _, heads, _, span = qkv_ref.shape
    length = length_ref[0]
    copies = fetch_rows(slots_ref, pieces, whole_ref, sems)
    size = 256
    if early:
        bases = [
            pl.multiple_of(slots_ref[2 * k] // 2 * size, size) for k in range(span // size)
        ]
        for base in bases[:early]:
            qkv_ref[:, :, :, pl.ds(base, size)] = early_ref[:, :, :, pl.ds(base, size)]
    else:
        bases = list(range(0, span, size))
    for copy in copies:
        copy.wait()
    leaving = pltpu.make_async_copy(whole_ref, whole_out, out_sem)
    leaving.start()
    for base in bases[early:]:
        block = whole_ref[pl.ds(base, size), :]
        project(block, weight_ref[...], bias_ref, cos_ref, sin_ref, qkv_ref, base)

    def head(i, carry):
        for start in range(0, span, BQ):
            end = start + BQ
            scores = masked_scores(
                qkv_ref[1, i, :, :end], qkv_ref[0, i, :, start:end], start, length
            )
            best = jnp.max(scores, axis=0, keepdims=True)
            weights = jnp.exp(scores - best)
            total = jnp.sum(weights, axis=0, keepdims=True)
            out = dot(qkv_ref[2, i, :, :end], weights.astype(BF16)) / total
            att_ref[i, :, start:end] = out
            low_ref[i, :, start:end] = out.astype(BF16)
            lse_ref[i, :, start:end] = best + jnp.log(total)
        return carry

    lax.fori_loop(0, heads, head, 0)
    leaving.wait()


def attention_forward(
    length, slots, weight, bias, cosine, sine, pieces, early, pairs, heads, after
):
    width = weight.shape[0]
    span = len(pieces) * pieces[0].shape[0]
    count = len(pieces)
    return kernel_call(
        functools.partial(forward_kernel, count, pairs),
        (length, slots, weight, bias, cosine, sine, *pieces, *early),
        after,
        in_specs=[SMEM, SMEM, VMEM, VMEM, VMEM, VMEM] + [ANY] * count + [VMEM] * len(early),
        out_specs=[ANY] + [VMEM] * 4,
        out_shape=[
            jax.ShapeDtypeStruct((span, width), BF16),
            jax.ShapeDtypeStruct((3, heads, HD, span), BF16),
            jax.ShapeDtypeStruct((heads, HD, span), F32),
            jax.ShapeDtypeStruct((heads, HD, span), BF16),
            jax.ShapeDtypeStruct((heads, 1, span), F32),
        ],
        scratch_shapes=[
            pltpu.VMEM((span, width), BF16),
            pltpu.SemaphoreType.DMA((count,)),
            pltpu.SemaphoreType.DMA,
        ],
        compiler_params=params(48),
        cost_estimate=takes(20),
        name="attention_forward",
    )


def backward_kernel(
    count, b_ref, length_ref, slots_ref, weight_ref, qkv_ref, att_ref, lse_ref, cos_ref, sin_ref, *refs
):
    pieces = refs[:count]
    (
        whole_out,
        out_ref,
        flat_ref,
        whole_ref,
        weight,
        grad_ref,
        dq,
        dk,
        dv,
        turned,
        weight_sem,
        sems,
        out_sem,
    ) = refs[count:]
    _, heads, _, span = qkv_ref.shape
    length = length_ref[0]
    scale = HD**-0.5
    cosine, sine = cos_ref[...], -sin_ref[...]
    n_blk = out_ref.shape[0]
    copies = fetch_rows(slots_ref, pieces, whole_ref, sems)
    for i in range(heads):
        row = pl.multiple_of((n_blk * i + b_ref[0]) * HD, HD)
        copies.append(
            pltpu.make_async_copy(
                weight_ref.at[pl.ds(row, HD), :],
                weight.at[pl.ds(i * HD, HD), :],
                weight_sem.at[i],
            )
        )
        copies[-1].start()
    for copy in copies:
        copy.wait()
    leaving = pltpu.make_async_copy(whole_ref, whole_out, out_sem)
    leaving.start()
    across = weight[...].T
    for start in range(0, span, BQ):
        grads = dot(whole_ref[start : start + BQ, :], across).T.astype(BF16)
        for i in range(heads):
            grad_ref[i, :, start : start + BQ] = grads[i * HD : (i + 1) * HD, :]

    def head(i, carry):
        dk[...] = jnp.zeros_like(dk)
        dv[...] = jnp.zeros_like(dv)
        for start in range(0, span, BQ):
            end = start + BQ
            keys, values = qkv_ref[1, i, :, :end], qkv_ref[2, i, :, :end]
            queries, grads = qkv_ref[0, i, :, start:end], grad_ref[i, :, start:end]
            delta = jnp.sum(grads.astype(F32) * att_ref[i, :, start:end], axis=0, keepdims=True)
            scores = masked_scores(keys, queries, start, length)
            prob = jnp.exp(scores - lse_ref[i, :, start:end])
            grad_prob = dot(values, grads, 0, 0)
            grad_score = (prob * (grad_prob - delta)).astype(BF16)
            dq[:, start:end] = dot(keys, grad_score) * scale
            dk[:, :end] += dot(queries, grad_score, 1, 1)
            dv[:, :end] += dot(grads, prob.astype(BF16), 1, 1)
        turned[0, i] = rotated(dq[...], cosine, sine).astype(BF16)
        turned[1, i] = rotated(dk[...] * scale, cosine, sine).astype(BF16)
        turned[2, i] = dv[...].astype(BF16)
        return carry

    lax.fori_loop(0, heads, head, 0)
    rows = out_ref.shape[2]
    for part in range(3):
        for i in range(heads):
            k = part * heads + i
            flat_ref[:, k * HD : (k + 1) * HD] = turned[part, i].T
            for j in range(n_blk):
                out_ref[j, k * HD : (k + 1) * HD, :] = turned[part, i, :, j * rows : (j + 1) * rows]
    for i in range(heads):
        k = 3 * heads + i
        for j in range(n_blk):
            out_ref[j, k * HD : (k + 1) * HD, :] = att_ref[
                i, :, j * rows : (j + 1) * rows
            ].astype(BF16)
    leaving.wait()


def attention_backward(
    b, length, slots, weight, qkv, att, lse, cosine, sine, pieces, n_blk, after=()
):
    _, heads, _, span = qkv.shape
    width = weight.shape[1]
    count = len(pieces)
    return kernel_call(
        functools.partial(backward_kernel, count),
        (b, length, slots, weight, qkv, att, lse, cosine, sine, *pieces),
        after,
        in_specs=[SMEM, SMEM, SMEM, ANY] + [VMEM] * 5 + [ANY] * count,
        out_specs=[ANY] + [VMEM] * 2,
        out_shape=[
            jax.ShapeDtypeStruct((span, width), BF16),
            jax.ShapeDtypeStruct((n_blk, 4 * heads * HD, span // n_blk), BF16),
            jax.ShapeDtypeStruct((span, 3 * heads * HD), BF16),
        ],
        scratch_shapes=[
            pltpu.VMEM((span, width), BF16),
            pltpu.VMEM((heads * HD, width), BF16),
            pltpu.VMEM((heads, HD, span), BF16),
        ]
        + [pltpu.VMEM((HD, span), F32)] * 3
        + [
            pltpu.VMEM((3, heads, HD, span), BF16),
            pltpu.SemaphoreType.DMA((heads,)),
            pltpu.SemaphoreType.DMA((count,)),
            pltpu.SemaphoreType.DMA,
        ],
        compiler_params=params(40),
        cost_estimate=takes(18),
        name="attention_backward",
    )


def grads_kernel(n_dp, n_ref, c_ref, gate_up_ref, down_ref, act_ref, grad_ref):
    cols = down_ref.shape[1]
    both = dot(n_ref[...], gate_up_ref[...])
    gate, up = both[:, :cols], both[:, cols:]
    sig = jax.nn.sigmoid(gate)
    silu = gate * sig
    act = silu * up
    part = cols // n_dp
    for i in range(n_dp):
        act_ref[i] = act[:, i * part : (i + 1) * part].T.astype(BF16)
    grad_act = dot(c_ref[...], down_ref[...])
    grad_ref[:, :cols] = (grad_act * up * sig * (1.0 + gate * (1.0 - sig))).astype(BF16)
    grad_ref[:, cols:] = (grad_act * silu).astype(BF16)


def local_grads(all_normed, all_grad, gate_up, down, n_dp, after=()):
    span, width = all_normed.shape
    cols = down.shape[1]
    size = 256
    return kernel_call(
        functools.partial(grads_kernel, n_dp),
        (all_normed, all_grad, gate_up, down),
        after,
        grid=(span // size,),
        in_specs=[
            pl.BlockSpec((size, width), lambda r: (r, 0)),
            pl.BlockSpec((size, width), lambda r: (r, 0)),
            pl.BlockSpec((width, 2 * cols), lambda r: (0, 0)),
            pl.BlockSpec((width, cols), lambda r: (0, 0)),
        ],
        out_specs=[
            pl.BlockSpec((n_dp, cols // n_dp, size), lambda r: (0, 0, r)),
            pl.BlockSpec((size, 2 * cols), lambda r: (r, 0)),
        ],
        out_shape=[
            jax.ShapeDtypeStruct((n_dp, cols // n_dp, span), BF16),
            jax.ShapeDtypeStruct((span, 2 * cols), BF16),
        ],
        compiler_params=params(48),
        cost_estimate=takes(15),
        name="local_grads",
    )


def keep(value, first, on_ref, mine_ref, cut):
    value += first.astype(F32)

    @pl.when(pl.program_id(0) < cut)
    def _():
        on_ref[...] = value.astype(BF16)

    @pl.when(pl.program_id(0) >= cut)
    def _():
        mine_ref[...] = value


def column_products_kernel(low, high, order_ref, left_ref, right_ref, *refs):
    value = dot(left_ref[...], right_ref[:, low:high], 0, 0)
    if len(refs) == 1:
        refs[0][0] = value.astype(BF16)
    else:
        keep(value, refs[0][0, :, low:high], *refs[1:], 2)


def column_products(order, left, right, low, high, n_dp, first=None, after=()):
    span, width = left.shape
    cols = high - low
    size = width // n_dp
    part = size // 2
    stay = [
        pl.BlockSpec((part, cols), lambda j, order: (jnp.minimum(j, 1), 0)),
        pl.BlockSpec((part, cols), lambda j, order: (jnp.maximum(j - 2, 0), 0)),
    ]
    block = pl.BlockSpec(
        (1, part, cols if first is None else right.shape[1]), lambda j, order: (j // 2, j % 2, 0)
    )
    return kernel_call(
        functools.partial(column_products_kernel, low, high),
        (order, left, right) + (() if first is None else (first,)),
        after,
        prefetch=1,
        grid=(4,),
        in_specs=[
            pl.BlockSpec((span, part), lambda j, order: (0, order[j // 2] * 2 + j % 2)),
            pl.BlockSpec(right.shape, lambda j, order: (0, 0)),
        ]
        + ([] if first is None else [block]),
        out_specs=block if first is None else stay,
        out_shape=jax.ShapeDtypeStruct((2, size, cols), BF16)
        if first is None
        else [jax.ShapeDtypeStruct((size, cols), dtype) for dtype in (BF16, F32)],
        compiler_params=params(24),
        cost_estimate=takes(8),
        name="column_products",
    )


def row_products_kernel(count, order_ref, *refs):
    lefts, right_ref, rest = refs[:count], refs[count], refs[count + 1 :]
    value = [dot(left[0], right_ref[...]) for left in lefts]
    value = jnp.concatenate(value, axis=0) if count > 1 else value[0]
    if len(rest) == 1:
        rest[0][0] = value.astype(BF16)
    else:
        keep(value, rest[0][0], *rest[1:], 1)


def row_products(order, lefts, right, first=None, after=()):
    span, width = right.shape
    size = sum(left.shape[1] for left in lefts)
    block = pl.BlockSpec((1, size, width), lambda j, order: (j, 0, 0))
    stay = pl.BlockSpec((size, width), lambda j, order: (0, 0))
    return kernel_call(
        functools.partial(row_products_kernel, len(lefts)),
        (order, *lefts, right) + (() if first is None else (first,)),
        after,
        prefetch=1,
        grid=(2,),
        in_specs=[
            pl.BlockSpec((1,) + left.shape[1:], lambda j, order: (order[j], 0, 0))
            for left in lefts
        ]
        + [pl.BlockSpec((span, width), lambda j, order: (0, 0))]
        + ([] if first is None else [block]),
        out_specs=block if first is None else [stay, stay],
        out_shape=jax.ShapeDtypeStruct((2, size, width), BF16)
        if first is None
        else [jax.ShapeDtypeStruct((size, width), dtype) for dtype in (BF16, F32)],
        compiler_params=params(24),
        cost_estimate=takes(8),
        name="row_products",
    )


def add_kernel(mine_ref, second_ref, *out_refs):
    total = mine_ref[...] + second_ref[...].astype(F32)
    start = 0
    for out_ref in out_refs:
        size = out_ref.shape[0]
        out_ref[...] = total[start : start + size].astype(out_ref.dtype)
        start += size


def add_second(mine, second, sizes, dtype, after=(), us=16):
    _, cols = mine.shape
    return kernel_call(
        add_kernel,
        (mine, second),
        after,
        in_specs=[VMEM] * 2,
        out_specs=[VMEM] * len(sizes),
        out_shape=[jax.ShapeDtypeStruct((part, cols), dtype) for part in sizes],
        compiler_params=params(16),
        cost_estimate=takes(us),
        name="add_second",
    )


def spread_kernel(count, outer, size, line, *refs):
    arrays, out_refs = refs[:count], refs[count:]
    n_blk = arrays[0].shape[0]
    if line:
        out_refs, line_refs = out_refs[:-3], out_refs[-3:]
        rows = out_refs[0].shape[0]
        sums = sum(arrays[-1][b, rows : rows + EXTRA, :line].astype(F32) for b in range(n_blk))
        start = 0
        for line_ref in line_refs:
            end = start + line_ref.shape[1]
            line_ref[...] = sums[:1, start:end]
            start = end
    for k, out_ref in enumerate(out_refs):
        rows = out_ref.shape[0]
        for i in range(outer):
            for b in range(n_blk):
                source = (k * outer + i) * size
                place = (i * n_blk + b) * size
                start = 0
                for array in arrays:
                    end = start + array.shape[2]
                    low, high = max(source, start), min(source + size, end)
                    if low < high:
                        out_ref[:, place + low - source : place + high - source] = array[
                            b, :rows, low - start : high - start
                        ].astype(F32)
                    start = end


def spread(arrays, rows, outputs, outer, size, line=0, after=()):
    n_blk = arrays[0].shape[0]
    return kernel_call(
        functools.partial(spread_kernel, len(arrays), outer, size, line),
        tuple(arrays),
        after,
        in_specs=[VMEM] * len(arrays),
        out_specs=[VMEM] * (outputs + 3 * (line > 0)),
        out_shape=[jax.ShapeDtypeStruct((rows, outer * n_blk * size), F32)] * outputs
        + [jax.ShapeDtypeStruct((1, n * line // 5), F32) for n in (1, 1, 3) if line],
        compiler_params=params(16),
        cost_estimate=takes(3),
        name="spread",
    )


def out_kernel(x_ref, ffn_ref, other_ref, weight_ref, pieces, out_ref, left, total):
    n_blk, lines, _ = pieces.shape
    heads = lines // HD // 4
    step = pl.program_id(0)
    size = left.shape[2]

    @pl.when(step == 0)
    def _():
        for i in range(heads):
            for b in range(n_blk):
                place = (i * n_blk + b) * HD
                block, start = place // size, place % size
                k = 3 * heads + i
                left[block, :, start : start + HD] = pieces[b, k * HD : (k + 1) * HD, :].T
        total[...] = x_ref[...].astype(F32) + ffn_ref[...] + other_ref[0].astype(F32)

    total[...] += dot(left[step], weight_ref[...])

    @pl.when(step == pl.num_programs(0) - 1)
    def _():
        out_ref[...] = total[...].astype(BF16)


def project_out(tokens, ffn_out, other, weight, pieces, after=()):
    rows, width = tokens.shape
    steps = 4
    size = width // steps
    whole = pl.BlockSpec((rows, width), lambda t: (0, 0))
    return kernel_call(
        out_kernel,
        (tokens, ffn_out, other, weight, pieces),
        after,
        grid=(steps,),
        in_specs=[
            whole,
            whole,
            pl.BlockSpec((1, rows, width), lambda t: (0, 0, 0)),
            pl.BlockSpec((size, width), lambda t: (t, 0)),
            pl.BlockSpec(pieces.shape, lambda t: (0, 0, 0)),
        ],
        out_specs=whole,
        out_shape=jax.ShapeDtypeStruct((rows, width), BF16),
        scratch_shapes=[pltpu.VMEM((steps, rows, size), BF16), pltpu.VMEM((rows, width), F32)],
        compiler_params=params(20),
        cost_estimate=takes(6),
        name="project_out",
    )


def input_kernel(
    x_ref, c_ref, gain_ref, ffn_ref, other_ref, weight_ref, pieces, out_ref, sums_ref, left, total
):
    n_blk, lines, _ = pieces.shape
    step, steps = pl.program_id(0), pl.num_programs(0)
    size = left.shape[1]

    @pl.when(step == 0)
    def _():
        for i in range(3 * (lines // HD // 4)):
            for b in range(n_blk):
                place = (i * n_blk + b) * HD
                block, start = place // size, place % size
                left[block, start : start + HD, :] = pieces[b, i * HD : (i + 1) * HD, :]
        total[...] = jnp.zeros_like(total)

    total[...] += dot(weight_ref[...], left[step])

    @pl.when(step == steps - 1)
    def _():
        x = x_ref[...].astype(F32)
        center = x - jnp.mean(x, axis=1, keepdims=True)
        inverse_std = lax.rsqrt(jnp.mean(center * center, axis=1, keepdims=True) + epsilon)
        normalized = center * inverse_std
        grad = ffn_ref[...] + other_ref[0].astype(F32) + total[...].T
        vectors = [
            jnp.sum(grad * normalized, axis=0, keepdims=True),
            jnp.sum(grad, axis=0, keepdims=True),
        ] + [jnp.sum(left[t].astype(F32).T, axis=0, keepdims=True) for t in range(left.shape[0])]
        flat = jnp.concatenate(vectors, axis=1)
        shards = sums_ref.shape[0]
        width = grad.shape[1]
        cut = width // shards
        for j in range(shards):
            sums_ref[j : j + 1, :cut] = flat[:, j * cut : (j + 1) * cut]
            sums_ref[j : j + 1, cut : 2 * cut] = flat[:, width + j * cut : width + (j + 1) * cut]
            start = 2 * width + 3 * j * cut
            sums_ref[j : j + 1, 2 * cut :] = flat[:, start : start + 3 * cut]
        grad = grad * gain_ref[...]
        grad_inputs = inverse_std * (
            grad
            - jnp.mean(grad, axis=1, keepdims=True)
            - normalized * jnp.mean(grad * normalized, axis=1, keepdims=True)
        )
        out_ref[...] = (c_ref[...].astype(F32) + grad_inputs).astype(BF16)


def input_grads(
    tokens, out_grad, gain, ffn_grad, other, weight, pieces, shards, after=()
):
    rows, width = tokens.shape
    cols = weight.shape[1]
    steps = 8
    size = cols // steps
    whole = pl.BlockSpec((rows, width), lambda t: (0, 0))
    return kernel_call(
        input_kernel,
        (tokens, out_grad, gain, ffn_grad, other, weight, pieces),
        after,
        grid=(steps,),
        in_specs=[
            whole,
            whole,
            pl.BlockSpec((1, width), lambda t: (0, 0)),
            whole,
            pl.BlockSpec((1, rows, width), lambda t: (1, 0, 0)),
            pl.BlockSpec((width, size), lambda t: (0, t)),
            pl.BlockSpec(pieces.shape, lambda t: (0, 0, 0)),
        ],
        out_specs=[whole, pl.BlockSpec((shards, 5 * width // shards), lambda t: (0, 0))],
        out_shape=[
            jax.ShapeDtypeStruct((rows, width), BF16),
            jax.ShapeDtypeStruct((shards, 5 * width // shards), F32),
        ],
        scratch_shapes=[pltpu.VMEM((steps, size, rows), BF16), pltpu.VMEM((width, rows), F32)],
        compiler_params=params(28),
        cost_estimate=takes(13),
        name="input_grads",
    )


def on_device(
    n_dp,
    n_blk,
    tokens,
    norm_gain,
    norm_bias,
    qkv_weight,
    qkv_bias,
    out_weight,
    gate_weight,
    up_weight,
    down_weight,
    cotangent,
    lengths,
):
    rows, width = tokens.shape[1:]
    span = rows * n_blk
    hidden = gate_weight.shape[1]
    per_dev = width // HD // n_blk
    ff_block = hidden // (n_dp * n_blk)
    d, b = lax.axis_index("dp").astype(jnp.int32), lax.axis_index("blk").astype(jnp.int32)
    own_tokens, out_grad = tokens[0], cotangent[0]

    inputs = own_tokens.astype(F32)
    center = inputs - jnp.mean(inputs, axis=1, keepdims=True)
    inverse_std = lax.rsqrt(jnp.mean(center * center, axis=1, keepdims=True) + epsilon)
    normed = (center * inverse_std * norm_gain + norm_bias).astype(BF16)

    position = b.reshape(1)

    def ff_starts(b):
        return [(n_blk * i + b) * ff_block for i in range(n_dp)]

    def qkv_starts(b):
        return [part * width + (n_blk * i + b) * HD for part in range(3) for i in range(per_dev)]

    def own_blocks(array, outer, size):
        cut = array.reshape((outer, n_blk, size) + array.shape[1:])
        return lax.dynamic_index_in_dim(cut, b, 1, keepdims=False).reshape(
            (-1,) + array.shape[1:]
        )

    down_rows = down_weight if ff_block % 16 == 0 else own_blocks(down_weight, n_dp, ff_block)

    def slices():
        return own_slices(
            position,
            gate_weight,
            up_weight,
            down_rows,
            qkv_weight,
            ff_starts,
            qkv_starts,
            n_dp,
            ff_block,
        )

    def ffn(normed_other, grad_other, after):
        return feed_forward(
            position,
            (normed, normed_other),
            (out_grad, grad_other),
            (gate_weight, up_weight, down_weight),
            after,
        )

    own_bias = own_blocks(qkv_bias, 3 * per_dev, HD).reshape(3, per_dev, HD, 1)
    frequency = 10000.0 ** (-2.0 * np.arange(HALF) / ROT)
    angles = frequency[:, None] * np.arange(span)[None, :]
    cosine, sine = np.cos(angles).astype(np.float32), np.sin(angles).astype(np.float32)


    if n_blk == 8:
        slots = piece_slots(b)
        n1, m0, c1, e0 = along(normed), beside(normed, 8), along(out_grad), beside(out_grad, 8)
        n3 = back(normed)
        own_gate_up, own_down, own_qkv = slices()
        c1, e0 = relay([c1, e0], [own_down])
        (n1,) = relay([n1], [c1])
        m1, e1, n2, c2 = beside(n1, 8), beside(c1, 8), along(n1), along(c1)
        (n3,) = relay([n3], [n1])
        m3 = beside(n3, 8)
        ffn_out, ffn_grad, passed = ffn(m0, e0, [n3])
        n2, c3, e3 = relay([n2, out_grad, e0], [ffn_out, m1, e1])
        m2, c3, e3 = beside(n2, 8), back(c3), back(e3)
        (c2,) = relay([c2], [n2])
        e2 = beside(c2, 8)
        normed_pieces = [normed, m0, n1, m1, n3, m3, n2, m2]
        grad_pieces = [out_grad, e0, c1, e1, c3, e3, c2, e2]
        early = [
            early_projection(
                slots, own_qkv, own_bias, cosine, sine, normed_pieces[:6], per_dev, span, [n2]
            )
        ]
        arrived = [c2]
    else:
        slots = jnp.zeros((1,), jnp.int32)
        normed_pieces = [lax.all_gather(normed, "blk", axis=0, tiled=True)]
        grad_pieces = [lax.all_gather(out_grad, "blk", axis=0, tiled=True)]
        own_gate_up, own_down, own_qkv = slices()
        ffn_out, ffn_grad, passed = ffn(
            beside(normed, n_blk), beside(out_grad, n_blk), [own_down]
        )
        early, arrived = [], []

    all_normed, qkv, att, att_low, lse = attention_forward(
        lengths,
        slots,
        own_qkv,
        own_bias,
        cosine,
        sine,
        normed_pieces,
        early,
        3 * len(early),
        per_dev,
        [ffn_out, *arrived],
    )
    all_grad, grad_cut, grad_qkv = attention_backward(
        position,
        lengths,
        slots,
        out_weight,
        qkv,
        att,
        lse,
        cosine,
        sine,
        grad_pieces,
        n_blk,
    )
    grad_rows = swap_blk(grad_cut)

    sent = jnp.stack([d ^ 3, d ^ 1])
    kept = jnp.stack([d ^ 2, d])

    def over_first(array):
        return lax.ppermute(array, "dp", [(i, i ^ 1) for i in range(4)])

    def over_second(array):
        return lax.ppermute(array, "dp", [(i, i ^ 2) for i in range(4)])

    def row_cut(total):
        return swap_blk(total.reshape(n_blk, -1, total.shape[1]))

    ff_cols, qkv_cols = 2 * n_dp * ff_block, 3 * per_dev * HD
    aligned = per_dev == n_dp
    shards = n_dp * n_blk
    line = 5 * width // shards
    full = [width // n_dp]

    qkv_sent = column_products(sent, all_normed, grad_qkv, 0, qkv_cols, n_dp)
    qkv_first = over_first(qkv_sent)
    act, grad_ff = local_grads(
        all_normed, all_grad, own_gate_up, own_down, n_dp, [qkv_sent]
    )
    lefts = [act, att_low] if aligned else [act]
    qkv_on, qkv_mine = column_products(
        kept, all_normed, grad_qkv, 0, qkv_cols, n_dp, qkv_first, [act]
    )
    qkv_second = over_second(qkv_on)
    ff_sent = column_products(sent, all_normed, grad_ff, 0, ff_cols, n_dp, None, [qkv_on])
    ff_first = over_first(ff_sent)
    row_sent = row_products(sent, lefts, all_grad, None, [ff_sent])
    row_first = over_first(row_sent)
    (qkv_total,) = add_second(qkv_mine, qkv_second, full, BF16, [row_sent], 24)
    qkv_pieces = row_cut(qkv_total)
    ff_on, ff_mine = column_products(
        kept, all_normed, grad_ff, 0, ff_cols, n_dp, ff_first, [qkv_total]
    )
    ff_second = over_second(ff_on)
    row_on, row_mine = row_products(kept, lefts, all_grad, row_first, [ff_on])
    (passed,) = relay([passed], [grad_cut])
    ffn_other = beside(passed, n_blk)
    input_grad, vectors = input_grads(
        own_tokens,
        out_grad,
        norm_gain[None],
        ffn_grad,
        ffn_other,
        qkv_weight,
        grad_rows,
        shards,
        [row_on],
    )
    (ff_total,) = add_second(ff_mine, ff_second, full, BF16, [input_grad], 1)
    vectors = vectors.reshape(n_dp, n_blk, line)

    def of(mask):
        return lax.dynamic_index_in_dim(vectors, d ^ mask, 0, keepdims=False)

    vector_first = over_first(jnp.stack([of(3), of(1)]))
    vector_second = over_second(of(2) + vector_first[0])
    (row_on,) = relay([row_on], [vector_second])
    row_second = over_second(row_on)
    layer_out = project_out(own_tokens, ffn_out, ffn_other, out_weight, grad_rows, [input_grad])
    vectors = of(0) + vector_first[1] + vector_second
    below = jnp.pad(vectors.astype(BF16)[:, None], ((0, 0), (0, EXTRA - 1), (0, ff_cols - line)))
    ff_pieces = swap_blk(
        jnp.concatenate([ff_total.reshape(n_blk, -1, ff_cols), below], axis=1)
    )
    sizes = [ff_block, HD] if aligned else [ff_block]
    shard_down, *shard_out = add_second(row_mine, row_second, sizes, F32)
    if aligned:
        shard_out = shard_out[0]
    else:
        grad_out = dot(att_low.reshape(-1, span), all_grad)
        wide = jnp.zeros((width, width), F32)
        for i in range(per_dev):
            start = (n_blk * i + b) * HD
            wide = lax.dynamic_update_slice(wide, grad_out[i * HD : (i + 1) * HD], (start, 0))
        shard_out = lax.psum_scatter(wide, ("dp", "blk"), scatter_dimension=0, tiled=True)
    cut = width // shards
    (shard_qkv,) = spread([qkv_pieces], cut, 1, 3 * per_dev, HD)
    shard_gate, shard_up, *sums = spread([ff_pieces], cut, 2, n_dp, ff_block, line)
    return (
        layer_out[None],
        input_grad[None],
        sums[0].reshape(-1),
        sums[1].reshape(-1),
        shard_qkv,
        sums[2].reshape(-1),
        shard_out,
        shard_gate,
        shard_up,
        shard_down,
    )


def solution(mesh):
    both = P(("dp", "blk"))
    row_cut = P(("dp", "blk"), None)
    activation = P("dp", "blk", None)
    return jax.shard_map(
        functools.partial(on_device, mesh.shape["dp"], mesh.shape["blk"]),
        mesh=mesh,
        in_specs=(activation,) + (P(),) * 8 + (activation, P("dp")),
        out_specs=(activation, activation, both, both, row_cut, both) + (row_cut,) * 4,
        check_vma=False,
    )
```

```python
import functools

import jax
import jax.numpy as jnp
import numpy as np
from jax import lax
from jax.experimental import pallas as pl
from jax.experimental.pallas import tpu as pltpu
from jax.sharding import PartitionSpec as P

HD = 64
ROT = 16
HALF = ROT // 2

epsilon = 1e-05
masked_score = -1e30
BQ = 256
LANES = 128
EXTRA = 8
SCALE = 1.0
F32 = jnp.float32
BF16 = jnp.bfloat16


def dot(left, right, left_dim=1, right_dim=0):
    return lax.dot_general(
        left, right, (((left_dim,), (right_dim,)), ((), ())), preferred_element_type=F32
    )


RING = [0, 1, 3, 2]
ALONG = [(2 * RING[r] + y, 2 * RING[(r + 1) % 4] + y) for r in range(4) for y in range(2)]


def along(piece):
    return lax.ppermute(piece, "blk", ALONG)


def back(piece):
    return lax.ppermute(piece, "blk", [(target, source) for source, target in ALONG])


def beside(piece, n_blk):
    return lax.ppermute(piece, "blk", [(i, i ^ 1) for i in range(n_blk)])


def piece_slots(b):
    z, y = b // 2, b % 2
    place = z ^ (z >> 1)
    slots = []
    for step in (0, 1, 3, 2):
        slot = (place - step) % 4
        source = slot ^ (slot >> 1)
        slots += [2 * source + y, 2 * source + 1 - y]
    return jnp.stack(slots).astype(jnp.int32)


def swap_blk(pieces):
    return lax.all_to_all(pieces, "blk", split_axis=0, concat_axis=0, tiled=True)


def rotated(block, cosine, sine):
    a, b = block[:HALF], block[HALF:ROT]
    return jnp.concatenate([a * cosine - b * sine, b * cosine + a * sine, block[ROT:]], axis=0)


def mark_keys(marked, triangle, length):
    shape = (marked.shape[1] - HD, marked.shape[2])
    line = lax.broadcasted_iota(jnp.int32, shape, 0)
    key = lax.broadcasted_iota(jnp.int32, shape, 1)
    beyond = jnp.where((line == 0) & (key >= length), masked_score, 0.0)
    marked[0, HD:, :] = beyond.astype(BF16)
    marked[1, HD:, :] = jnp.where(line == 0, 1.0, 0.0).astype(BF16)
    key = lax.broadcasted_iota(jnp.int32, triangle.shape, 0)
    query = lax.broadcasted_iota(jnp.int32, triangle.shape, 1)
    triangle[...] = jnp.where(key <= query, 0.0, masked_score)


def score_parts(marked, triangle, start):
    queries = marked[1, :, start : start + BQ]
    parts = [
        (start, start + BQ, dot(marked[0, :, start : start + BQ], queries, 0, 0) + triangle[...])
    ]
    if start:
        parts.append((0, start, dot(marked[0, :, :start], queries, 0, 0)))
    return parts


def scores_until(marked, triangle, start):
    end = start + BQ
    scores = dot(marked[0, :, :end], marked[1, :, start:end], 0, 0)
    if not start:
        return scores + triangle[...]
    return jnp.concatenate([scores[:start], scores[start:] + triangle[...]], axis=0)


MARKED = 16


def mark_shapes(span):
    return [pltpu.VMEM((2, HD + MARKED, span), BF16), pltpu.VMEM((BQ, BQ), F32)]


ANY = pl.BlockSpec(memory_space=pl.ANY)
VMEM = pl.BlockSpec(memory_space=pltpu.VMEM)
SMEM = pl.BlockSpec(memory_space=pltpu.SMEM)


def kernel_call(kernel, args, after=(), prefetch=0, **options):
    in_specs = list(options.pop("in_specs")) + [ANY] * len(after)
    count = len(args)

    def body(*refs):
        kernel(*refs[:count], *refs[count + len(after) :])

    if prefetch:
        options["grid_spec"] = pltpu.PrefetchScalarGridSpec(
            num_scalar_prefetch=prefetch,
            in_specs=in_specs,
            **{k: options.pop(k) for k in ("grid", "out_specs", "scratch_shapes") if k in options},
        )
    else:
        options["in_specs"] = in_specs
    return pl.pallas_call(body, **options)(*args, *after)


def relay(arrays, after):
    count = len(arrays)
    return pl.pallas_call(
        lambda *refs: None,
        in_specs=[ANY] * (count + len(after)),
        out_specs=[ANY] * count,
        out_shape=[jax.ShapeDtypeStruct(array.shape, array.dtype) for array in arrays],
        input_output_aliases={k: k for k in range(count)},
        compiler_params=pltpu.CompilerParams(has_side_effects=True),
        cost_estimate=takes(1),
        name="relay",
    )(*arrays, *after)


def takes(us):
    return pl.CostEstimate(flops=int(us * SCALE * 1.15e9), bytes_accessed=1 << 16, transcendentals=0)


def params(mib):
    return pltpu.CompilerParams(vmem_limit_bytes=mib << 20)


def ffn_kernel(
    tile,
    b_ref,
    n_ref,
    n_other,
    c_ref,
    c_other,
    gate_ref,
    up_ref,
    down_ref,
    out_ref,
    grad_ref,
    pass_ref,
    normed,
    flipped,
    gate_w,
    up_w,
    down_w,
    act,
    grad_gate,
    grad_up,
    sems,
):
    rows, width = n_ref.shape
    half = gate_w.shape[1]
    count = half // tile
    base = b_ref[0] % 2 * half

    def copies(t):
        here = pl.ds(pl.multiple_of(t * tile, tile), tile)
        there = pl.ds(pl.multiple_of(base + t * tile, LANES), tile)
        return [
            pltpu.make_async_copy(gate_ref.at[:, there], gate_w.at[:, here], sems.at[0, t]),
            pltpu.make_async_copy(up_ref.at[:, there], up_w.at[:, here], sems.at[1, t]),
            pltpu.make_async_copy(down_ref.at[there, :], down_w.at[here, :], sems.at[2, t]),
        ]

    for t in range(count):
        for copy in copies(t):
            copy.start()
    normed[:rows, :] = n_ref[...]
    normed[rows:, :] = n_other[...]
    flipped[:, :rows] = c_ref[...].T
    flipped[:, rows:] = c_other[...].T

    def first(t, carry):
        for copy in copies(t):
            copy.wait()
        here = pl.ds(pl.multiple_of(t * tile, tile), tile)
        gate = dot(normed[...], gate_w[:, here])
        up = dot(normed[...], up_w[:, here])
        grad_act = dot(down_w[here, :], flipped[...])
        sig = jax.nn.sigmoid(gate)
        silu = gate * sig
        act[:, here] = (silu * up).astype(BF16)
        by_gate = (up * sig * (1.0 + gate * (1.0 - sig))).T
        grad_gate[here, :] = (grad_act * by_gate).astype(BF16)
        grad_up[here, :] = (grad_act * silu.T).astype(BF16)
        return carry

    lax.fori_loop(0, count, first, 0)
    step = 512

    def second(r, carry):
        here = pl.ds(pl.multiple_of(r * step, step), step)
        out = dot(act[...], down_w[:, here])
        out_ref[:, here] = out[:rows]
        pass_ref[0, :, here] = out[rows:].astype(BF16)
        grad = (dot(gate_w[here, :], grad_gate[...]) + dot(up_w[here, :], grad_up[...])).T
        grad_ref[:, here] = grad[:rows]
        pass_ref[1, :, here] = grad[rows:].astype(BF16)
        return carry

    lax.fori_loop(0, width // step, second, 0)


def feed_forward(b, normed, out_grad, weights, after):
    rows, width = normed[0].shape
    half = weights[0].shape[1] // 2
    tile = 256
    return kernel_call(
        functools.partial(ffn_kernel, tile),
        (b, *normed, *out_grad, *weights),
        after,
        in_specs=[SMEM] + [VMEM] * 4 + [ANY] * 3,
        out_specs=[VMEM] * 3,
        out_shape=[
            jax.ShapeDtypeStruct((rows, width), F32),
            jax.ShapeDtypeStruct((rows, width), F32),
            jax.ShapeDtypeStruct((2, rows, width), BF16),
        ],
        scratch_shapes=[
            pltpu.VMEM((2 * rows, width), BF16),
            pltpu.VMEM((width, 2 * rows), BF16),
            pltpu.VMEM((width, half), BF16),
            pltpu.VMEM((width, half), BF16),
            pltpu.VMEM((half, width), BF16),
            pltpu.VMEM((2 * rows, half), BF16),
            pltpu.VMEM((half, 2 * rows), BF16),
            pltpu.VMEM((half, 2 * rows), BF16),
            pltpu.SemaphoreType.DMA((3, half // tile)),
        ],
        compiler_params=params(54),
        cost_estimate=takes(24),
        name="feed_forward",
    )


def cut_columns(size, weight, starts, window, held, sems):
    copies = []
    for k, column in enumerate(starts):
        aligned = pl.multiple_of(
            jnp.minimum(column // LANES * LANES, weight.shape[1] - window), LANES
        )
        copy = pltpu.make_async_copy(weight.at[:, pl.ds(aligned, window)], held.at[k], sems.at[k])
        copy.start()
        copies.append((copy, column - aligned))
    return copies


def place_columns(size, copies, held, out_ref, first):
    depth, window = held.shape[-2:]
    step = min(256, depth)
    for k, (copy, offset) in enumerate(copies):
        copy.wait()
        start = (first + k) * size
        place = start % LANES
        for r in range(0, depth, step):
            block = pltpu.roll(held[k, r : r + step, :], window - offset + place, 1)
            out_ref[r : r + step, start : start + size] = block[:, place : place + size]


def slice_kernel(
    size,
    starts,
    qkv_starts,
    b_ref,
    gate_ref,
    up_ref,
    down_ref,
    qkv_ref,
    out_ref,
    turned_ref,
    qkv_out,
    gate_held,
    up_held,
    qkv_held,
    rows,
    gate_sems,
    up_sems,
    qkv_sems,
    row_sems,
):
    depth, window = gate_held.shape[-2:]
    b = b_ref[0]
    gates = cut_columns(size, gate_ref, starts(b), window, gate_held, gate_sems)
    ups = cut_columns(size, up_ref, starts(b), window, up_held, up_sems)
    row_copies = []
    if down_ref.shape[0] > rows.shape[0]:
        for i, row in enumerate(starts(b)):
            row_copies.append(
                pltpu.make_async_copy(
                    down_ref.at[pl.ds(pl.multiple_of(row, size), size), :],
                    rows.at[pl.ds(i * size, size), :],
                    row_sems.at[i],
                )
            )
    else:
        row_copies.append(pltpu.make_async_copy(down_ref, rows, row_sems.at[0]))
    for copy in row_copies:
        copy.start()
    heads = cut_columns(HD, qkv_ref, qkv_starts(b), LANES, qkv_held, qkv_sems)
    place_columns(size, gates, gate_held, out_ref, 0)
    place_columns(size, ups, up_held, out_ref, len(gates))
    for copy in row_copies:
        copy.wait()
    step = min(256, depth)
    for r in range(0, depth, step):
        turned_ref[r : r + step, :] = rows[:, r : r + step].T
    place_columns(HD, heads, qkv_held, qkv_out, 0)


def own_slices(b, gate, up, down, qkv, starts, qkv_starts, count, size, after=()):
    depth = gate.shape[0]
    heads = len(qkv_starts(0))
    window = LANES * ((size + 2 * LANES - 2) // LANES)
    held = pltpu.VMEM((count, depth, window), BF16)
    sems = pltpu.SemaphoreType.DMA((count,))
    return kernel_call(
        functools.partial(slice_kernel, size, starts, qkv_starts),
        (b, gate, up, down, qkv),
        after,
        in_specs=[SMEM] + [ANY] * 4,
        out_specs=[VMEM] * 3,
        out_shape=[
            jax.ShapeDtypeStruct((depth, 2 * count * size), BF16),
            jax.ShapeDtypeStruct((depth, count * size), BF16),
            jax.ShapeDtypeStruct((depth, heads * HD), BF16),
        ],
        scratch_shapes=[
            held,
            held,
            pltpu.VMEM((heads, depth, LANES), BF16),
            pltpu.VMEM((count * size, depth), BF16),
            sems,
            sems,
            pltpu.SemaphoreType.DMA((heads,)),
            sems,
        ],
        compiler_params=params(44),
        cost_estimate=takes(14),
        name="own_slices",
    )


def fetch_rows(slots_ref, pieces, whole_ref, sems):
    rows = pieces[0].shape[0]
    copies = []
    for k, piece in enumerate(pieces):
        place = pl.multiple_of(slots_ref[k] * rows, rows)
        copies.append(
            pltpu.make_async_copy(piece, whole_ref.at[pl.ds(place, rows), :], sems.at[k])
        )
        copies[-1].start()
    return copies


def project(block, weight, bias_ref, cos_ref, sin_ref, qkv_ref, base):
    here = pl.ds(base, block.shape[0])
    cosine, sine = cos_ref[:, here], sin_ref[:, here]
    heads = qkv_ref.shape[1]
    flat = dot(block, weight).T
    for k in range(3 * heads):
        part, i = k // heads, k % heads
        own = flat[k * HD : (k + 1) * HD, :] + bias_ref[part, i]
        if part < 2:
            own = rotated(own, cosine, sine)
        own = own.astype(BF16)
        qkv_ref[part, i, :, here] = own if part else own * HD**-0.5


def early_kernel(count, slots_ref, weight_ref, bias_ref, cos_ref, sin_ref, *refs):
    pieces, (qkv_ref, held, sems) = refs[:count], refs[count:]
    rows = pieces[0].shape[0]
    copies = []
    for k, piece in enumerate(pieces):
        place = pl.multiple_of((k // 2 * 2 + slots_ref[k] % 2) * rows, rows)
        copies.append(pltpu.make_async_copy(piece, held.at[pl.ds(place, rows), :], sems.at[k]))
        copies[-1].start()
    for copy in copies:
        copy.wait()
    size = 2 * rows
    for k in range(count // 2):
        base = pl.multiple_of(slots_ref[2 * k] // 2 * size, size)
        block = held[k * size : (k + 1) * size, :]
        project(block, weight_ref[...], bias_ref, cos_ref, sin_ref, qkv_ref, base)


def early_projection(slots, weight, bias, cosine, sine, pieces, heads, span, after):
    rows, width = pieces[0].shape
    count = len(pieces)
    return kernel_call(
        functools.partial(early_kernel, count),
        (slots, weight, bias, cosine, sine, *pieces),
        after,
        in_specs=[SMEM, VMEM, VMEM, VMEM, VMEM] + [ANY] * count,
        out_specs=VMEM,
        out_shape=jax.ShapeDtypeStruct((3, heads, HD, span), BF16),
        scratch_shapes=[
            pltpu.VMEM((count * rows, width), BF16),
            pltpu.SemaphoreType.DMA((count,)),
        ],
        compiler_params=params(32),
        cost_estimate=takes(8),
        name="early_projection",
    )


def forward_kernel(
    count, early, length_ref, slots_ref, weight_ref, bias_ref, cos_ref, sin_ref, *refs
):
    pieces = refs[:count]
    refs = refs[count:]
    if early:
        early_ref, refs = refs[0], refs[1:]
    (
        whole_out,
        qkv_ref,
        att_ref,
        low_ref,
        lse_ref,
        whole_ref,
        marked,
        triangle,
        sems,
        out_sem,
    ) = refs
    _, heads, _, span = qkv_ref.shape
    length = length_ref[0]
    copies = fetch_rows(slots_ref, pieces, whole_ref, sems)
    size = 256
    if early:
        bases = [
            pl.multiple_of(slots_ref[2 * k] // 2 * size, size) for k in range(span // size)
        ]
        for base in bases[:early]:
            qkv_ref[:, :, :, pl.ds(base, size)] = early_ref[:, :, :, pl.ds(base, size)]
    else:
        bases = list(range(0, span, size))
    for copy in copies:
        copy.wait()
    leaving = pltpu.make_async_copy(whole_ref, whole_out, out_sem)
    leaving.start()
    for base in bases[early:]:
        block = whole_ref[pl.ds(base, size), :]
        project(block, weight_ref[...], bias_ref, cos_ref, sin_ref, qkv_ref, base)

    mark_keys(marked, triangle, length)

    def head(i, carry):
        marked[0, :HD, :] = qkv_ref[1, i]
        marked[1, :HD, :] = qkv_ref[0, i]
        for start in range(0, span, BQ):
            end = start + BQ
            parts = score_parts(marked, triangle, start)
            best = functools.reduce(
                jnp.maximum, [jnp.max(scores, axis=0, keepdims=True) for _, _, scores in parts]
            )
            total, out = 0.0, 0.0
            for low, high, scores in parts:
                weights = jnp.exp(scores - best)
                total += jnp.sum(weights, axis=0, keepdims=True)
                out += dot(qkv_ref[2, i, :, low:high], weights.astype(BF16))
            out = out / total
            att_ref[i, :, start:end] = out
            low_ref[i, :, start:end] = out.astype(BF16)
            lse_ref[i, :, start:end] = best + jnp.log(total)
        return carry

    lax.fori_loop(0, heads, head, 0)
    leaving.wait()


def attention_forward(
    length, slots, weight, bias, cosine, sine, pieces, early, pairs, heads, after
):
    width = weight.shape[0]
    span = len(pieces) * pieces[0].shape[0]
    count = len(pieces)
    return kernel_call(
        functools.partial(forward_kernel, count, pairs),
        (length, slots, weight, bias, cosine, sine, *pieces, *early),
        after,
        in_specs=[SMEM, SMEM, VMEM, VMEM, VMEM, VMEM] + [ANY] * count + [VMEM] * len(early),
        out_specs=[ANY] + [VMEM] * 4,
        out_shape=[
            jax.ShapeDtypeStruct((span, width), BF16),
            jax.ShapeDtypeStruct((3, heads, HD, span), BF16),
            jax.ShapeDtypeStruct((heads, HD, span), F32),
            jax.ShapeDtypeStruct((heads, HD, span), BF16),
            jax.ShapeDtypeStruct((heads, 1, span), F32),
        ],
        scratch_shapes=[
            pltpu.VMEM((span, width), BF16),
            *mark_shapes(span),
            pltpu.SemaphoreType.DMA((count,)),
            pltpu.SemaphoreType.DMA,
        ],
        compiler_params=params(48),
        cost_estimate=takes(20),
        name="attention_forward",
    )


def backward_kernel(
    count, b_ref, length_ref, slots_ref, weight_ref, qkv_ref, att_ref, lse_ref, cos_ref, sin_ref, *refs
):
    pieces = refs[:count]
    (
        whole_out,
        out_ref,
        flat_ref,
        whole_ref,
        weight,
        grad_ref,
        dq,
        dk,
        dv,
        turned,
        marked,
        triangle,
        weight_sem,
        sems,
        out_sem,
    ) = refs[count:]
    _, heads, _, span = qkv_ref.shape
    cosine, sine = cos_ref[...], -sin_ref[...]
    n_blk = out_ref.shape[0]
    weight_copies = []
    for i in range(heads):
        row = pl.multiple_of((n_blk * i + b_ref[0]) * HD, HD)
        weight_copies.append(
            pltpu.make_async_copy(
                weight_ref.at[pl.ds(row, HD), :],
                weight.at[pl.ds(i * HD, HD), :],
                weight_sem.at[i],
            )
        )
        weight_copies[-1].start()
    copies = fetch_rows(slots_ref, pieces, whole_ref, sems)
    mark_keys(marked, triangle, length_ref[0])
    for copy in weight_copies:
        copy.wait()
    across = weight[...].T
    for copy in copies:
        copy.wait()
    leaving = pltpu.make_async_copy(whole_ref, whole_out, out_sem)
    leaving.start()
    for start in range(0, span, BQ):
        grads = dot(whole_ref[start : start + BQ, :], across).T.astype(BF16)
        for i in range(heads):
            grad_ref[i, :, start : start + BQ] = grads[i * HD : (i + 1) * HD, :]

    def head(i, carry):
        dk[...] = jnp.zeros_like(dk)
        dv[...] = jnp.zeros_like(dv)
        marked[0, :HD, :] = qkv_ref[1, i]
        marked[1, :HD, :] = qkv_ref[0, i]
        for start in range(0, span, BQ):
            end = start + BQ
            queries, grads = qkv_ref[0, i, :, start:end], grad_ref[i, :, start:end]
            delta = jnp.sum(grads.astype(F32) * att_ref[i, :, start:end], axis=0, keepdims=True)
            prob = jnp.exp(scores_until(marked, triangle, start) - lse_ref[i, :, start:end])
            grad_prob = dot(qkv_ref[2, i, :, :end], grads, 0, 0)
            grad_score = (prob * (grad_prob - delta)).astype(BF16)
            dq[:, start:end] = dot(qkv_ref[1, i, :, :end], grad_score) * HD**-0.5
            dk[:, :end] += dot(queries, grad_score, 1, 1)
            dv[:, :end] += dot(grads, prob.astype(BF16), 1, 1)
        turned[0, i] = rotated(dq[...], cosine, sine).astype(BF16)
        turned[1, i] = rotated(dk[...], cosine, sine).astype(BF16)
        turned[2, i] = dv[...].astype(BF16)
        return carry

    lax.fori_loop(0, heads, head, 0)
    rows = out_ref.shape[2]
    for part in range(3):
        for i in range(heads):
            k = part * heads + i
            flat_ref[:, k * HD : (k + 1) * HD] = turned[part, i].T
            for j in range(n_blk):
                out_ref[j, k * HD : (k + 1) * HD, :] = turned[part, i, :, j * rows : (j + 1) * rows]
    for i in range(heads):
        k = 3 * heads + i
        for j in range(n_blk):
            out_ref[j, k * HD : (k + 1) * HD, :] = att_ref[
                i, :, j * rows : (j + 1) * rows
            ].astype(BF16)
    leaving.wait()


def attention_backward(
    b, length, slots, weight, qkv, att, lse, cosine, sine, pieces, n_blk, after=()
):
    _, heads, _, span = qkv.shape
    width = weight.shape[1]
    count = len(pieces)
    return kernel_call(
        functools.partial(backward_kernel, count),
        (b, length, slots, weight, qkv, att, lse, cosine, sine, *pieces),
        after,
        in_specs=[SMEM, SMEM, SMEM, ANY] + [VMEM] * 5 + [ANY] * count,
        out_specs=[ANY] + [VMEM] * 2,
        out_shape=[
            jax.ShapeDtypeStruct((span, width), BF16),
            jax.ShapeDtypeStruct((n_blk, 4 * heads * HD, span // n_blk), BF16),
            jax.ShapeDtypeStruct((span, 3 * heads * HD), BF16),
        ],
        scratch_shapes=[
            pltpu.VMEM((span, width), BF16),
            pltpu.VMEM((heads * HD, width), BF16),
            pltpu.VMEM((heads, HD, span), BF16),
        ]
        + [pltpu.VMEM((HD, span), F32)] * 3
        + [
            pltpu.VMEM((3, heads, HD, span), BF16),
            *mark_shapes(span),
            pltpu.SemaphoreType.DMA((heads,)),
            pltpu.SemaphoreType.DMA((count,)),
            pltpu.SemaphoreType.DMA,
        ],
        compiler_params=params(40),
        cost_estimate=takes(18),
        name="attention_backward",
    )


def grads_kernel(n_dp, n_ref, c_ref, gate_up_ref, down_ref, act_ref, grad_ref):
    cols = down_ref.shape[1]
    both = dot(n_ref[...], gate_up_ref[...])
    gate, up = both[:, :cols], both[:, cols:]
    sig = jax.nn.sigmoid(gate)
    silu = gate * sig
    act = silu * up
    part = cols // n_dp
    for i in range(n_dp):
        act_ref[i] = act[:, i * part : (i + 1) * part].T.astype(BF16)
    grad_act = dot(c_ref[...], down_ref[...])
    grad_ref[:, :cols] = (grad_act * up * sig * (1.0 + gate * (1.0 - sig))).astype(BF16)
    grad_ref[:, cols:] = (grad_act * silu).astype(BF16)


def local_grads(all_normed, all_grad, gate_up, down, n_dp, after=()):
    span, width = all_normed.shape
    cols = down.shape[1]
    size = 256
    return kernel_call(
        functools.partial(grads_kernel, n_dp),
        (all_normed, all_grad, gate_up, down),
        after,
        grid=(span // size,),
        in_specs=[
            pl.BlockSpec((size, width), lambda r: (r, 0)),
            pl.BlockSpec((size, width), lambda r: (r, 0)),
            pl.BlockSpec((width, 2 * cols), lambda r: (0, 0)),
            pl.BlockSpec((width, cols), lambda r: (0, 0)),
        ],
        out_specs=[
            pl.BlockSpec((n_dp, cols // n_dp, size), lambda r: (0, 0, r)),
            pl.BlockSpec((size, 2 * cols), lambda r: (r, 0)),
        ],
        out_shape=[
            jax.ShapeDtypeStruct((n_dp, cols // n_dp, span), BF16),
            jax.ShapeDtypeStruct((span, 2 * cols), BF16),
        ],
        compiler_params=params(48),
        cost_estimate=takes(15),
        name="local_grads",
    )


def keep(value, first, on_ref, mine_ref, cut):
    value += first.astype(F32)

    @pl.when(pl.program_id(0) < cut)
    def _():
        on_ref[...] = value.astype(BF16)

    @pl.when(pl.program_id(0) >= cut)
    def _():
        mine_ref[...] = value


def column_products_kernel(low, high, order_ref, left_ref, right_ref, *refs):
    value = dot(left_ref[...], right_ref[:, low:high], 0, 0)
    if len(refs) == 1:
        refs[0][0] = value.astype(BF16)
    else:
        keep(value, refs[0][0, :, low:high], *refs[1:], 2)


def column_products(order, left, right, low, high, n_dp, first=None, after=()):
    span, width = left.shape
    cols = high - low
    size = width // n_dp
    part = size // 2
    stay = [
        pl.BlockSpec((part, cols), lambda j, order: (jnp.minimum(j, 1), 0)),
        pl.BlockSpec((part, cols), lambda j, order: (jnp.maximum(j - 2, 0), 0)),
    ]
    block = pl.BlockSpec(
        (1, part, cols if first is None else right.shape[1]), lambda j, order: (j // 2, j % 2, 0)
    )
    return kernel_call(
        functools.partial(column_products_kernel, low, high),
        (order, left, right) + (() if first is None else (first,)),
        after,
        prefetch=1,
        grid=(4,),
        in_specs=[
            pl.BlockSpec((span, part), lambda j, order: (0, order[j // 2] * 2 + j % 2)),
            pl.BlockSpec(right.shape, lambda j, order: (0, 0)),
        ]
        + ([] if first is None else [block]),
        out_specs=block if first is None else stay,
        out_shape=jax.ShapeDtypeStruct((2, size, cols), BF16)
        if first is None
        else [jax.ShapeDtypeStruct((size, cols), dtype) for dtype in (BF16, F32)],
        compiler_params=params(24),
        cost_estimate=takes(8),
        name="column_products",
    )


def row_products_kernel(count, order_ref, *refs):
    lefts, right_ref, rest = refs[:count], refs[count], refs[count + 1 :]
    value = [dot(left[0], right_ref[...]) for left in lefts]
    value = jnp.concatenate(value, axis=0) if count > 1 else value[0]
    if len(rest) == 1:
        rest[0][0] = value.astype(BF16)
    else:
        keep(value, rest[0][0], *rest[1:], 1)


def row_products(order, lefts, right, first=None, after=()):
    span, width = right.shape
    size = sum(left.shape[1] for left in lefts)
    block = pl.BlockSpec((1, size, width), lambda j, order: (j, 0, 0))
    stay = pl.BlockSpec((size, width), lambda j, order: (0, 0))
    return kernel_call(
        functools.partial(row_products_kernel, len(lefts)),
        (order, *lefts, right) + (() if first is None else (first,)),
        after,
        prefetch=1,
        grid=(2,),
        in_specs=[
            pl.BlockSpec((1,) + left.shape[1:], lambda j, order: (order[j], 0, 0))
            for left in lefts
        ]
        + [pl.BlockSpec((span, width), lambda j, order: (0, 0))]
        + ([] if first is None else [block]),
        out_specs=block if first is None else [stay, stay],
        out_shape=jax.ShapeDtypeStruct((2, size, width), BF16)
        if first is None
        else [jax.ShapeDtypeStruct((size, width), dtype) for dtype in (BF16, F32)],
        compiler_params=params(24),
        cost_estimate=takes(8),
        name="row_products",
    )


def add_kernel(mine_ref, second_ref, *out_refs):
    total = mine_ref[...] + second_ref[...].astype(F32)
    start = 0
    for out_ref in out_refs:
        size = out_ref.shape[0]
        out_ref[...] = total[start : start + size].astype(out_ref.dtype)
        start += size


def add_second(mine, second, sizes, dtype, after=(), us=16):
    _, cols = mine.shape
    return kernel_call(
        add_kernel,
        (mine, second),
        after,
        in_specs=[VMEM] * 2,
        out_specs=[VMEM] * len(sizes),
        out_shape=[jax.ShapeDtypeStruct((part, cols), dtype) for part in sizes],
        compiler_params=params(16),
        cost_estimate=takes(us),
        name="add_second",
    )


def spread_kernel(count, outer, size, line, *refs):
    arrays, out_refs = refs[:count], refs[count:]
    n_blk = arrays[0].shape[0]
    if line:
        out_refs, line_refs = out_refs[:-3], out_refs[-3:]
        rows = out_refs[0].shape[0]
        sums = sum(arrays[-1][b, rows : rows + EXTRA, :line].astype(F32) for b in range(n_blk))
        start = 0
        for line_ref in line_refs:
            end = start + line_ref.shape[1]
            line_ref[...] = sums[:1, start:end]
            start = end
    for k, out_ref in enumerate(out_refs):
        rows = out_ref.shape[0]
        for i in range(outer):
            for b in range(n_blk):
                source = (k * outer + i) * size
                place = (i * n_blk + b) * size
                start = 0
                for array in arrays:
                    end = start + array.shape[2]
                    low, high = max(source, start), min(source + size, end)
                    if low < high:
                        out_ref[:, place + low - source : place + high - source] = array[
                            b, :rows, low - start : high - start
                        ].astype(F32)
                    start = end


def spread(arrays, rows, outputs, outer, size, line=0, after=()):
    n_blk = arrays[0].shape[0]
    return kernel_call(
        functools.partial(spread_kernel, len(arrays), outer, size, line),
        tuple(arrays),
        after,
        in_specs=[VMEM] * len(arrays),
        out_specs=[VMEM] * (outputs + 3 * (line > 0)),
        out_shape=[jax.ShapeDtypeStruct((rows, outer * n_blk * size), F32)] * outputs
        + [jax.ShapeDtypeStruct((1, n * line // 5), F32) for n in (1, 1, 3) if line],
        compiler_params=params(16),
        cost_estimate=takes(3),
        name="spread",
    )


def out_kernel(x_ref, ffn_ref, other_ref, weight_ref, pieces, out_ref, left, total):
    n_blk, lines, _ = pieces.shape
    heads = lines // HD // 4
    step = pl.program_id(0)
    size = left.shape[2]

    @pl.when(step == 0)
    def _():
        for i in range(heads):
            for b in range(n_blk):
                place = (i * n_blk + b) * HD
                block, start = place // size, place % size
                k = 3 * heads + i
                left[block, :, start : start + HD] = pieces[b, k * HD : (k + 1) * HD, :].T
        total[...] = x_ref[...].astype(F32) + ffn_ref[...] + other_ref[0].astype(F32)

    total[...] += dot(left[step], weight_ref[...])

    @pl.when(step == pl.num_programs(0) - 1)
    def _():
        out_ref[...] = total[...].astype(BF16)


def project_out(tokens, ffn_out, other, weight, pieces, after=()):
    rows, width = tokens.shape
    steps = 4
    size = width // steps
    whole = pl.BlockSpec((rows, width), lambda t: (0, 0))
    return kernel_call(
        out_kernel,
        (tokens, ffn_out, other, weight, pieces),
        after,
        grid=(steps,),
        in_specs=[
            whole,
            whole,
            pl.BlockSpec((1, rows, width), lambda t: (0, 0, 0)),
            pl.BlockSpec((size, width), lambda t: (t, 0)),
            pl.BlockSpec(pieces.shape, lambda t: (0, 0, 0)),
        ],
        out_specs=whole,
        out_shape=jax.ShapeDtypeStruct((rows, width), BF16),
        scratch_shapes=[pltpu.VMEM((steps, rows, size), BF16), pltpu.VMEM((rows, width), F32)],
        compiler_params=params(20),
        cost_estimate=takes(6),
        name="project_out",
    )


def input_kernel(
    x_ref, c_ref, gain_ref, ffn_ref, other_ref, weight_ref, pieces, out_ref, sums_ref, left, total
):
    n_blk, lines, _ = pieces.shape
    step, steps = pl.program_id(0), pl.num_programs(0)
    size = left.shape[1]

    @pl.when(step == 0)
    def _():
        for i in range(3 * (lines // HD // 4)):
            for b in range(n_blk):
                place = (i * n_blk + b) * HD
                block, start = place // size, place % size
                left[block, start : start + HD, :] = pieces[b, i * HD : (i + 1) * HD, :]
        total[...] = jnp.zeros_like(total)

    total[...] += dot(weight_ref[...], left[step])

    @pl.when(step == steps - 1)
    def _():
        x = x_ref[...].astype(F32)
        center = x - jnp.mean(x, axis=1, keepdims=True)
        inverse_std = lax.rsqrt(jnp.mean(center * center, axis=1, keepdims=True) + epsilon)
        normalized = center * inverse_std
        grad = ffn_ref[...] + other_ref[0].astype(F32) + total[...].T
        vectors = [
            jnp.sum(grad * normalized, axis=0, keepdims=True),
            jnp.sum(grad, axis=0, keepdims=True),
        ] + [jnp.sum(left[t].astype(F32).T, axis=0, keepdims=True) for t in range(left.shape[0])]
        flat = jnp.concatenate(vectors, axis=1)
        shards = sums_ref.shape[0]
        width = grad.shape[1]
        cut = width // shards
        for j in range(shards):
            sums_ref[j : j + 1, :cut] = flat[:, j * cut : (j + 1) * cut]
            sums_ref[j : j + 1, cut : 2 * cut] = flat[:, width + j * cut : width + (j + 1) * cut]
            start = 2 * width + 3 * j * cut
            sums_ref[j : j + 1, 2 * cut :] = flat[:, start : start + 3 * cut]
        grad = grad * gain_ref[...]
        grad_inputs = inverse_std * (
            grad
            - jnp.mean(grad, axis=1, keepdims=True)
            - normalized * jnp.mean(grad * normalized, axis=1, keepdims=True)
        )
        out_ref[...] = (c_ref[...].astype(F32) + grad_inputs).astype(BF16)


def input_grads(
    tokens, out_grad, gain, ffn_grad, other, weight, pieces, shards, after=()
):
    rows, width = tokens.shape
    cols = weight.shape[1]
    steps = 8
    size = cols // steps
    whole = pl.BlockSpec((rows, width), lambda t: (0, 0))
    return kernel_call(
        input_kernel,
        (tokens, out_grad, gain, ffn_grad, other, weight, pieces),
        after,
        grid=(steps,),
        in_specs=[
            whole,
            whole,
            pl.BlockSpec((1, width), lambda t: (0, 0)),
            whole,
            pl.BlockSpec((1, rows, width), lambda t: (1, 0, 0)),
            pl.BlockSpec((width, size), lambda t: (0, t)),
            pl.BlockSpec(pieces.shape, lambda t: (0, 0, 0)),
        ],
        out_specs=[whole, pl.BlockSpec((shards, 5 * width // shards), lambda t: (0, 0))],
        out_shape=[
            jax.ShapeDtypeStruct((rows, width), BF16),
            jax.ShapeDtypeStruct((shards, 5 * width // shards), F32),
        ],
        scratch_shapes=[pltpu.VMEM((steps, size, rows), BF16), pltpu.VMEM((width, rows), F32)],
        compiler_params=params(28),
        cost_estimate=takes(13),
        name="input_grads",
    )


def on_device(
    n_dp,
    n_blk,
    tokens,
    norm_gain,
    norm_bias,
    qkv_weight,
    qkv_bias,
    out_weight,
    gate_weight,
    up_weight,
    down_weight,
    cotangent,
    lengths,
):
    rows, width = tokens.shape[1:]
    span = rows * n_blk
    hidden = gate_weight.shape[1]
    per_dev = width // HD // n_blk
    ff_block = hidden // (n_dp * n_blk)
    d, b = lax.axis_index("dp").astype(jnp.int32), lax.axis_index("blk").astype(jnp.int32)
    own_tokens, out_grad = tokens[0], cotangent[0]

    inputs = own_tokens.astype(F32)
    center = inputs - jnp.mean(inputs, axis=1, keepdims=True)
    inverse_std = lax.rsqrt(jnp.mean(center * center, axis=1, keepdims=True) + epsilon)
    normed = (center * inverse_std * norm_gain + norm_bias).astype(BF16)

    position = b.reshape(1)

    def ff_starts(b):
        return [(n_blk * i + b) * ff_block for i in range(n_dp)]

    def qkv_starts(b):
        return [part * width + (n_blk * i + b) * HD for part in range(3) for i in range(per_dev)]

    def own_blocks(array, outer, size):
        cut = array.reshape((outer, n_blk, size) + array.shape[1:])
        return lax.dynamic_index_in_dim(cut, b, 1, keepdims=False).reshape(
            (-1,) + array.shape[1:]
        )

    down_rows = down_weight if ff_block % 16 == 0 else own_blocks(down_weight, n_dp, ff_block)

    def slices():
        return own_slices(
            position,
            gate_weight,
            up_weight,
            down_rows,
            qkv_weight,
            ff_starts,
            qkv_starts,
            n_dp,
            ff_block,
        )

    def ffn(normed_other, grad_other, after):
        return feed_forward(
            position,
            (normed, normed_other),
            (out_grad, grad_other),
            (gate_weight, up_weight, down_weight),
            after,
        )

    own_bias = own_blocks(qkv_bias, 3 * per_dev, HD).reshape(3, per_dev, HD, 1)
    frequency = 10000.0 ** (-2.0 * np.arange(HALF) / ROT)
    angles = frequency[:, None] * np.arange(span)[None, :]
    cosine, sine = np.cos(angles).astype(np.float32), np.sin(angles).astype(np.float32)


    if n_blk == 8:
        slots = piece_slots(b)
        n1, m0, c1, e0 = along(normed), beside(normed, 8), along(out_grad), beside(out_grad, 8)
        n3 = back(normed)
        own_gate_up, own_down, own_qkv = slices()
        c1, e0 = relay([c1, e0], [own_down])
        (n1,) = relay([n1], [c1])
        m1, e1, n2, c2 = beside(n1, 8), beside(c1, 8), along(n1), along(c1)
        (n3,) = relay([n3], [n1])
        m3 = beside(n3, 8)
        ffn_out, ffn_grad, passed = ffn(m0, e0, [n3])
        n2, c3, e3 = relay([n2, out_grad, e0], [ffn_out, m1, e1])
        m2, c3, e3 = beside(n2, 8), back(c3), back(e3)
        (c2,) = relay([c2], [n2])
        e2 = beside(c2, 8)
        normed_pieces = [normed, m0, n1, m1, n3, m3, n2, m2]
        grad_pieces = [out_grad, e0, c1, e1, c3, e3, c2, e2]
        early = [
            early_projection(
                slots, own_qkv, own_bias, cosine, sine, normed_pieces[:6], per_dev, span, [n2]
            )
        ]
        arrived = [c2]
    else:
        slots = jnp.zeros((1,), jnp.int32)
        normed_pieces = [lax.all_gather(normed, "blk", axis=0, tiled=True)]
        grad_pieces = [lax.all_gather(out_grad, "blk", axis=0, tiled=True)]
        own_gate_up, own_down, own_qkv = slices()
        ffn_out, ffn_grad, passed = ffn(
            beside(normed, n_blk), beside(out_grad, n_blk), [own_down]
        )
        early, arrived = [], []

    all_normed, qkv, att, att_low, lse = attention_forward(
        lengths,
        slots,
        own_qkv,
        own_bias,
        cosine,
        sine,
        normed_pieces,
        early,
        3 * len(early),
        per_dev,
        [ffn_out, *arrived],
    )
    all_grad, grad_cut, grad_qkv = attention_backward(
        position,
        lengths,
        slots,
        out_weight,
        qkv,
        att,
        lse,
        cosine,
        sine,
        grad_pieces,
        n_blk,
    )
    grad_rows = swap_blk(grad_cut)

    sent = jnp.stack([d ^ 3, d ^ 1])
    kept = jnp.stack([d ^ 2, d])

    def over_first(array):
        return lax.ppermute(array, "dp", [(i, i ^ 1) for i in range(4)])

    def over_second(array):
        return lax.ppermute(array, "dp", [(i, i ^ 2) for i in range(4)])

    def row_cut(total):
        return swap_blk(total.reshape(n_blk, -1, total.shape[1]))

    ff_cols, qkv_cols = 2 * n_dp * ff_block, 3 * per_dev * HD
    aligned = per_dev == n_dp
    shards = n_dp * n_blk
    line = 5 * width // shards
    full = [width // n_dp]

    qkv_sent = column_products(sent, all_normed, grad_qkv, 0, qkv_cols, n_dp)
    qkv_first = over_first(qkv_sent)
    act, grad_ff = local_grads(
        all_normed, all_grad, own_gate_up, own_down, n_dp, [qkv_sent]
    )
    lefts = [act, att_low] if aligned else [act]
    qkv_on, qkv_mine = column_products(
        kept, all_normed, grad_qkv, 0, qkv_cols, n_dp, qkv_first, [act]
    )
    qkv_second = over_second(qkv_on)
    ff_sent = column_products(sent, all_normed, grad_ff, 0, ff_cols, n_dp, None, [qkv_on])
    ff_first = over_first(ff_sent)
    row_sent = row_products(sent, lefts, all_grad, None, [ff_sent])
    row_first = over_first(row_sent)
    (qkv_total,) = add_second(qkv_mine, qkv_second, full, BF16, [row_sent], 24)
    qkv_pieces = row_cut(qkv_total)
    ff_on, ff_mine = column_products(
        kept, all_normed, grad_ff, 0, ff_cols, n_dp, ff_first, [qkv_total]
    )
    ff_second = over_second(ff_on)
    row_on, row_mine = row_products(kept, lefts, all_grad, row_first, [ff_on])
    (passed,) = relay([passed], [grad_cut])
    ffn_other = beside(passed, n_blk)
    input_grad, vectors = input_grads(
        own_tokens,
        out_grad,
        norm_gain[None],
        ffn_grad,
        ffn_other,
        qkv_weight,
        grad_rows,
        shards,
        [row_on],
    )
    (ff_total,) = add_second(ff_mine, ff_second, full, BF16, [input_grad], 1)
    vectors = vectors.reshape(n_dp, n_blk, line)

    def of(mask):
        return lax.dynamic_index_in_dim(vectors, d ^ mask, 0, keepdims=False)

    vector_first = over_first(jnp.stack([of(3), of(1)]))
    vector_second = over_second(of(2) + vector_first[0])
    (row_on,) = relay([row_on], [vector_second])
    row_second = over_second(row_on)
    layer_out = project_out(own_tokens, ffn_out, ffn_other, out_weight, grad_rows, [input_grad])
    vectors = of(0) + vector_first[1] + vector_second
    below = jnp.pad(vectors.astype(BF16)[:, None], ((0, 0), (0, EXTRA - 1), (0, ff_cols - line)))
    ff_pieces = swap_blk(
        jnp.concatenate([ff_total.reshape(n_blk, -1, ff_cols), below], axis=1)
    )
    sizes = [ff_block, HD] if aligned else [ff_block]
    shard_down, *shard_out = add_second(row_mine, row_second, sizes, F32)
    if aligned:
        shard_out = shard_out[0]
    else:
        grad_out = dot(att_low.reshape(-1, span), all_grad)
        wide = jnp.zeros((width, width), F32)
        for i in range(per_dev):
            start = (n_blk * i + b) * HD
            wide = lax.dynamic_update_slice(wide, grad_out[i * HD : (i + 1) * HD], (start, 0))
        shard_out = lax.psum_scatter(wide, ("dp", "blk"), scatter_dimension=0, tiled=True)
    cut = width // shards
    (shard_qkv,) = spread([qkv_pieces], cut, 1, 3 * per_dev, HD)
    shard_gate, shard_up, *sums = spread([ff_pieces], cut, 2, n_dp, ff_block, line)
    return (
        layer_out[None],
        input_grad[None],
        sums[0].reshape(-1),
        sums[1].reshape(-1),
        shard_qkv,
        sums[2].reshape(-1),
        shard_out,
        shard_gate,
        shard_up,
        shard_down,
    )


def solution(mesh):
    both = P(("dp", "blk"))
    row_cut = P(("dp", "blk"), None)
    activation = P("dp", "blk", None)
    return jax.shard_map(
        functools.partial(on_device, mesh.shape["dp"], mesh.shape["blk"]),
        mesh=mesh,
        in_specs=(activation,) + (P(),) * 8 + (activation, P("dp")),
        out_specs=(activation, activation, both, both, row_cut, both) + (row_cut,) * 4,
        check_vma=False,
    )
```

```python
import functools

import jax
import jax.numpy as jnp
import numpy as np
from jax import lax
from jax.experimental import pallas as pl
from jax.experimental.pallas import tpu as pltpu
from jax.sharding import PartitionSpec as P

HD = 64
ROT = 16
HALF = ROT // 2

epsilon = 1e-05
masked_score = -1e30
BQ = 256
LANES = 128
EXTRA = 8
SCALE = 1.0
F32 = jnp.float32
BF16 = jnp.bfloat16


def dot(left, right, left_dim=1, right_dim=0):
    return lax.dot_general(
        left, right, (((left_dim,), (right_dim,)), ((), ())), preferred_element_type=F32
    )


RING = [0, 1, 3, 2]
ALONG = [(2 * RING[r] + y, 2 * RING[(r + 1) % 4] + y) for r in range(4) for y in range(2)]


def along(piece):
    return lax.ppermute(piece, "blk", ALONG)


def back(piece):
    return lax.ppermute(piece, "blk", [(target, source) for source, target in ALONG])


def beside(piece, n_blk):
    return lax.ppermute(piece, "blk", [(i, i ^ 1) for i in range(n_blk)])


def piece_slots(b):
    z, y = b // 2, b % 2
    place = z ^ (z >> 1)
    slots = []
    for step in (0, 1, 3, 2):
        slot = (place - step) % 4
        source = slot ^ (slot >> 1)
        slots += [2 * source + y, 2 * source + 1 - y]
    return jnp.stack(slots).astype(jnp.int32)


def swap_blk(pieces):
    return lax.all_to_all(pieces, "blk", split_axis=0, concat_axis=0, tiled=True)


def rotated(block, cosine, sine):
    a, b = block[:HALF], block[HALF:ROT]
    return jnp.concatenate([a * cosine - b * sine, b * cosine + a * sine, block[ROT:]], axis=0)


def mark_keys(marked, triangle, length):
    shape = (marked.shape[1] - HD, marked.shape[2])
    line = lax.broadcasted_iota(jnp.int32, shape, 0)
    key = lax.broadcasted_iota(jnp.int32, shape, 1)
    beyond = jnp.where((line == 0) & (key >= length), masked_score, 0.0)
    marked[0, HD:, :] = beyond.astype(BF16)
    marked[1, HD:, :] = jnp.where(line == 0, 1.0, 0.0).astype(BF16)
    key = lax.broadcasted_iota(jnp.int32, triangle.shape, 0)
    query = lax.broadcasted_iota(jnp.int32, triangle.shape, 1)
    triangle[...] = jnp.where(key <= query, 0.0, masked_score)


def score_parts(marked, triangle, start):
    queries = marked[1, :, start : start + BQ]
    parts = [
        (start, start + BQ, dot(marked[0, :, start : start + BQ], queries, 0, 0) + triangle[...])
    ]
    if start:
        parts.append((0, start, dot(marked[0, :, :start], queries, 0, 0)))
    return parts


def scores_until(marked, triangle, start):
    end = start + BQ
    scores = dot(marked[0, :, :end], marked[1, :, start:end], 0, 0)
    if not start:
        return scores + triangle[...]
    return jnp.concatenate([scores[:start], scores[start:] + triangle[...]], axis=0)


MARKED = 16


def mark_shapes(span):
    return [pltpu.VMEM((2, HD + MARKED, span), BF16), pltpu.VMEM((BQ, BQ), F32)]


ANY = pl.BlockSpec(memory_space=pl.ANY)
VMEM = pl.BlockSpec(memory_space=pltpu.VMEM)
SMEM = pl.BlockSpec(memory_space=pltpu.SMEM)


def kernel_call(kernel, args, after=(), prefetch=0, **options):
    in_specs = list(options.pop("in_specs")) + [ANY] * len(after)
    count = len(args)

    def body(*refs):
        kernel(*refs[:count], *refs[count + len(after) :])

    if prefetch:
        options["grid_spec"] = pltpu.PrefetchScalarGridSpec(
            num_scalar_prefetch=prefetch,
            in_specs=in_specs,
            **{k: options.pop(k) for k in ("grid", "out_specs", "scratch_shapes") if k in options},
        )
    else:
        options["in_specs"] = in_specs
    return pl.pallas_call(body, **options)(*args, *after)


def relay(arrays, after):
    count = len(arrays)
    return pl.pallas_call(
        lambda *refs: None,
        in_specs=[ANY] * (count + len(after)),
        out_specs=[ANY] * count,
        out_shape=[jax.ShapeDtypeStruct(array.shape, array.dtype) for array in arrays],
        input_output_aliases={k: k for k in range(count)},
        compiler_params=pltpu.CompilerParams(has_side_effects=True),
        cost_estimate=takes(1),
        name="relay",
    )(*arrays, *after)


def takes(us):
    return pl.CostEstimate(flops=int(us * SCALE * 1.15e9), bytes_accessed=1 << 16, transcendentals=0)


def params(mib):
    return pltpu.CompilerParams(vmem_limit_bytes=mib << 20)


def ffn_kernel(
    tile,
    b_ref,
    n_ref,
    n_other,
    c_ref,
    c_other,
    gate_ref,
    up_ref,
    down_ref,
    out_ref,
    grad_ref,
    pass_ref,
    normed,
    flipped,
    gate_w,
    up_w,
    down_w,
    act,
    grad_gate,
    grad_up,
    sems,
):
    rows, width = n_ref.shape
    half = gate_w.shape[1]
    count = half // tile
    base = b_ref[0] % 2 * half

    def copies(t):
        here = pl.ds(pl.multiple_of(t * tile, tile), tile)
        there = pl.ds(pl.multiple_of(base + t * tile, LANES), tile)
        return [
            pltpu.make_async_copy(gate_ref.at[:, there], gate_w.at[:, here], sems.at[0, t]),
            pltpu.make_async_copy(up_ref.at[:, there], up_w.at[:, here], sems.at[1, t]),
            pltpu.make_async_copy(down_ref.at[there, :], down_w.at[here, :], sems.at[2, t]),
        ]

    for t in range(count):
        for copy in copies(t):
            copy.start()
    normed[:rows, :] = n_ref[...]
    normed[rows:, :] = n_other[...]
    flipped[:, :rows] = c_ref[...].T
    flipped[:, rows:] = c_other[...].T

    def first(t, carry):
        for copy in copies(t):
            copy.wait()
        here = pl.ds(pl.multiple_of(t * tile, tile), tile)
        gate = dot(normed[...], gate_w[:, here])
        up = dot(normed[...], up_w[:, here])
        grad_act = dot(down_w[here, :], flipped[...])
        sig = jax.nn.sigmoid(gate)
        silu = gate * sig
        act[:, here] = (silu * up).astype(BF16)
        by_gate = (up * sig * (1.0 + gate * (1.0 - sig))).T
        grad_gate[here, :] = (grad_act * by_gate).astype(BF16)
        grad_up[here, :] = (grad_act * silu.T).astype(BF16)
        return carry

    lax.fori_loop(0, count, first, 0)
    step = 1024

    def second(r, carry):
        here = pl.ds(pl.multiple_of(r * step, step), step)
        out = dot(act[...], down_w[:, here])
        out_ref[:, here] = out[:rows]
        pass_ref[0, :, here] = out[rows:].astype(BF16)
        grad = (dot(gate_w[here, :], grad_gate[...]) + dot(up_w[here, :], grad_up[...])).T
        grad_ref[:, here] = grad[:rows]
        pass_ref[1, :, here] = grad[rows:].astype(BF16)
        return carry

    lax.fori_loop(0, width // step, second, 0)


def feed_forward(b, normed, out_grad, weights, after):
    rows, width = normed[0].shape
    half = weights[0].shape[1] // 2
    tile = 256
    return kernel_call(
        functools.partial(ffn_kernel, tile),
        (b, *normed, *out_grad, *weights),
        after,
        in_specs=[SMEM] + [VMEM] * 4 + [ANY] * 3,
        out_specs=[VMEM] * 3,
        out_shape=[
            jax.ShapeDtypeStruct((rows, width), F32),
            jax.ShapeDtypeStruct((rows, width), F32),
            jax.ShapeDtypeStruct((2, rows, width), BF16),
        ],
        scratch_shapes=[
            pltpu.VMEM((2 * rows, width), BF16),
            pltpu.VMEM((width, 2 * rows), BF16),
            pltpu.VMEM((width, half), BF16),
            pltpu.VMEM((width, half), BF16),
            pltpu.VMEM((half, width), BF16),
            pltpu.VMEM((2 * rows, half), BF16),
            pltpu.VMEM((half, 2 * rows), BF16),
            pltpu.VMEM((half, 2 * rows), BF16),
            pltpu.SemaphoreType.DMA((3, half // tile)),
        ],
        compiler_params=params(54),
        cost_estimate=takes(24),
        name="feed_forward",
    )


def cut_columns(size, weight, starts, window, held, sems):
    copies = []
    for k, column in enumerate(starts):
        aligned = pl.multiple_of(
            jnp.minimum(column // LANES * LANES, weight.shape[1] - window), LANES
        )
        copy = pltpu.make_async_copy(weight.at[:, pl.ds(aligned, window)], held.at[k], sems.at[k])
        copy.start()
        copies.append((copy, column - aligned))
    return copies


def place_columns(size, copies, held, out_ref, first):
    depth, window = held.shape[-2:]
    step = min(256, depth)
    for k, (copy, offset) in enumerate(copies):
        copy.wait()
        start = (first + k) * size
        place = start % LANES
        for r in range(0, depth, step):
            block = pltpu.roll(held[k, r : r + step, :], window - offset + place, 1)
            out_ref[r : r + step, start : start + size] = block[:, place : place + size]


def slice_kernel(
    size,
    starts,
    qkv_starts,
    b_ref,
    gate_ref,
    up_ref,
    down_ref,
    qkv_ref,
    out_ref,
    turned_ref,
    qkv_out,
    gate_held,
    up_held,
    qkv_held,
    rows,
    gate_sems,
    up_sems,
    qkv_sems,
    row_sems,
):
    depth, window = gate_held.shape[-2:]
    b = b_ref[0]
    gates = cut_columns(size, gate_ref, starts(b), window, gate_held, gate_sems)
    ups = cut_columns(size, up_ref, starts(b), window, up_held, up_sems)
    row_copies = []
    if down_ref.shape[0] > rows.shape[0]:
        for i, row in enumerate(starts(b)):
            row_copies.append(
                pltpu.make_async_copy(
                    down_ref.at[pl.ds(pl.multiple_of(row, size), size), :],
                    rows.at[pl.ds(i * size, size), :],
                    row_sems.at[i],
                )
            )
    else:
        row_copies.append(pltpu.make_async_copy(down_ref, rows, row_sems.at[0]))
    for copy in row_copies:
        copy.start()
    heads = cut_columns(HD, qkv_ref, qkv_starts(b), LANES, qkv_held, qkv_sems)
    place_columns(size, gates, gate_held, out_ref, 0)
    place_columns(size, ups, up_held, out_ref, len(gates))
    for copy in row_copies:
        copy.wait()
    step = min(256, depth)
    for r in range(0, depth, step):
        turned_ref[r : r + step, :] = rows[:, r : r + step].T
    place_columns(HD, heads, qkv_held, qkv_out, 0)


def own_slices(b, gate, up, down, qkv, starts, qkv_starts, count, size, after=()):
    depth = gate.shape[0]
    heads = len(qkv_starts(0))
    window = LANES * ((size + 2 * LANES - 2) // LANES)
    held = pltpu.VMEM((count, depth, window), BF16)
    sems = pltpu.SemaphoreType.DMA((count,))
    return kernel_call(
        functools.partial(slice_kernel, size, starts, qkv_starts),
        (b, gate, up, down, qkv),
        after,
        in_specs=[SMEM] + [ANY] * 4,
        out_specs=[VMEM] * 3,
        out_shape=[
            jax.ShapeDtypeStruct((depth, 2 * count * size), BF16),
            jax.ShapeDtypeStruct((depth, count * size), BF16),
            jax.ShapeDtypeStruct((depth, heads * HD), BF16),
        ],
        scratch_shapes=[
            held,
            held,
            pltpu.VMEM((heads, depth, LANES), BF16),
            pltpu.VMEM((count * size, depth), BF16),
            sems,
            sems,
            pltpu.SemaphoreType.DMA((heads,)),
            sems,
        ],
        compiler_params=params(44),
        cost_estimate=takes(14),
        name="own_slices",
    )


def fetch_rows(slots_ref, pieces, whole_ref, sems):
    rows = pieces[0].shape[0]
    copies = []
    for k, piece in enumerate(pieces):
        place = pl.multiple_of(slots_ref[k] * rows, rows)
        copies.append(
            pltpu.make_async_copy(piece, whole_ref.at[pl.ds(place, rows), :], sems.at[k])
        )
        copies[-1].start()
    return copies


def project(block, weight, bias_ref, cos_ref, sin_ref, qkv_ref, base):
    here = pl.ds(base, block.shape[0])
    cosine, sine = cos_ref[:, here], sin_ref[:, here]
    heads = qkv_ref.shape[1]
    flat = dot(block, weight).T
    for k in range(3 * heads):
        part, i = k // heads, k % heads
        own = flat[k * HD : (k + 1) * HD, :] + bias_ref[part, i]
        if part < 2:
            own = rotated(own, cosine, sine)
        own = own.astype(BF16)
        qkv_ref[part, i, :, here] = own if part else own * HD**-0.5


def early_kernel(count, slots_ref, weight_ref, bias_ref, cos_ref, sin_ref, *refs):
    pieces, (qkv_ref, held, sems) = refs[:count], refs[count:]
    rows = pieces[0].shape[0]
    copies = []
    for k, piece in enumerate(pieces):
        place = pl.multiple_of((k // 2 * 2 + slots_ref[k] % 2) * rows, rows)
        copies.append(pltpu.make_async_copy(piece, held.at[pl.ds(place, rows), :], sems.at[k]))
        copies[-1].start()
    for copy in copies:
        copy.wait()
    size = 2 * rows
    for k in range(count // 2):
        base = pl.multiple_of(slots_ref[2 * k] // 2 * size, size)
        block = held[k * size : (k + 1) * size, :]
        project(block, weight_ref[...], bias_ref, cos_ref, sin_ref, qkv_ref, base)


def early_projection(slots, weight, bias, cosine, sine, pieces, heads, span, after):
    rows, width = pieces[0].shape
    count = len(pieces)
    return kernel_call(
        functools.partial(early_kernel, count),
        (slots, weight, bias, cosine, sine, *pieces),
        after,
        in_specs=[SMEM, VMEM, VMEM, VMEM, VMEM] + [ANY] * count,
        out_specs=VMEM,
        out_shape=jax.ShapeDtypeStruct((3, heads, HD, span), BF16),
        scratch_shapes=[
            pltpu.VMEM((count * rows, width), BF16),
            pltpu.SemaphoreType.DMA((count,)),
        ],
        compiler_params=params(32),
        cost_estimate=takes(8),
        name="early_projection",
    )


def forward_kernel(
    count, early, length_ref, slots_ref, weight_ref, bias_ref, cos_ref, sin_ref, *refs
):
    pieces = refs[:count]
    refs = refs[count:]
    if early:
        early_ref, refs = refs[0], refs[1:]
    (
        whole_out,
        qkv_ref,
        att_ref,
        low_ref,
        lse_ref,
        whole_ref,
        marked,
        triangle,
        sems,
        out_sem,
    ) = refs
    _, heads, _, span = qkv_ref.shape
    length = length_ref[0]
    copies = fetch_rows(slots_ref, pieces, whole_ref, sems)
    size = 256
    if early:
        bases = [
            pl.multiple_of(slots_ref[2 * k] // 2 * size, size) for k in range(span // size)
        ]
        for base in bases[:early]:
            qkv_ref[:, :, :, pl.ds(base, size)] = early_ref[:, :, :, pl.ds(base, size)]
    else:
        bases = list(range(0, span, size))
    for copy in copies:
        copy.wait()
    leaving = pltpu.make_async_copy(whole_ref, whole_out, out_sem)
    leaving.start()
    for base in bases[early:]:
        block = whole_ref[pl.ds(base, size), :]
        project(block, weight_ref[...], bias_ref, cos_ref, sin_ref, qkv_ref, base)

    mark_keys(marked, triangle, length)

    def head(i, carry):
        marked[0, :HD, :] = qkv_ref[1, i]
        marked[1, :HD, :] = qkv_ref[0, i]
        for start in range(0, span, BQ):
            end = start + BQ
            parts = score_parts(marked, triangle, start)
            best = functools.reduce(
                jnp.maximum, [jnp.max(scores, axis=0, keepdims=True) for _, _, scores in parts]
            )
            total, out = 0.0, 0.0
            for low, high, scores in parts:
                weights = jnp.exp(scores - best)
                total += jnp.sum(weights, axis=0, keepdims=True)
                out += dot(qkv_ref[2, i, :, low:high], weights.astype(BF16))
            out = out / total
            att_ref[i, :, start:end] = out
            low_ref[i, :, start:end] = out.astype(BF16)
            lse_ref[i, :, start:end] = best + jnp.log(total)
        return carry

    lax.fori_loop(0, heads, head, 0)
    leaving.wait()


def attention_forward(
    length, slots, weight, bias, cosine, sine, pieces, early, pairs, heads, after
):
    width = weight.shape[0]
    span = len(pieces) * pieces[0].shape[0]
    count = len(pieces)
    return kernel_call(
        functools.partial(forward_kernel, count, pairs),
        (length, slots, weight, bias, cosine, sine, *pieces, *early),
        after,
        in_specs=[SMEM, SMEM, VMEM, VMEM, VMEM, VMEM] + [ANY] * count + [VMEM] * len(early),
        out_specs=[ANY] + [VMEM] * 4,
        out_shape=[
            jax.ShapeDtypeStruct((span, width), BF16),
            jax.ShapeDtypeStruct((3, heads, HD, span), BF16),
            jax.ShapeDtypeStruct((heads, HD, span), F32),
            jax.ShapeDtypeStruct((heads, HD, span), BF16),
            jax.ShapeDtypeStruct((heads, 1, span), F32),
        ],
        scratch_shapes=[
            pltpu.VMEM((span, width), BF16),
            *mark_shapes(span),
            pltpu.SemaphoreType.DMA((count,)),
            pltpu.SemaphoreType.DMA,
        ],
        compiler_params=params(48),
        cost_estimate=takes(20),
        name="attention_forward",
    )


def backward_kernel(
    count, b_ref, length_ref, slots_ref, weight_ref, qkv_ref, att_ref, lse_ref, cos_ref, sin_ref, *refs
):
    pieces = refs[:count]
    (
        whole_out,
        out_ref,
        flat_ref,
        whole_ref,
        weight,
        grad_ref,
        dq,
        dk,
        dv,
        turned,
        marked,
        triangle,
        weight_sem,
        sems,
        out_sem,
    ) = refs[count:]
    _, heads, _, span = qkv_ref.shape
    cosine, sine = cos_ref[...], -sin_ref[...]
    n_blk = out_ref.shape[0]
    weight_copies = []
    for i in range(heads):
        row = pl.multiple_of((n_blk * i + b_ref[0]) * HD, HD)
        weight_copies.append(
            pltpu.make_async_copy(
                weight_ref.at[pl.ds(row, HD), :],
                weight.at[pl.ds(i * HD, HD), :],
                weight_sem.at[i],
            )
        )
        weight_copies[-1].start()
    copies = fetch_rows(slots_ref, pieces, whole_ref, sems)
    mark_keys(marked, triangle, length_ref[0])
    for copy in weight_copies:
        copy.wait()
    across = weight[...].T
    for copy in copies:
        copy.wait()
    leaving = pltpu.make_async_copy(whole_ref, whole_out, out_sem)
    leaving.start()
    for start in range(0, span, BQ):
        grads = dot(whole_ref[start : start + BQ, :], across).T.astype(BF16)
        for i in range(heads):
            grad_ref[i, :, start : start + BQ] = grads[i * HD : (i + 1) * HD, :]

    def head(i, carry):
        dk[...] = jnp.zeros_like(dk)
        dv[...] = jnp.zeros_like(dv)
        marked[0, :HD, :] = qkv_ref[1, i]
        marked[1, :HD, :] = qkv_ref[0, i]
        for start in range(0, span, BQ):
            end = start + BQ
            queries, grads = qkv_ref[0, i, :, start:end], grad_ref[i, :, start:end]
            delta = jnp.sum(grads.astype(F32) * att_ref[i, :, start:end], axis=0, keepdims=True)
            prob = jnp.exp(scores_until(marked, triangle, start) - lse_ref[i, :, start:end])
            grad_prob = dot(qkv_ref[2, i, :, :end], grads, 0, 0)
            grad_score = (prob * (grad_prob - delta)).astype(BF16)
            dq[:, start:end] = dot(qkv_ref[1, i, :, :end], grad_score) * HD**-0.5
            dk[:, :end] += dot(queries, grad_score, 1, 1)
            dv[:, :end] += dot(grads, prob.astype(BF16), 1, 1)
        turned[0, i] = rotated(dq[...], cosine, sine).astype(BF16)
        turned[1, i] = rotated(dk[...], cosine, sine).astype(BF16)
        turned[2, i] = dv[...].astype(BF16)
        return carry

    lax.fori_loop(0, heads, head, 0)
    rows = out_ref.shape[2]
    for part in range(3):
        for i in range(heads):
            k = part * heads + i
            flat_ref[:, k * HD : (k + 1) * HD] = turned[part, i].T
            for j in range(n_blk):
                out_ref[j, k * HD : (k + 1) * HD, :] = turned[part, i, :, j * rows : (j + 1) * rows]
    for i in range(heads):
        k = 3 * heads + i
        for j in range(n_blk):
            out_ref[j, k * HD : (k + 1) * HD, :] = att_ref[
                i, :, j * rows : (j + 1) * rows
            ].astype(BF16)
    leaving.wait()


def attention_backward(
    b, length, slots, weight, qkv, att, lse, cosine, sine, pieces, n_blk, after=()
):
    _, heads, _, span = qkv.shape
    width = weight.shape[1]
    count = len(pieces)
    return kernel_call(
        functools.partial(backward_kernel, count),
        (b, length, slots, weight, qkv, att, lse, cosine, sine, *pieces),
        after,
        in_specs=[SMEM, SMEM, SMEM, ANY] + [VMEM] * 5 + [ANY] * count,
        out_specs=[ANY] + [VMEM] * 2,
        out_shape=[
            jax.ShapeDtypeStruct((span, width), BF16),
            jax.ShapeDtypeStruct((n_blk, 4 * heads * HD, span // n_blk), BF16),
            jax.ShapeDtypeStruct((span, 3 * heads * HD), BF16),
        ],
        scratch_shapes=[
            pltpu.VMEM((span, width), BF16),
            pltpu.VMEM((heads * HD, width), BF16),
            pltpu.VMEM((heads, HD, span), BF16),
        ]
        + [pltpu.VMEM((HD, span), F32)] * 3
        + [
            pltpu.VMEM((3, heads, HD, span), BF16),
            *mark_shapes(span),
            pltpu.SemaphoreType.DMA((heads,)),
            pltpu.SemaphoreType.DMA((count,)),
            pltpu.SemaphoreType.DMA,
        ],
        compiler_params=params(40),
        cost_estimate=takes(18),
        name="attention_backward",
    )


def grads_kernel(n_dp, n_ref, c_ref, gate_up_ref, down_ref, act_ref, grad_ref):
    cols = down_ref.shape[1]
    both = dot(n_ref[...], gate_up_ref[...])
    gate, up = both[:, :cols], both[:, cols:]
    sig = jax.nn.sigmoid(gate)
    silu = gate * sig
    act = silu * up
    part = cols // n_dp
    for i in range(n_dp):
        act_ref[i] = act[:, i * part : (i + 1) * part].T.astype(BF16)
    grad_act = dot(c_ref[...], down_ref[...])
    grad_ref[:, :cols] = (grad_act * up * sig * (1.0 + gate * (1.0 - sig))).astype(BF16)
    grad_ref[:, cols:] = (grad_act * silu).astype(BF16)


def local_grads(all_normed, all_grad, gate_up, down, n_dp, after=()):
    span, width = all_normed.shape
    cols = down.shape[1]
    size = min(512, span)
    return kernel_call(
        functools.partial(grads_kernel, n_dp),
        (all_normed, all_grad, gate_up, down),
        after,
        grid=(span // size,),
        in_specs=[
            pl.BlockSpec((size, width), lambda r: (r, 0)),
            pl.BlockSpec((size, width), lambda r: (r, 0)),
            pl.BlockSpec((width, 2 * cols), lambda r: (0, 0)),
            pl.BlockSpec((width, cols), lambda r: (0, 0)),
        ],
        out_specs=[
            pl.BlockSpec((n_dp, cols // n_dp, size), lambda r: (0, 0, r)),
            pl.BlockSpec((size, 2 * cols), lambda r: (r, 0)),
        ],
        out_shape=[
            jax.ShapeDtypeStruct((n_dp, cols // n_dp, span), BF16),
            jax.ShapeDtypeStruct((span, 2 * cols), BF16),
        ],
        compiler_params=params(48),
        cost_estimate=takes(15),
        name="local_grads",
    )


def keep(value, first, on_ref, mine_ref, cut):
    value += first.astype(F32)

    @pl.when(pl.program_id(0) < cut)
    def _():
        on_ref[...] = value.astype(BF16)

    @pl.when(pl.program_id(0) >= cut)
    def _():
        mine_ref[...] = value


def column_products_kernel(low, high, order_ref, left_ref, right_ref, *refs):
    value = dot(left_ref[...], right_ref[:, low:high], 0, 0)
    if len(refs) == 1:
        refs[0][0] = value.astype(BF16)
    else:
        keep(value, refs[0][0, :, low:high], *refs[1:], 2)


def column_products(order, left, right, low, high, n_dp, first=None, after=()):
    span, width = left.shape
    cols = high - low
    size = width // n_dp
    part = size // 2
    stay = [
        pl.BlockSpec((part, cols), lambda j, order: (jnp.minimum(j, 1), 0)),
        pl.BlockSpec((part, cols), lambda j, order: (jnp.maximum(j - 2, 0), 0)),
    ]
    block = pl.BlockSpec(
        (1, part, cols if first is None else right.shape[1]), lambda j, order: (j // 2, j % 2, 0)
    )
    return kernel_call(
        functools.partial(column_products_kernel, low, high),
        (order, left, right) + (() if first is None else (first,)),
        after,
        prefetch=1,
        grid=(4,),
        in_specs=[
            pl.BlockSpec((span, part), lambda j, order: (0, order[j // 2] * 2 + j % 2)),
            pl.BlockSpec(right.shape, lambda j, order: (0, 0)),
        ]
        + ([] if first is None else [block]),
        out_specs=block if first is None else stay,
        out_shape=jax.ShapeDtypeStruct((2, size, cols), BF16)
        if first is None
        else [jax.ShapeDtypeStruct((size, cols), dtype) for dtype in (BF16, F32)],
        compiler_params=params(24),
        cost_estimate=takes(8),
        name="column_products",
    )


def row_products_kernel(count, order_ref, *refs):
    lefts, right_ref, rest = refs[:count], refs[count], refs[count + 1 :]
    value = [dot(left[0], right_ref[...]) for left in lefts]
    value = jnp.concatenate(value, axis=0) if count > 1 else value[0]
    if len(rest) == 1:
        rest[0][0] = value.astype(BF16)
    else:
        keep(value, rest[0][0], *rest[1:], 1)


def row_products(order, lefts, right, first=None, after=()):
    span, width = right.shape
    size = sum(left.shape[1] for left in lefts)
    block = pl.BlockSpec((1, size, width), lambda j, order: (j, 0, 0))
    stay = pl.BlockSpec((size, width), lambda j, order: (0, 0))
    return kernel_call(
        functools.partial(row_products_kernel, len(lefts)),
        (order, *lefts, right) + (() if first is None else (first,)),
        after,
        prefetch=1,
        grid=(2,),
        in_specs=[
            pl.BlockSpec((1,) + left.shape[1:], lambda j, order: (order[j], 0, 0))
            for left in lefts
        ]
        + [pl.BlockSpec((span, width), lambda j, order: (0, 0))]
        + ([] if first is None else [block]),
        out_specs=block if first is None else [stay, stay],
        out_shape=jax.ShapeDtypeStruct((2, size, width), BF16)
        if first is None
        else [jax.ShapeDtypeStruct((size, width), dtype) for dtype in (BF16, F32)],
        compiler_params=params(24),
        cost_estimate=takes(8),
        name="row_products",
    )


def add_kernel(mine_ref, second_ref, *out_refs):
    total = mine_ref[...] + second_ref[...].astype(F32)
    start = 0
    for out_ref in out_refs:
        size = out_ref.shape[0]
        out_ref[...] = total[start : start + size].astype(out_ref.dtype)
        start += size


def add_second(mine, second, sizes, dtype, after=(), us=16):
    _, cols = mine.shape
    return kernel_call(
        add_kernel,
        (mine, second),
        after,
        in_specs=[VMEM] * 2,
        out_specs=[VMEM] * len(sizes),
        out_shape=[jax.ShapeDtypeStruct((part, cols), dtype) for part in sizes],
        compiler_params=params(16),
        cost_estimate=takes(us),
        name="add_second",
    )


def spread_kernel(count, outer, size, line, *refs):
    arrays, out_refs = refs[:count], refs[count:]
    n_blk = arrays[0].shape[0]
    if line:
        out_refs, line_refs = out_refs[:-3], out_refs[-3:]
        rows = out_refs[0].shape[0]
        sums = sum(arrays[-1][b, rows : rows + EXTRA, :line].astype(F32) for b in range(n_blk))
        start = 0
        for line_ref in line_refs:
            end = start + line_ref.shape[1]
            line_ref[...] = sums[:1, start:end]
            start = end
    for k, out_ref in enumerate(out_refs):
        rows = out_ref.shape[0]
        for i in range(outer):
            for b in range(n_blk):
                source = (k * outer + i) * size
                place = (i * n_blk + b) * size
                start = 0
                for array in arrays:
                    end = start + array.shape[2]
                    low, high = max(source, start), min(source + size, end)
                    if low < high:
                        out_ref[:, place + low - source : place + high - source] = array[
                            b, :rows, low - start : high - start
                        ].astype(F32)
                    start = end


def spread(arrays, rows, outputs, outer, size, line=0, after=()):
    n_blk = arrays[0].shape[0]
    return kernel_call(
        functools.partial(spread_kernel, len(arrays), outer, size, line),
        tuple(arrays),
        after,
        in_specs=[VMEM] * len(arrays),
        out_specs=[VMEM] * (outputs + 3 * (line > 0)),
        out_shape=[jax.ShapeDtypeStruct((rows, outer * n_blk * size), F32)] * outputs
        + [jax.ShapeDtypeStruct((1, n * line // 5), F32) for n in (1, 1, 3) if line],
        compiler_params=params(16),
        cost_estimate=takes(3),
        name="spread",
    )


def out_kernel(x_ref, ffn_ref, other_ref, weight_ref, pieces, out_ref, left, total):
    n_blk, lines, _ = pieces.shape
    heads = lines // HD // 4
    step = pl.program_id(0)
    size = left.shape[2]

    @pl.when(step == 0)
    def _():
        for i in range(heads):
            for b in range(n_blk):
                place = (i * n_blk + b) * HD
                block, start = place // size, place % size
                k = 3 * heads + i
                left[block, :, start : start + HD] = pieces[b, k * HD : (k + 1) * HD, :].T
        total[...] = x_ref[...].astype(F32) + ffn_ref[...] + other_ref[0].astype(F32)

    total[...] += dot(left[step], weight_ref[...])

    @pl.when(step == pl.num_programs(0) - 1)
    def _():
        out_ref[...] = total[...].astype(BF16)


def project_out(tokens, ffn_out, other, weight, pieces, after=()):
    rows, width = tokens.shape
    steps = 4
    size = width // steps
    whole = pl.BlockSpec((rows, width), lambda t: (0, 0))
    return kernel_call(
        out_kernel,
        (tokens, ffn_out, other, weight, pieces),
        after,
        grid=(steps,),
        in_specs=[
            whole,
            whole,
            pl.BlockSpec((1, rows, width), lambda t: (0, 0, 0)),
            pl.BlockSpec((size, width), lambda t: (t, 0)),
            pl.BlockSpec(pieces.shape, lambda t: (0, 0, 0)),
        ],
        out_specs=whole,
        out_shape=jax.ShapeDtypeStruct((rows, width), BF16),
        scratch_shapes=[pltpu.VMEM((steps, rows, size), BF16), pltpu.VMEM((rows, width), F32)],
        compiler_params=params(20),
        cost_estimate=takes(6),
        name="project_out",
    )


def input_kernel(
    x_ref, c_ref, gain_ref, ffn_ref, other_ref, weight_ref, pieces, out_ref, sums_ref, left, total
):
    n_blk, lines, _ = pieces.shape
    step, steps = pl.program_id(0), pl.num_programs(0)
    size = left.shape[1]

    @pl.when(step == 0)
    def _():
        for i in range(3 * (lines // HD // 4)):
            for b in range(n_blk):
                place = (i * n_blk + b) * HD
                block, start = place // size, place % size
                left[block, start : start + HD, :] = pieces[b, i * HD : (i + 1) * HD, :]
        total[...] = jnp.zeros_like(total)

    total[...] += dot(weight_ref[...], left[step])

    @pl.when(step == steps - 1)
    def _():
        x = x_ref[...].astype(F32)
        center = x - jnp.mean(x, axis=1, keepdims=True)
        inverse_std = lax.rsqrt(jnp.mean(center * center, axis=1, keepdims=True) + epsilon)
        normalized = center * inverse_std
        grad = ffn_ref[...] + other_ref[0].astype(F32) + total[...].T
        vectors = [
            jnp.sum(grad * normalized, axis=0, keepdims=True),
            jnp.sum(grad, axis=0, keepdims=True),
        ] + [jnp.sum(left[t].astype(F32).T, axis=0, keepdims=True) for t in range(left.shape[0])]
        flat = jnp.concatenate(vectors, axis=1)
        shards = sums_ref.shape[0]
        width = grad.shape[1]
        cut = width // shards
        for j in range(shards):
            sums_ref[j : j + 1, :cut] = flat[:, j * cut : (j + 1) * cut]
            sums_ref[j : j + 1, cut : 2 * cut] = flat[:, width + j * cut : width + (j + 1) * cut]
            start = 2 * width + 3 * j * cut
            sums_ref[j : j + 1, 2 * cut :] = flat[:, start : start + 3 * cut]
        grad = grad * gain_ref[...]
        grad_inputs = inverse_std * (
            grad
            - jnp.mean(grad, axis=1, keepdims=True)
            - normalized * jnp.mean(grad * normalized, axis=1, keepdims=True)
        )
        out_ref[...] = (c_ref[...].astype(F32) + grad_inputs).astype(BF16)


def input_grads(
    tokens, out_grad, gain, ffn_grad, other, weight, pieces, shards, after=()
):
    rows, width = tokens.shape
    cols = weight.shape[1]
    steps = 8
    size = cols // steps
    whole = pl.BlockSpec((rows, width), lambda t: (0, 0))
    return kernel_call(
        input_kernel,
        (tokens, out_grad, gain, ffn_grad, other, weight, pieces),
        after,
        grid=(steps,),
        in_specs=[
            whole,
            whole,
            pl.BlockSpec((1, width), lambda t: (0, 0)),
            whole,
            pl.BlockSpec((1, rows, width), lambda t: (1, 0, 0)),
            pl.BlockSpec((width, size), lambda t: (0, t)),
            pl.BlockSpec(pieces.shape, lambda t: (0, 0, 0)),
        ],
        out_specs=[whole, pl.BlockSpec((shards, 5 * width // shards), lambda t: (0, 0))],
        out_shape=[
            jax.ShapeDtypeStruct((rows, width), BF16),
            jax.ShapeDtypeStruct((shards, 5 * width // shards), F32),
        ],
        scratch_shapes=[pltpu.VMEM((steps, size, rows), BF16), pltpu.VMEM((width, rows), F32)],
        compiler_params=params(28),
        cost_estimate=takes(13),
        name="input_grads",
    )


def on_device(
    n_dp,
    n_blk,
    tokens,
    norm_gain,
    norm_bias,
    qkv_weight,
    qkv_bias,
    out_weight,
    gate_weight,
    up_weight,
    down_weight,
    cotangent,
    lengths,
):
    rows, width = tokens.shape[1:]
    span = rows * n_blk
    hidden = gate_weight.shape[1]
    per_dev = width // HD // n_blk
    ff_block = hidden // (n_dp * n_blk)
    d, b = lax.axis_index("dp").astype(jnp.int32), lax.axis_index("blk").astype(jnp.int32)
    own_tokens, out_grad = tokens[0], cotangent[0]

    inputs = own_tokens.astype(F32)
    center = inputs - jnp.mean(inputs, axis=1, keepdims=True)
    inverse_std = lax.rsqrt(jnp.mean(center * center, axis=1, keepdims=True) + epsilon)
    normed = (center * inverse_std * norm_gain + norm_bias).astype(BF16)

    position = b.reshape(1)

    def ff_starts(b):
        return [(n_blk * i + b) * ff_block for i in range(n_dp)]

    def qkv_starts(b):
        return [part * width + (n_blk * i + b) * HD for part in range(3) for i in range(per_dev)]

    def own_blocks(array, outer, size):
        cut = array.reshape((outer, n_blk, size) + array.shape[1:])
        return lax.dynamic_index_in_dim(cut, b, 1, keepdims=False).reshape(
            (-1,) + array.shape[1:]
        )

    down_rows = down_weight if ff_block % 16 == 0 else own_blocks(down_weight, n_dp, ff_block)

    def slices():
        return own_slices(
            position,
            gate_weight,
            up_weight,
            down_rows,
            qkv_weight,
            ff_starts,
            qkv_starts,
            n_dp,
            ff_block,
        )

    def ffn(normed_other, grad_other, after):
        return feed_forward(
            position,
            (normed, normed_other),
            (out_grad, grad_other),
            (gate_weight, up_weight, down_weight),
            after,
        )

    own_bias = own_blocks(qkv_bias, 3 * per_dev, HD).reshape(3, per_dev, HD, 1)
    frequency = 10000.0 ** (-2.0 * np.arange(HALF) / ROT)
    angles = frequency[:, None] * np.arange(span)[None, :]
    cosine, sine = np.cos(angles).astype(np.float32), np.sin(angles).astype(np.float32)


    if n_blk == 8:
        slots = piece_slots(b)
        n1, m0, c1, e0 = along(normed), beside(normed, 8), along(out_grad), beside(out_grad, 8)
        n3 = back(normed)
        own_gate_up, own_down, own_qkv = slices()
        c1, e0 = relay([c1, e0], [own_down])
        (n1,) = relay([n1], [c1])
        m1, e1, n2, c2 = beside(n1, 8), beside(c1, 8), along(n1), along(c1)
        (n3,) = relay([n3], [n1])
        m3 = beside(n3, 8)
        ffn_out, ffn_grad, passed = ffn(m0, e0, [n3])
        n2, c3, e3 = relay([n2, out_grad, e0], [ffn_out, m1, e1])
        m2, c3, e3 = beside(n2, 8), back(c3), back(e3)
        (c2,) = relay([c2], [n2])
        e2 = beside(c2, 8)
        normed_pieces = [normed, m0, n1, m1, n3, m3, n2, m2]
        grad_pieces = [out_grad, e0, c1, e1, c3, e3, c2, e2]
        early = [
            early_projection(
                slots, own_qkv, own_bias, cosine, sine, normed_pieces[:6], per_dev, span, [n2]
            )
        ]
        arrived = [c2]
    else:
        slots = jnp.zeros((1,), jnp.int32)
        normed_pieces = [lax.all_gather(normed, "blk", axis=0, tiled=True)]
        grad_pieces = [lax.all_gather(out_grad, "blk", axis=0, tiled=True)]
        own_gate_up, own_down, own_qkv = slices()
        ffn_out, ffn_grad, passed = ffn(
            beside(normed, n_blk), beside(out_grad, n_blk), [own_down]
        )
        early, arrived = [], []

    all_normed, qkv, att, att_low, lse = attention_forward(
        lengths,
        slots,
        own_qkv,
        own_bias,
        cosine,
        sine,
        normed_pieces,
        early,
        3 * len(early),
        per_dev,
        [ffn_out, *arrived],
    )
    all_grad, grad_cut, grad_qkv = attention_backward(
        position,
        lengths,
        slots,
        out_weight,
        qkv,
        att,
        lse,
        cosine,
        sine,
        grad_pieces,
        n_blk,
    )
    grad_rows = swap_blk(grad_cut)

    sent = jnp.stack([d ^ 3, d ^ 1])
    kept = jnp.stack([d ^ 2, d])

    def over_first(array):
        return lax.ppermute(array, "dp", [(i, i ^ 1) for i in range(4)])

    def over_second(array):
        return lax.ppermute(array, "dp", [(i, i ^ 2) for i in range(4)])

    def row_cut(total):
        return swap_blk(total.reshape(n_blk, -1, total.shape[1]))

    ff_cols, qkv_cols = 2 * n_dp * ff_block, 3 * per_dev * HD
    aligned = per_dev == n_dp
    shards = n_dp * n_blk
    line = 5 * width // shards
    full = [width // n_dp]

    qkv_sent = column_products(sent, all_normed, grad_qkv, 0, qkv_cols, n_dp)
    qkv_first = over_first(qkv_sent)
    act, grad_ff = local_grads(
        all_normed, all_grad, own_gate_up, own_down, n_dp, [qkv_sent]
    )
    lefts = [act, att_low] if aligned else [act]
    qkv_on, qkv_mine = column_products(
        kept, all_normed, grad_qkv, 0, qkv_cols, n_dp, qkv_first, [act]
    )
    qkv_second = over_second(qkv_on)
    ff_sent = column_products(sent, all_normed, grad_ff, 0, ff_cols, n_dp, None, [qkv_on])
    ff_first = over_first(ff_sent)
    row_sent = row_products(sent, lefts, all_grad, None, [ff_sent])
    row_first = over_first(row_sent)
    (qkv_total,) = add_second(qkv_mine, qkv_second, full, BF16, [row_sent], 24)
    qkv_pieces = row_cut(qkv_total)
    ff_on, ff_mine = column_products(
        kept, all_normed, grad_ff, 0, ff_cols, n_dp, ff_first, [qkv_total]
    )
    ff_second = over_second(ff_on)
    row_on, row_mine = row_products(kept, lefts, all_grad, row_first, [ff_on])
    (passed,) = relay([passed], [grad_cut])
    ffn_other = beside(passed, n_blk)
    input_grad, vectors = input_grads(
        own_tokens,
        out_grad,
        norm_gain[None],
        ffn_grad,
        ffn_other,
        qkv_weight,
        grad_rows,
        shards,
        [row_on],
    )
    (ff_total,) = add_second(ff_mine, ff_second, full, BF16, [input_grad], 1)
    vectors = vectors.reshape(n_dp, n_blk, line)

    def of(mask):
        return lax.dynamic_index_in_dim(vectors, d ^ mask, 0, keepdims=False)

    vector_first = over_first(jnp.stack([of(3), of(1)]))
    vector_second = over_second(of(2) + vector_first[0])
    (row_on,) = relay([row_on], [vector_second])
    row_second = over_second(row_on)
    layer_out = project_out(own_tokens, ffn_out, ffn_other, out_weight, grad_rows, [input_grad])
    vectors = of(0) + vector_first[1] + vector_second
    below = jnp.pad(vectors.astype(BF16)[:, None], ((0, 0), (0, EXTRA - 1), (0, ff_cols - line)))
    ff_pieces = swap_blk(
        jnp.concatenate([ff_total.reshape(n_blk, -1, ff_cols), below], axis=1)
    )
    sizes = [ff_block, HD] if aligned else [ff_block]
    shard_down, *shard_out = add_second(row_mine, row_second, sizes, F32)
    if aligned:
        shard_out = shard_out[0]
    else:
        grad_out = dot(att_low.reshape(-1, span), all_grad)
        wide = jnp.zeros((width, width), F32)
        for i in range(per_dev):
            start = (n_blk * i + b) * HD
            wide = lax.dynamic_update_slice(wide, grad_out[i * HD : (i + 1) * HD], (start, 0))
        shard_out = lax.psum_scatter(wide, ("dp", "blk"), scatter_dimension=0, tiled=True)
    cut = width // shards
    (shard_qkv,) = spread([qkv_pieces], cut, 1, 3 * per_dev, HD)
    shard_gate, shard_up, *sums = spread([ff_pieces], cut, 2, n_dp, ff_block, line)
    return (
        layer_out[None],
        input_grad[None],
        sums[0].reshape(-1),
        sums[1].reshape(-1),
        shard_qkv,
        sums[2].reshape(-1),
        shard_out,
        shard_gate,
        shard_up,
        shard_down,
    )


def solution(mesh):
    both = P(("dp", "blk"))
    row_cut = P(("dp", "blk"), None)
    activation = P("dp", "blk", None)
    return jax.shard_map(
        functools.partial(on_device, mesh.shape["dp"], mesh.shape["blk"]),
        mesh=mesh,
        in_specs=(activation,) + (P(),) * 8 + (activation, P("dp")),
        out_specs=(activation, activation, both, both, row_cut, both) + (row_cut,) * 4,
        check_vma=False,
    )
```
